32 devices in a mesh: dp: 8 (over z, x), tensor: 4 (over y, core).
Axes of the slice: x: 2, y: 2, z: 4, core: 2. Of those that a mesh axis runs over, the one named last changes fastest.
Arguments:
- tokens_in: bfloat16 [96, 200, 768], P(('dp', 'tensor')), may hold values from -6 to 6
- key_mask: int32 [96, 200], P('dp'), may hold values from 0 to 1, as said below
- expert_ids: int32 [96, 200, 2], P('dp'), may hold values from 0 to 7, as said below
- expert_slots: int32 [96, 200, 2], P('dp'), may hold values from 0 to 127, as said below
- norm1_gain: float32 [768], P('dp'), may hold values from 0.5 to 1.5
- norm1_shift: float32 [768], P('dp'), may hold values from -1.5 to 1.5
- qkv_weight: float32 [3, 768, 768], P(None, 'dp', 'tensor'), may hold values from -0.21875 to 0.21875
- qv_bias: float32 [2, 768], P(None, 'dp'), may hold values from -1.5 to 1.5
- out_weight: float32 [768, 768], P('tensor', 'dp'), may hold values from -1.75 to 1.75
- out_bias: float32 [768], P('dp'), may hold values from -1.5 to 1.5
- norm2_gain: float32 [768], P('dp'), may hold values from 0.5 to 1.5
- norm2_shift: float32 [768], P('dp'), may hold values from -1.5 to 1.5
- router_weight: float32 [768, 8], P('dp'), may hold values from -0.15625 to 0.15625
- up_weight: float32 [8, 768, 3072], P(None, 'dp', 'tensor'), may hold values from -0.21875 to 0.21875
- up_bias: float32 [8, 3072], P(None, 'dp'), may hold values from -1.5 to 1.5
- down_weight: float32 [8, 3072, 768], P(None, 'tensor', 'dp'), may hold values from -0.875 to 0.875
- down_bias: float32 [8, 768], P(None, 'dp'), may hold values from -5 to 5
- out_grad: bfloat16 [96, 200, 768], P(('dp', 'tensor')), may hold values from -6 to 6
Outputs:
- output: bfloat16 [96, 200, 768], P(('dp', 'tensor'))
- input_grad: float32 [96, 200, 768], P(('dp', 'tensor'))
- norm1_gain_grad: float32 [768], P('dp')
- norm1_shift_grad: float32 [768], P('dp')
- qkv_weight_grad: float32 [3, 768, 768], P(None, 'dp', 'tensor')
- qv_bias_grad: float32 [2, 768], P(None, 'dp')
- out_weight_grad: float32 [768, 768], P('tensor', 'dp')
- out_bias_grad: float32 [768], P('dp')
- norm2_gain_grad: float32 [768], P('dp')
- norm2_shift_grad: float32 [768], P('dp')
- router_weight_grad: float32 [768, 8], P('dp')
- up_weight_grad: float32 [8, 768, 3072], P(None, 'dp', 'tensor')
- up_bias_grad: float32 [8, 3072], P(None, 'dp')
- down_weight_grad: float32 [8, 3072, 768], P(None, 'tensor', 'dp')
- down_bias_grad: float32 [8, 768], P(None, 'dp')
The draws below stay inside these ranges and needn't reach their ends.
Inputs may be any that keep to these rules, and one draw needn't show every extreme that they name: `key_mask`: each image's keys with value 1 are its first 200 - p positions, with p from 1 to 3; some image has p = 3 and some has p = 1. `expert_ids`: A token's two ids differ. In each group of 2 consecutive images expert e is named by L_e of the 800 choices, L_e at most 128, and some expert of every group has exactly 128. Within a group the pairs (expert_ids, expert_slots) of all tokens and both choices are distinct, and the slots of expert e are exactly 0 to L_e - 1.
All inputs are finite; a program needn't handle non-finite values.
Results may differ from the reference program's by a relative error of at most 0.017.
Values may be sent and summed in bfloat16 or wider, within the bound.
No kernel may reach another device: no remote copies, remote signals or barrier semaphores. Data moves between devices by JAX's collectives and lax.ppermute only.
A program may use at most 320 MiB of HBM per device.

```python
import jax
import jax.numpy as jnp
from jax import lax

D = 768
HEADS = 12
HD = 64
FF = 3072
EXPERTS = 8
SEQ = 200
PAD = 3
CAP = 128
GROUP_IMG = 2
HEAD_WIDTH = 768
IMAGES = 96


def route_table(key):
    groups = IMAGES // GROUP_IMG
    total = GROUP_IMG * SEQ
    mean_load = 2 * total // EXPERTS
    spread = CAP - mean_load

    def one_group(group_key):
        key_loads, key_order, key_tokens, key_flip = jax.random.split(group_key, 4)
        half = EXPERTS // 2
        offset = jax.random.randint(key_loads, (half,), 0, spread + 1)
        offset = offset.at[0].set(spread)
        loads = jnp.concatenate([mean_load + offset, mean_load - offset])
        loads = loads[jax.random.permutation(key_order, EXPERTS)]
        ends = jnp.cumsum(loads)
        starts = ends - loads
        position = jnp.arange(2 * total)
        owner = jnp.sum((position[:, None] >= ends[None, :]).astype(jnp.int32), 1).astype(jnp.int32)
        slot = (position - starts[owner]).astype(jnp.int32)
        order = jax.random.permutation(key_tokens, total)
        pair_ids = jnp.stack([owner[order], owner[order + total]], -1)
        pair_slots = jnp.stack([slot[order], slot[order + total]], -1)
        flip = jax.random.randint(key_flip, (total, 1), 0, 2)
        pair_ids = jnp.where(flip == 1, pair_ids[:, ::-1], pair_ids)
        pair_slots = jnp.where(flip == 1, pair_slots[:, ::-1], pair_slots)
        return (pair_ids.astype(jnp.int32), pair_slots.astype(jnp.int32))
    group_keys = jax.random.split(key, groups)
    all_ids, all_slots = jax.vmap(one_group)(group_keys)
    return (all_ids.reshape(IMAGES, SEQ, 2), all_slots.reshape(IMAGES, SEQ, 2))


def draw_expert_ids(key, part):
    return route_table(key)[0]


def draw_expert_slots(key, part):
    return route_table(key)[1]


def draw_key_mask(key, part):
    key = jax.random.fold_in(key, 11)
    missing = jax.random.randint(key, (IMAGES,), 1, PAD + 1)
    missing = missing.at[0].set(PAD).at[1].set(1)
    return (jnp.arange(SEQ)[None, :] < (SEQ - missing)[:, None]).astype(jnp.int32)


def with_spikes(values, stream_key, source, target, blocks, factor):
    owner, partner = [(jnp.arange(values.shape[axis_at]) // (values.shape[axis_at] // blocks)).reshape([-1 if axis == axis_at else 1 for axis in range(values.ndim)]) for axis_at in (source, target)]
    chosen = jax.random.permutation(stream_key, blocks)[partner]
    strong = (owner == chosen) | (owner == (partner + blocks // 2) % blocks)
    return jnp.where(strong, factor * values, values)


def steps_of(key, dims, pieces, least, high):
    loudness, own = 1.0, jax.random.fold_in(key, 6)
    for axis_at, shards_of in pieces:
        draws = jnp.exp(jax.random.uniform(jax.random.fold_in(own, axis_at), (shards_of,), jnp.float32, least / len(pieces), high / len(pieces)))
        loudness = loudness * jnp.repeat(draws, dims[axis_at] // shards_of).reshape([-1 if axis == axis_at else 1 for axis in range(len(dims))])
    return loudness


def scatter_about(own_key, dims, scale, bound, shards=(), held_as=jnp.bfloat16):
    values = jax.random.normal(own_key, dims, jnp.float32) * scale
    if len(shards) > 0:
        values = steps_of(own_key, dims, shards, -0.22, 0.18) * values
    return jnp.clip(values, min=-bound, max=bound).astype(held_as)


def noise_with(own_key, dims, scale, reach, shards, heavy, kind=jnp.bfloat16):
    values = scale * jax.random.normal(own_key, dims, jnp.float32)
    if shards:
        values = values * steps_of(own_key, dims, shards, -0.22, 0.18)
    return jnp.clip(with_spikes(values, jax.random.fold_in(own_key, 3), *heavy), -reach, reach).astype(kind)


def setup_inputs(seed: int = 0) -> dict:
    seeds = jax.random.split(jax.random.key(seed), 19)
    return {
        "tokens_in": scatter_about(seeds[0], (IMAGES, SEQ, D), 1.0, 6.0, ((0, 32),)),
        "key_mask": draw_key_mask(jax.random.fold_in(seeds[18], 71), 0),
        "expert_ids": draw_expert_ids(jax.random.fold_in(seeds[18], 71), 0),
        "expert_slots": draw_expert_slots(jax.random.fold_in(seeds[18], 71), 0),
        "norm1_gain": jnp.clip(1.0 + 0.1 * jax.random.normal(seeds[4], (D,), jnp.float32), 0.5, 1.5),
        "norm1_shift": scatter_about(seeds[5], (D,), 0.3, 1.5, ((0, 8),), jnp.float32),
        "qkv_weight": scatter_about(seeds[6], (3, D, HEAD_WIDTH), D ** -0.5, 0.21875, ((1, 8), (2, 4)), jnp.float32),
        "qv_bias": scatter_about(seeds[7], (2, HEAD_WIDTH), 0.3, 1.5, ((1, 8),), jnp.float32),
        "out_weight": scatter_about(seeds[8], (HEAD_WIDTH, D), (HEAD_WIDTH // 64) ** -0.5, 1.75, ((0, 4), (1, 8)), jnp.float32),
        "out_bias": scatter_about(seeds[9], (D,), 0.3, 1.5, ((0, 8),), jnp.float32),
        "norm2_gain": jnp.clip(1.0 + 0.1 * jax.random.normal(seeds[10], (D,), jnp.float32), 0.5, 1.5),
        "norm2_shift": scatter_about(seeds[11], (D,), 0.3, 1.5, ((0, 8),), jnp.float32),
        "router_weight": scatter_about(seeds[12], (D, EXPERTS), (2 * D) ** -0.5, 0.15625, ((0, 8),), jnp.float32),
        "up_weight": scatter_about(seeds[13], (EXPERTS, D, FF), D ** -0.5, 0.21875, ((1, 8), (2, 4)), jnp.float32),
        "up_bias": scatter_about(seeds[14], (EXPERTS, FF), 0.3, 1.5, ((1, 8),), jnp.float32),
        "down_weight": scatter_about(seeds[15], (EXPERTS, FF, D), (FF // 64) ** -0.5, 0.875, ((1, 4), (2, 8)), jnp.float32),
        "down_bias": scatter_about(seeds[16], (EXPERTS, D), 1.0, 5.0, ((1, 8),), jnp.float32),
        "out_grad": noise_with(seeds[17], (IMAGES, SEQ, D), 1.0, 6.0, ((0, 32),), (0, 2, 32, 2.75)),
    }


EPSILON = 1e-06
NEGATIVE = -1e+30
HIGHEST_PRECISION = lax.Precision.HIGHEST

@jax.custom_vjp
def low(v):
    return lax.optimization_barrier(v.astype(jnp.bfloat16)).astype(jnp.float32)

@jax.custom_vjp
def low_back(v):
    return v

def low_keep(v):
    return (low(v), None)

def low_pass(kept, grad):
    return (grad,)

def back_keep(v):
    return (v, None)

def back_low(kept, grad):
    return (low(grad),)
low.defvjp(low_keep, low_pass)
low_back.defvjp(back_keep, back_low)

def round_both(values):
    return low_back(low(values))

def layer_norm(values, gains, shifts):
    middle = lax.optimization_barrier(jnp.mean(values, -1, keepdims=True))
    centred = values - middle
    inverse = lax.rsqrt(lax.optimization_barrier(jnp.mean(centred * centred, -1, keepdims=True)) + EPSILON)
    return centred * inverse * gains + shifts

def group_forward(inputs, key_mask, expert_ids, expert_slots, params):
    gain_one, shift_one, qkv_weight, qv_bias, out_weight, out_bias, gain_two, shift_two, router_weight, up_weight, up_bias, down_weight, down_bias = tuple((low(item) for item in params))
    images = inputs.shape[0]
    tokens = images * SEQ
    normed_one = low(layer_norm(inputs, gain_one, shift_one))

    def project(matrix):
        return jnp.einsum('bsd,dk->bsk', normed_one, matrix, precision=HIGHEST_PRECISION)
    shape_heads = (images, SEQ, HEADS, HD)
    queries = round_both(project(qkv_weight[0]) + qv_bias[0]).reshape(shape_heads)
    key_rows = round_both(project(qkv_weight[1])).reshape(shape_heads)
    value_rows = round_both(project(qkv_weight[2]) + qv_bias[1]).reshape(shape_heads)
    scores = low_back(jnp.einsum('bihc,bjhc->bhij', queries, key_rows, precision=HIGHEST_PRECISION) * HD ** (-0.5))
    masked = jnp.where(key_mask[:, None, None, :] > 0, scores, NEGATIVE)
    largest = lax.optimization_barrier(jnp.max(masked, -1, keepdims=True))
    expanded = jnp.exp(masked - largest)
    chances = low(expanded / lax.optimization_barrier(jnp.sum(expanded, -1, keepdims=True)))
    attended = round_both(jnp.einsum('bhij,bjhc->bihc', chances, value_rows, precision=HIGHEST_PRECISION).reshape(images, SEQ, HEAD_WIDTH))
    residual = inputs + low_back(jnp.einsum('bsk,kd->bsd', attended, out_weight, precision=HIGHEST_PRECISION)) + out_bias
    normed_two = low(layer_norm(residual, gain_two, shift_two))
    logits = low_back(jnp.einsum('bsd,de->bse', normed_two, router_weight, precision=HIGHEST_PRECISION))
    probabilities = jax.nn.softmax(logits, -1)
    gates = jnp.take_along_axis(probabilities, expert_ids, -1).reshape(tokens, 2)
    flat_ids = expert_ids.reshape(tokens, 2)
    position = (expert_ids * CAP + expert_slots).reshape(tokens * 2)
    flat_rows = normed_two.reshape(tokens, D)
    dispatched = jnp.zeros((EXPERTS * CAP, D), normed_two.dtype).at[position].set(jnp.repeat(flat_rows, 2, 0))
    dispatched = dispatched.reshape(EXPERTS, CAP, D)
    hidden = low_back(jnp.einsum('ecd,edf->ecf', dispatched, up_weight, precision=HIGHEST_PRECISION) + up_bias[:, None, :])
    active = low(jax.nn.gelu(hidden, approximate=False))
    produced = low_back(jnp.einsum('ecf,efd->ecd', active, down_weight, precision=HIGHEST_PRECISION))
    picked = produced.reshape(EXPERTS * CAP, D)[position].reshape(tokens, 2, D)
    mixture = low_back(lax.optimization_barrier(jnp.sum(gates[:, :, None] * picked, 1)))
    bias_term = lax.optimization_barrier(jnp.sum(gates[:, :, None] * down_bias[flat_ids], 1))
    return residual + (mixture + bias_term).reshape(images, SEQ, D)

def reference(tokens_in, key_mask, expert_ids, expert_slots, norm1_gain, norm1_shift, qkv_weight, qv_bias, out_weight, out_bias, norm2_gain, norm2_shift, router_weight, up_weight, up_bias, down_weight, down_bias, out_grad):
    params = (norm1_gain, norm1_shift, qkv_weight, qv_bias, out_weight, out_bias, norm2_gain, norm2_shift, router_weight, up_weight, up_bias, down_weight, down_bias)
    groups = IMAGES // GROUP_IMG

    def by_group(values):
        return values.reshape((groups, GROUP_IMG) + values.shape[1:])

    def advance(totals, items):
        inputs_one, mask_one, ids_one, slots_one, cotangent_one = items

        def forward(values, weights):
            return group_forward(values, mask_one, ids_one, slots_one, weights)
        result, pull = jax.vjp(forward, inputs_one, params)
        input_grad, weight_grads = pull(cotangent_one)
        return (jax.tree.map(jnp.add, totals, weight_grads), (result.astype(jnp.bfloat16), input_grad))
    zeros = jax.tree.map(jnp.zeros_like, params)
    items = (by_group(tokens_in.astype(jnp.float32)), by_group(key_mask), by_group(expert_ids), by_group(expert_slots), by_group(out_grad.astype(jnp.float32)))
    totals, (outputs, input_grads) = lax.scan(advance, zeros, items)
    return (outputs.reshape(IMAGES, SEQ, D), input_grads.reshape(IMAGES, SEQ, D), totals[0], totals[1], totals[2], totals[3], totals[4], totals[5], totals[6], totals[7], totals[8], totals[9], totals[10], totals[11], totals[12])
```

```python
import jax
import jax.numpy as jnp
from jax import lax
from jax.sharding import Mesh
from jax.sharding import PartitionSpec as P

HD = 64
CAP = 128
GROUP_IMG = 2
CHUNK = 128

EPSILON = 1e-06
NEGATIVE = -1e30
HIGHEST = lax.Precision.HIGHEST
F32 = jnp.float32
BF16 = jnp.bfloat16
PLANE = ("x", "t")
EVERY = ("t", "z", "x")


def norm_forward(values, gains, shifts):
    middle = jnp.mean(values, -1, keepdims=True)
    centred = values - middle
    inverse = lax.rsqrt(jnp.mean(centred * centred, -1, keepdims=True) + EPSILON)
    unit_rows = centred * inverse
    return (unit_rows * gains + shifts, unit_rows, inverse)


def norm_backward(grad_rows, unit_rows, inverse, gains):
    scaled = grad_rows * gains
    return inverse * (
        scaled
        - jnp.mean(scaled, -1, keepdims=True)
        - unit_rows * jnp.mean(scaled * unit_rows, -1, keepdims=True)
    )


def gelu_exact(values):
    return jax.nn.gelu(values, approximate=False)


def dot(left, right, left_dim=1, right_dim=0):
    return lax.dot_general(
        left, right, (((left_dim,), (right_dim,)), ((), ())), preferred_element_type=F32
    )


def gather_line(own, length):
    if length != 4:
        return lax.all_gather(own, "z", axis=1, tiled=True)
    rows = own.shape[1]
    place = lax.axis_index("z")
    inward = lax.ppermute(own, "z", [(0, 1), (3, 2)])
    middle = lax.ppermute(jnp.concatenate([own, inward], 1), "z", [(1, 2), (2, 1)])
    outward = lax.ppermute(jnp.concatenate([own, middle], 1), "z", [(1, 0), (2, 3)])
    inner = (place == 1) | (place == 2)
    near = jnp.where(inner, inward, outward[:, :rows])
    far = jnp.where(inner, middle, outward[:, rows:])
    far_one, far_two = far[:, :rows], far[:, rows:]
    low = jnp.concatenate(
        [
            jnp.where(place == 0, own, near),
            jnp.where(place == 0, near, own),
            far_one,
            far_two,
        ],
        1,
    )
    high = jnp.concatenate(
        [
            far_two,
            far_one,
            jnp.where(place == 2, own, near),
            jnp.where(place == 2, near, own),
        ],
        1,
    )
    return jnp.where(place < 2, low, high)


def scatter_line(full, length):
    if length != 4:
        return lax.psum_scatter(
            full.astype(BF16), "z", scatter_dimension=1, tiled=True
        ).astype(F32)
    rows = full.shape[1] // 4
    place = lax.axis_index("z")
    piece = [full[:, k * rows : (k + 1) * rows] for k in range(4)]
    low = place < 2
    own = jnp.where(
        low,
        jnp.where(place == 0, piece[0], piece[1]),
        jnp.where(place == 2, piece[2], piece[3]),
    )
    near = jnp.where(
        low,
        jnp.where(place == 0, piece[1], piece[0]),
        jnp.where(place == 2, piece[3], piece[2]),
    )
    far_one = jnp.where(low, piece[2], piece[1])
    far_two = jnp.where(low, piece[3], piece[0])
    far = jnp.concatenate([far_one, far_two], 1)
    inward = lax.ppermute(
        jnp.concatenate([near, far], 1).astype(BF16), "z", [(0, 1), (3, 2)]
    )
    middle = lax.ppermute(
        (far + inward[:, rows:].astype(F32)).astype(BF16), "z", [(1, 2), (2, 1)]
    )
    outward = lax.ppermute(
        (near + middle[:, rows:].astype(F32)).astype(BF16), "z", [(1, 0), (2, 3)]
    )
    return (
        own
        + inward[:, :rows].astype(F32)
        + middle[:, :rows].astype(F32)
        + outward.astype(F32)
    )


def shards(
    tokens_in,
    key_mask,
    expert_ids,
    expert_slots,
    norm1_gain,
    norm1_shift,
    qkv_weight,
    qv_bias,
    out_weight,
    out_bias,
    norm2_gain,
    norm2_shift,
    router_weight,
    up_weight,
    up_bias,
    down_weight,
    down_bias,
    out_grad,
):
    length = lax.axis_size("z")
    quarter = lax.axis_size("t")
    core = lax.axis_index("t") % 2
    chip_y = lax.axis_index("t") // 2
    expert = lax.axis_index("x") * quarter + lax.axis_index("t")
    piece, sequence, model = tokens_in.shape
    experts, part, units = up_weight.shape
    dp = model // part
    width = qkv_weight.shape[2]
    heads = width // HD
    tokens = piece * sequence
    chunks = units // CHUNK

    smalls = jnp.concatenate(
        [
            norm1_gain[None],
            norm1_shift[None],
            qv_bias,
            out_bias[None],
            norm2_gain[None],
            norm2_shift[None],
            down_bias,
            router_weight.T,
            up_bias.reshape(experts * quarter, part),
        ],
        0,
    ).astype(BF16)
    small_rows = smalls.shape[0]
    pad = -(small_rows * part) % (16 * model)
    small_block = jnp.pad(smalls.reshape(-1), (0, pad)).reshape(-1, model)
    pack = jnp.concatenate(
        [
            jnp.concatenate(
                [qkv_weight[0], qkv_weight[1], qkv_weight[2], out_weight.T], 1
            ).astype(BF16),
            small_block,
        ],
        0,
    )
    packs = lax.all_gather(pack, EVERY, axis=0, tiled=False)
    packs = packs.reshape(quarter, dp, pack.shape[0], model)
    block = packs[:, :, :part].reshape(quarter, model, model)
    vectors = packs[0, :, part:].reshape(dp, -1)[:, : small_rows * part]
    vectors = vectors.reshape(dp, small_rows, part).transpose(1, 0, 2)
    lines = vectors[: 7 + 2 * experts].reshape(-1, model).astype(F32)
    gain_one, shift_one, bias_q, bias_v, bias_out, gain_two, shift_two = [
        lines[k] for k in range(7)
    ]
    bias_down = lines[7 : 7 + experts]
    router = lines[7 + experts :].astype(BF16)
    bias_up = vectors[7 + 2 * experts :].reshape(experts, quarter, dp, part)
    bias_up = bias_up.transpose(0, 2, 1, 3).reshape(experts, quarter, chunks, CHUNK)
    bias_up = lax.dynamic_index_in_dim(bias_up, expert, 0, keepdims=False)
    bias_up = bias_up.transpose(1, 0, 2).reshape(chunks, quarter * CHUNK).astype(F32)

    weights = jnp.stack(
        [up_weight.astype(BF16), down_weight.astype(BF16).transpose(0, 2, 1)], 1
    )
    parts = []
    for first, last in ((0, 1), (1, 3), (3, 6)):
        if first >= chunks:
            continue
        last = min(last, chunks) if last < 6 else chunks
        some = lax.all_to_all(
            weights[:, :, :, first * CHUNK : last * CHUNK], PLANE, 0, 0, tiled=True
        )
        some = some.reshape(2, quarter, 2, part, last - first, CHUNK)
        some = some.transpose(4, 2, 0, 3, 1, 5)
        some = some.reshape(last - first, 2, 2 * part, quarter * CHUNK)
        parts += [some[k] for k in range(last - first)]

    first_group = chip_y * 3
    group_tokens = GROUP_IMG * sequence
    position = (expert_ids * CAP + expert_slots).reshape(-1, group_tokens, 2)
    position_full = lax.dynamic_index_in_dim(position, first_group + 2 * core, 0, keepdims=False)
    position_half = lax.dynamic_index_in_dim(position, first_group + 1, 0, keepdims=False)
    slots_full = jnp.arange(experts * CAP, dtype=jnp.int32)
    half = CAP // 2
    slots_half = (
        jnp.arange(experts, dtype=jnp.int32)[:, None] * CAP
        + core * half
        + jnp.arange(half, dtype=jnp.int32)
    ).reshape(-1)
    match_full = slots_full[:, None, None] == position_full.T[None]
    match_half = slots_half[:, None, None] == position_half.T[None]
    hot_full = (match_full[:, 0] | match_full[:, 1]).astype(BF16)
    hot_half = (match_half[:, 0] | match_half[:, 1]).astype(BF16)
    swap = [(k, k ^ 1) for k in range(quarter)]

    def both_groups(values):
        lent = jnp.where(core == 0, values[2], values[0])
        other = lax.ppermute(lent, "t", swap)
        full = jnp.where(core == 0, values[:2], values[1:])
        shared = jnp.where(
            core == 0, jnp.stack([lent, other]), jnp.stack([other, lent])
        )
        return (
            full.reshape(group_tokens, -1),
            shared.reshape(group_tokens, -1),
        )

    def join_rows(full, shared):
        full = full.reshape((experts, CAP) + full.shape[1:])
        shared = shared.reshape((experts, half) + shared.shape[1:])
        return jnp.concatenate([full, shared], 1)

    def dispatch(full, shared):
        rows = join_rows(dot(hot_full, full).astype(BF16), dot(hot_half, shared).astype(BF16))
        return lax.all_to_all(rows, PLANE, 0, 0, tiled=True).reshape(-1, model)

    def combine(rows):
        back = lax.all_to_all(
            rows.reshape(experts, CAP + half, model), PLANE, 0, 0, tiled=True
        )
        full = dot(hot_full, back[:, :CAP].reshape(-1, model), 0, 0)
        shared = dot(hot_half, back[:, CAP:].reshape(-1, model), 0, 0)
        full = full.reshape(GROUP_IMG, sequence, model)
        shared = shared.reshape(GROUP_IMG, sequence, model)
        mine = jnp.where(core == 0, shared[0], shared[1])
        theirs = jnp.where(core == 0, shared[1], shared[0])
        mine = mine + lax.ppermute(theirs, "t", swap)
        return jnp.where(
            core == 0,
            jnp.concatenate([full, mine[None]]),
            jnp.concatenate([mine[None], full]),
        ).reshape(tokens, model)

    grad_full, grad_shared = both_groups(out_grad)
    incoming = dispatch(grad_full, grad_shared)

    local_start = lax.axis_index("t") * piece
    mask_here = lax.dynamic_slice_in_dim(key_mask, local_start, piece, 0)
    inputs = tokens_in.reshape(tokens, model).astype(F32)
    normed_one, unit_one, inverse_one = norm_forward(inputs, gain_one, shift_one)
    normed_one = normed_one.astype(BF16)
    projected = jnp.einsum(
        "sd,tdk->tsk", normed_one, block[:, :, : 3 * width], preferred_element_type=F32
    )
    shape_heads = (quarter, piece, sequence, heads, HD)

    def to_heads(values):
        return values.astype(BF16).reshape(shape_heads)

    queries = to_heads(projected[..., :width] + bias_q.reshape(quarter, 1, width))
    key_rows = to_heads(projected[..., width : 2 * width])
    value_rows = to_heads(projected[..., 2 * width :] + bias_v.reshape(quarter, 1, width))

    def scores_of():
        scores = jnp.einsum(
            "tbihc,tbjhc->tbhij", queries, key_rows, preferred_element_type=F32
        ) * HD ** (-0.5)
        return jnp.where(mask_here[None, :, None, None, :] > 0, scores, NEGATIVE)

    masked = scores_of()
    largest = jnp.max(masked, -1, keepdims=True)
    log_total = largest + jnp.log(jnp.sum(jnp.exp(masked - largest), -1, keepdims=True))
    chances = jnp.exp(masked - log_total)
    chances_low = chances.astype(BF16)
    attended = jnp.einsum(
        "tbhij,tbjhc->tbihc", chances_low, value_rows, preferred_element_type=F32
    )
    attended = attended.astype(BF16).reshape(quarter, tokens, width)
    out_rows = block[:, :, 3 * width :]
    attention_out = jnp.einsum("tsk,tdk->sd", attended, out_rows, preferred_element_type=F32)
    residual = inputs + attention_out + bias_out
    normed_two, unit_two, inverse_two = norm_forward(residual, gain_two, shift_two)
    normed_two = normed_two.astype(BF16)

    normed_full, normed_shared = both_groups(normed_two.reshape(piece, sequence, model))

    def chances_of(rows):
        return jax.nn.softmax(dot(rows, router, 1, 1), -1)

    probabilities = chances_of(normed_two)
    hot_ids = expert_ids[..., None] == jnp.arange(experts, dtype=jnp.int32)
    hot_here = lax.dynamic_slice_in_dim(hot_ids, local_start, piece, 0).astype(F32)
    hot_here = hot_here.reshape(tokens, 2, experts)
    share_here = jnp.sum(hot_here, 1) * probabilities

    def slot_gates(match, rows, position_here):
        chance = chances_of(rows)
        hot = (position_here // CAP)[..., None] == jnp.arange(experts, dtype=jnp.int32)
        gates = jnp.sum(hot.astype(F32) * chance[:, None], -1)
        return jnp.sum(jnp.where(match, gates.T[None], 0.0), (1, 2))

    gates_sent = join_rows(
        slot_gates(match_full, normed_full, position_full),
        slot_gates(match_half, normed_shared, position_half),
    )
    chosen = dispatch(normed_full, normed_shared)
    slot_gate = lax.all_to_all(gates_sent, PLANE, 0, 0, tiled=True).reshape(-1, 1)

    incoming_f = incoming.astype(F32)
    out_part = (incoming_f * slot_gate).astype(BF16)
    produced = jnp.zeros((chosen.shape[0], model), F32)
    pulled = jnp.zeros((chosen.shape[0], model), F32)
    bias_parts = []
    reduced = []
    for k in range(chunks):
        both = gather_line(parts[k], length)
        up_one, down_one = both[0], both[1]
        hidden = dot(chosen, up_one) + bias_up[k]
        active, pull_gelu = jax.vjp(gelu_exact, hidden)
        active = active.astype(BF16)
        produced = produced + dot(active, down_one, 1, 1)
        hidden_grad = pull_gelu(dot(out_part, down_one))[0].astype(BF16)
        pulled = pulled + dot(hidden_grad, up_one, 1, 1)
        bias_parts.append(jnp.sum(hidden_grad.astype(F32), 0))
        weight_grads = jnp.stack([dot(chosen, hidden_grad, 0, 0), dot(out_part, active, 0, 0)])
        reduced.append(scatter_line(weight_grads, length).astype(BF16))

    gate_part = jnp.sum(incoming_f * produced, -1)
    gate_back = lax.all_to_all(
        gate_part.reshape(experts, CAP + half), PLANE, 0, 0, tiled=True
    )
    norm_two_grad = combine(pulled.astype(BF16))
    mixture = combine((produced * slot_gate).astype(BF16))

    def slots_to_tokens(match, parts_here):
        parts_here = parts_here.reshape(experts, -1)
        match = (match[:, 0] | match[:, 1]).reshape(experts, -1, group_tokens)
        return jnp.sum(jnp.where(match, parts_here[..., None], 0.0), 1).T

    prob_full = slots_to_tokens(match_full, gate_back[:, :CAP])
    prob_shared = slots_to_tokens(match_half, gate_back[:, CAP:])
    prob_full = prob_full.reshape(GROUP_IMG, sequence, experts)
    prob_shared = prob_shared.reshape(GROUP_IMG, sequence, experts)
    mine = jnp.where(core == 0, prob_shared[0], prob_shared[1])
    theirs = jnp.where(core == 0, prob_shared[1], prob_shared[0])
    mine = mine + lax.ppermute(theirs, "t", swap)
    chance_grad = jnp.where(
        core == 0,
        jnp.concatenate([prob_full, mine[None]]),
        jnp.concatenate([mine[None], prob_full]),
    ).reshape(tokens, experts)
    grad_rows = out_grad.reshape(tokens, model)
    bias_dot = dot(grad_rows, bias_down.astype(BF16), 1, 1)
    chance_grad = chance_grad + jnp.sum(hot_here, 1) * bias_dot
    logit_grad = probabilities * (
        chance_grad - jnp.sum(probabilities * chance_grad, -1, keepdims=True)
    )
    logit_grad = logit_grad.astype(BF16)
    router_grad = dot(logit_grad, normed_two, 0, 0)
    bias_term = jnp.dot(share_here, bias_down, precision=HIGHEST)
    output = (residual + mixture + bias_term).astype(BF16).reshape(tokens_in.shape)

    grad_f = grad_rows.astype(F32)
    norm_two_grad = norm_two_grad + dot(logit_grad, router)
    down_bias_grad = lax.dot_general(
        share_here, grad_f, (((0,), (0,)), ((), ())), precision=HIGHEST
    )
    gain_two_grad = jnp.sum(norm_two_grad * unit_two, 0)
    shift_two_grad = jnp.sum(norm_two_grad, 0)
    residual_grad = grad_f + norm_backward(norm_two_grad, unit_two, inverse_two, gain_two)
    out_bias_grad = jnp.sum(residual_grad, 0)
    residual_low = residual_grad.astype(BF16)
    out_rows_grad = jnp.einsum(
        "sd,tsk->tdk", residual_low, attended, preferred_element_type=F32
    )
    attended_grad = jnp.einsum(
        "sd,tdk->tsk", residual_low, out_rows, preferred_element_type=F32
    )
    attended_grad = to_heads(attended_grad)
    value_grad = jnp.einsum(
        "tbhij,tbihc->tbjhc", chances_low, attended_grad, preferred_element_type=F32
    ).astype(BF16)
    weight_grad = jnp.einsum(
        "tbihc,tbjhc->tbhij", attended_grad, value_rows, preferred_element_type=F32
    )
    score_grad = chances * (
        weight_grad - jnp.sum(chances * weight_grad, -1, keepdims=True)
    )
    score_grad = score_grad.astype(BF16)
    scale = HD ** (-0.5)
    query_grad = (
        jnp.einsum("tbhij,tbjhc->tbihc", score_grad, key_rows, preferred_element_type=F32)
        * scale
    ).astype(BF16)
    key_grad = (
        jnp.einsum("tbhij,tbihc->tbjhc", score_grad, queries, preferred_element_type=F32)
        * scale
    ).astype(BF16)
    joined_grad = jnp.concatenate(
        [v.reshape(quarter, tokens, width) for v in (query_grad, key_grad, value_grad)], -1
    )
    qkv_grad = jnp.einsum(
        "sd,tsk->tdk", normed_one, joined_grad, preferred_element_type=F32
    )
    query_bias_grad = jnp.sum(query_grad.astype(F32), (1, 2)).reshape(model)
    value_bias_grad = jnp.sum(value_grad.astype(F32), (1, 2)).reshape(model)
    norm_one_grad = jnp.einsum(
        "tsk,tdk->sd", joined_grad, block[:, :, : 3 * width], preferred_element_type=F32
    )
    gain_one_grad = jnp.sum(norm_one_grad * unit_one, 0)
    shift_one_grad = jnp.sum(norm_one_grad, 0)
    input_grad = residual_grad + norm_backward(
        norm_one_grad, unit_one, inverse_one, gain_one
    )

    bias_rows = jnp.stack(bias_parts).reshape(chunks, quarter, CHUNK)
    bias_rows = bias_rows.transpose(1, 0, 2).reshape(dp, quarter, part)
    bias_rows = jnp.where(
        jnp.arange(experts)[:, None, None, None] == expert, bias_rows[None], 0.0
    )
    bias_rows = bias_rows.transpose(0, 2, 1, 3).reshape(experts * quarter, dp, part)
    line_grads = jnp.concatenate(
        [
            jnp.stack(
                [
                    gain_one_grad,
                    shift_one_grad,
                    query_bias_grad,
                    value_bias_grad,
                    out_bias_grad,
                    gain_two_grad,
                    shift_two_grad,
                ]
            ),
            down_bias_grad,
            router_grad,
        ],
        0,
    ).reshape(-1, dp, part)
    vector_grads = jnp.concatenate([line_grads, bias_rows], 0).astype(BF16)
    vector_grads = vector_grads.transpose(1, 0, 2).reshape(dp, small_rows * part)
    vector_grads = jnp.pad(vector_grads, ((0, 0), (0, pad))).reshape(dp, -1, model)
    pack_grads = jnp.concatenate(
        [
            jnp.concatenate([qkv_grad, out_rows_grad], -1)
            .astype(BF16)
            .reshape(quarter, dp, part, model),
            jnp.broadcast_to(vector_grads[None], (quarter,) + vector_grads.shape),
        ],
        2,
    )
    pack_grads = pack_grads.reshape((quarter * dp,) + pack_grads.shape[2:])
    pack_grad = lax.psum_scatter(pack_grads, EVERY, scatter_dimension=0, tiled=False)
    pack_grad = pack_grad.astype(F32)
    qkv_out = pack_grad[:part, : 3 * width].reshape(part, 3, width).transpose(1, 0, 2)
    out_weight_grad = pack_grad[:part, 3 * width :].T
    small_grads = pack_grad[part:].reshape(-1)[: small_rows * part].reshape(small_rows, part)

    ups, downs = [], []
    for first, last in ((0, 2), (2, 4), (4, 6)):
        if first >= chunks:
            continue
        last = min(last, chunks) if last < 6 else chunks
        some = jnp.stack(reduced[first:last])
        some = some.reshape(last - first, 2, 2, part, quarter, CHUNK)
        some = some.transpose(2, 4, 1, 3, 0, 5).reshape(experts, 2, part, -1)
        some = lax.all_to_all(some, PLANE, 0, 0, tiled=True).astype(F32)
        ups.append(some[:, 0])
        downs.append(some[:, 1])
    up_grad = jnp.concatenate(ups, -1)
    down_grad = jnp.concatenate(downs, -1).transpose(0, 2, 1)
    return (
        output,
        input_grad.reshape(tokens_in.shape),
        small_grads[0],
        small_grads[1],
        qkv_out,
        small_grads[2:4],
        out_weight_grad,
        small_grads[4],
        small_grads[5],
        small_grads[6],
        small_grads[7 + experts : 7 + 2 * experts].T,
        up_grad,
        small_grads[7 + 2 * experts :].reshape(experts, -1),
        down_grad,
        small_grads[7 : 7 + experts],
    )


def solution(mesh):
    dp, tensor = mesh.devices.shape
    planes = Mesh(mesh.devices.reshape(dp // 2, 2, tensor), ("z", "x", "t"))
    rows = ("z", "x")
    images = P(("z", "x", "t"), None, None)
    return jax.shard_map(
        shards,
        mesh=planes,
        in_specs=(
            images,
            P(rows, None),
            P(rows, None, None),
            P(rows, None, None),
            P(rows),
            P(rows),
            P(None, rows, "t"),
            P(None, rows),
            P("t", rows),
            P(rows),
            P(rows),
            P(rows),
            P(rows, None),
            P(None, rows, "t"),
            P(None, rows),
            P(None, "t", rows),
            P(None, rows),
            images,
        ),
        out_specs=(
            images,
            images,
            P(rows),
            P(rows),
            P(None, rows, "t"),
            P(None, rows),
            P("t", rows),
            P(rows),
            P(rows),
            P(rows),
            P(rows, None),
            P(None, rows, "t"),
            P(None, rows),
            P(None, "t", rows),
            P(None, rows),
        ),
        check_vma=False,
    )
```

```python
import functools
import jax
import jax.numpy as jnp
from jax import lax
from jax.experimental import pallas as pl
from jax.experimental.pallas import tpu as pltpu
from jax.sharding import PartitionSpec as P

HD = 64
EPSILON = 1e-06
NEGATIVE = -1e30
F32 = jnp.float32
BF16 = jnp.bfloat16


def dot(left, right, left_dim=1, right_dim=0):
    return lax.dot_general(
        left, right, (((left_dim,), (right_dim,)), ((), ())), preferred_element_type=F32
    )


def norm_forward(values, gains, shifts):
    middle = jnp.mean(values, -1, keepdims=True)
    centred = values - middle
    inverse = lax.rsqrt(jnp.mean(centred * centred, -1, keepdims=True) + EPSILON)
    unit_rows = centred * inverse
    return (unit_rows * gains + shifts, unit_rows, inverse)


def norm_backward(grad_rows, unit_rows, inverse, gains):
    scaled = grad_rows * gains
    return inverse * (
        scaled
        - jnp.mean(scaled, -1, keepdims=True)
        - unit_rows * jnp.mean(scaled * unit_rows, -1, keepdims=True)
    )


def head_masks(width):
    lane = lax.broadcasted_iota(jnp.int32, (1, width), 1)
    return [(lane // HD == k) for k in range(width // HD)]


def attend_forward_kernel(
    tokens_ref, mask_ref, wq_ref, wk_ref, wv_ref, wo_ref, lines_ref, bias_ref,
    n1_ref, n2_ref, h_ref, q_ref, k_ref, v_ref, o_ref, lse_ref,
):
    x = tokens_ref[0].astype(F32)
    n1, _, _ = norm_forward(x, lines_ref[0:1, :], lines_ref[1:2, :])
    n1 = n1.astype(BF16)
    n1_ref[0] = n1
    width = wq_ref.shape[2]
    masks = head_masks(width)
    keys = mask_ref[0] > 0
    total = x + lines_ref[4:5, :]
    for t in range(wq_ref.shape[0]):
        q = (dot(n1, wq_ref[t]) + bias_ref[t, 0:1, :]).astype(BF16)
        k = dot(n1, wk_ref[t]).astype(BF16)
        v = (dot(n1, wv_ref[t]) + bias_ref[t, 1:2, :]).astype(BF16)
        q_ref[0, t] = q
        k_ref[0, t] = k
        v_ref[0, t] = v
        scaled = q * jnp.asarray(HD ** (-0.5), BF16)
        o = jnp.zeros(q.shape, F32)
        for h, here in enumerate(masks):
            s = dot(jnp.where(here, scaled, jnp.zeros_like(scaled)), k, 1, 1)
            s = jnp.where(keys, s, NEGATIVE)
            largest = jnp.max(s, -1, keepdims=True)
            e = jnp.exp(s - largest)
            total_e = jnp.sum(e, -1, keepdims=True)
            p = (e / total_e).astype(BF16)
            o = jnp.where(here, dot(p, v), o)
            index = t * len(masks) + h
            lse_ref[0, :, index : index + 1] = largest + jnp.log(total_e)
        o = o.astype(BF16)
        o_ref[0, t] = o
        total = total + dot(o, wo_ref[t], 1, 1)
    h_ref[0] = total
    n2, _, _ = norm_forward(total, lines_ref[5:6, :], lines_ref[6:7, :])
    n2_ref[0] = n2.astype(BF16)


def whole(shape):
    return pl.BlockSpec(shape, lambda b: (0,) * len(shape))


def by_image(shape):
    return pl.BlockSpec((1,) + shape[1:], lambda b: (b,) + (0,) * (len(shape) - 1))


def attend_forward(tokens_in, mask, wq, wk, wv, wo, lines, bias_pairs):
    images, sequence, model = tokens_in.shape
    quarter, _, width = wq.shape
    rows = (images, sequence, model)
    heads = (images, quarter, sequence, width)
    outs = [
        (rows, BF16), (rows, BF16), (rows, F32), (heads, BF16), (heads, BF16),
        (heads, BF16), (heads, BF16), ((images, sequence, 128), F32),
    ]
    return pl.pallas_call(
        attend_forward_kernel,
        grid=(images,),
        in_specs=[
            by_image(tokens_in.shape),
            by_image(mask.shape),
            whole(wq.shape), whole(wk.shape), whole(wv.shape), whole(wo.shape),
            whole(lines.shape), whole(bias_pairs.shape),
        ],
        out_specs=[by_image(s) for s, _ in outs],
        out_shape=[jax.ShapeDtypeStruct(s, d) for s, d in outs],
        compiler_params=pltpu.CompilerParams(vmem_limit_bytes=56 * 2**20),
        cost_estimate=pl.CostEstimate(flops=3 * 10**9, bytes_accessed=2 * 10**7, transcendentals=2 * 10**6),
        name="attend_forward",
    )(tokens_in, mask, wq, wk, wv, wo, lines, bias_pairs)


def attend_backward_kernel(
    n2_grad_ref, grad_ref, tokens_ref, h_ref, mask_ref, wq_ref, wk_ref, wv_ref, wo_ref, lines_ref,
    n1_ref, q_ref, k_ref, v_ref, o_ref, lse_ref,
    input_grad_ref, dwq_ref, dwk_ref, dwv_ref, dwo_ref, vec_ref, pair_ref,
):
    first = pl.program_id(0) == 0

    @pl.when(first)
    def _():
        for ref in (dwq_ref, dwk_ref, dwv_ref, dwo_ref, vec_ref, pair_ref):
            ref[...] = jnp.zeros_like(ref)

    grad = grad_ref[0].astype(F32)
    n2_grad = n2_grad_ref[0]
    _, unit_two, inverse_two = norm_forward(h_ref[0], lines_ref[5:6, :], lines_ref[6:7, :])
    vec_ref[5:6, :] += jnp.sum(n2_grad * unit_two, 0, keepdims=True)
    vec_ref[6:7, :] += jnp.sum(n2_grad, 0, keepdims=True)
    h_grad = grad + norm_backward(n2_grad, unit_two, inverse_two, lines_ref[5:6, :])
    vec_ref[4:5, :] += jnp.sum(h_grad, 0, keepdims=True)
    hb = h_grad.astype(BF16)
    n1 = n1_ref[0]
    width = wq_ref.shape[2]
    masks = head_masks(width)
    keys = mask_ref[0] > 0
    scale = HD ** (-0.5)
    n1_grad = jnp.zeros(grad.shape, F32)
    for t in range(wq_ref.shape[0]):
        o = o_ref[0, t]
        dwo_ref[t] += dot(hb, o, 0, 0)
        do = dot(hb, wo_ref[t]).astype(BF16)
        q, k, v = q_ref[0, t], k_ref[0, t], v_ref[0, t]
        zero = jnp.zeros_like(q)
        scaled = q * jnp.asarray(scale, BF16)
        dq = jnp.zeros(q.shape, F32)
        dk = jnp.zeros(q.shape, F32)
        dv = jnp.zeros(q.shape, F32)
        for h, here in enumerate(masks):
            index = t * len(masks) + h
            s = dot(jnp.where(here, scaled, zero), k, 1, 1)
            s = jnp.where(keys, s, NEGATIVE)
            p = jnp.exp(s - lse_ref[0, :, index : index + 1])
            dp = dot(jnp.where(here, do, zero), v, 1, 1)
            ds = p * (dp - jnp.sum(p * dp, -1, keepdims=True))
            ds = ds.astype(BF16)
            dv = jnp.where(here, dot(p.astype(BF16), do, 0, 0), dv)
            dq = jnp.where(here, dot(ds, k), dq)
            dk = jnp.where(here, dot(ds, q, 0, 0), dk)
        dq = (dq * scale).astype(BF16)
        dk = (dk * scale).astype(BF16)
        dv = dv.astype(BF16)
        pair_ref[t, 0:1, :] += jnp.sum(dq.astype(F32), 0, keepdims=True)
        pair_ref[t, 1:2, :] += jnp.sum(dv.astype(F32), 0, keepdims=True)
        dwq_ref[t] += dot(n1, dq, 0, 0)
        dwk_ref[t] += dot(n1, dk, 0, 0)
        dwv_ref[t] += dot(n1, dv, 0, 0)
        n1_grad += dot(dq, wq_ref[t], 1, 1) + dot(dk, wk_ref[t], 1, 1) + dot(dv, wv_ref[t], 1, 1)
    _, unit_one, inverse_one = norm_forward(
        tokens_ref[0].astype(F32), lines_ref[0:1, :], lines_ref[1:2, :]
    )
    vec_ref[0:1, :] += jnp.sum(n1_grad * unit_one, 0, keepdims=True)
    vec_ref[1:2, :] += jnp.sum(n1_grad, 0, keepdims=True)
    input_grad_ref[0] = h_grad + norm_backward(n1_grad, unit_one, inverse_one, lines_ref[0:1, :])


def attend_backward(n2_grad, out_grad, tokens_in, h, mask, wq, wk, wv, wo, lines, n1, q, k, v, o, lse):
    ins = (n2_grad, out_grad, tokens_in, h, mask, wq, wk, wv, wo, lines, n1, q, k, v, o, lse)
    shared = {5, 6, 7, 8, 9}
    outs = [
        (n2_grad.shape, F32), (wq.shape, F32), (wq.shape, F32), (wq.shape, F32), (wq.shape, F32),
        ((8, n2_grad.shape[2]), F32), ((wq.shape[0], 8, wq.shape[2]), F32),
    ]
    return pl.pallas_call(
        attend_backward_kernel,
        grid=(n2_grad.shape[0],),
        in_specs=[whole(a.shape) if i in shared else by_image(a.shape) for i, a in enumerate(ins)],
        out_specs=[by_image(outs[0][0])] + [whole(s) for s, _ in outs[1:]],
        out_shape=[jax.ShapeDtypeStruct(s, d) for s, d in outs],
        compiler_params=pltpu.CompilerParams(vmem_limit_bytes=56 * 2**20),
        cost_estimate=pl.CostEstimate(flops=8 * 10**9, bytes_accessed=4 * 10**7, transcendentals=2 * 10**6),
        name="attend_backward",
    )(*ins)


def expert_kernel(first, order_ref, x_ref, g_ref, w_ref, b_ref, *refs):
    if first:
        y_out, p_out, bias_ref, *grads, acc_ref = refs
    else:
        y_in, p_in, y_out, p_out, bias_ref, *grads, acc_ref = refs
    step = pl.program_id(0)

    @pl.when(step == 0)
    def _():
        acc_ref[...] = jnp.zeros_like(acc_ref)
        bias_ref[...] = jnp.zeros_like(bias_ref)

    x = x_ref[...]
    g = g_ref[...]
    hidden = dot(x, w_ref[0]) + b_ref[...]
    cdf = 0.5 * (1.0 + lax.erf(hidden * (0.5 ** 0.5)))
    active = (hidden * cdf).astype(BF16)
    slope = cdf + hidden * (jnp.exp(-0.5 * hidden * hidden) * 0.3989422804014327)
    hidden_grad = (dot(g, w_ref[1]) * slope).astype(BF16)
    y = dot(active, w_ref[1], 1, 1)
    p = dot(hidden_grad, w_ref[0], 1, 1)
    if first:
        y_out[...] = y
        p_out[...] = p
    else:
        y_out[...] = y_in[...] + y
        p_out[...] = p_in[...] + p
    bias_ref[...] += jnp.sum(hidden_grad.astype(F32), 0, keepdims=True)
    acc_ref[0] += dot(x, hidden_grad, 0, 0)
    acc_ref[1] += dot(g, active, 0, 0)

    @pl.when(step == pl.num_programs(0) - 1)
    def _():
        for k, ref in enumerate(grads):
            rows = ref.shape[1]
            start = pl.multiple_of(order_ref[k] * rows, 16)
            for side in range(2):
                ref[side] = acc_ref[side, pl.ds(start, rows), :].astype(ref.dtype)


def expert_chunk(order, x, g, w, b, sums, pieces, piece_type):
    count, model = x.shape
    block = 256
    units = w.shape[2]
    row = lambda: pl.BlockSpec((block, model), lambda i, o: (i, 0))
    full = lambda shape: pl.BlockSpec(shape, lambda i, o: (0,) * len(shape))
    first = sums is None
    ins = [x, g, w, b] + ([] if first else list(sums))
    in_specs = [row(), row(), full(w.shape), full(b.shape)] + ([] if first else [row(), row()])
    piece = (2, model // pieces, units)
    outs = [((count, model), F32), ((count, model), F32), (b.shape, F32)] + [(piece, piece_type)] * pieces
    return pl.pallas_call(
        functools.partial(expert_kernel, first),
        grid_spec=pltpu.PrefetchScalarGridSpec(
            num_scalar_prefetch=1,
            grid=(count // block,),
            in_specs=in_specs,
            out_specs=[row(), row(), full(b.shape)] + [full(piece)] * pieces,
            scratch_shapes=[pltpu.VMEM((2, model, units), F32)],
        ),
        out_shape=[jax.ShapeDtypeStruct(s, d) for s, d in outs],
        input_output_aliases={} if first else {5: 0, 6: 1},
        compiler_params=pltpu.CompilerParams(vmem_limit_bytes=56 * 2**20),
        cost_estimate=pl.CostEstimate(flops=12 * count * model * units, bytes_accessed=3 * 10**7, transcendentals=2 * count * units),
        name="expert_chunk",
    )(order, *ins)


CAP = 128
GROUP_IMG = 2
CHUNK = 128
HIGHEST = lax.Precision.HIGHEST
PLANE = ("x", "t")
EVERY = ("t", "z", "x")
INWARD = [(0, 1), (3, 2)]
MIDDLE = [(1, 2), (2, 1)]
OUTWARD = [(1, 0), (2, 3)]
ORDER = ((0, 1, 2, 3), (1, 0, 2, 3), (2, 3, 1, 0), (3, 2, 1, 0))


def tie(values, *events):
    events = [e for e in events if e is not None]
    if not events:
        return values
    return lax.optimization_barrier((values, *events))[0]


def gather_lines(owns, length):
    if length != 4:
        return [lax.all_gather(own, "z", axis=1, tiled=True) for own in owns]
    place = lax.axis_index("z")
    inner = (place == 1) | (place == 2)
    result = []
    last_in = last_mid = last_out = None
    for own in owns:
        inward = lax.ppermute(tie(own, last_in), "z", INWARD)
        middle_one = lax.ppermute(tie(own, last_mid), "z", MIDDLE)
        outward_one = lax.ppermute(tie(own, last_out), "z", OUTWARD)
        middle_two = lax.ppermute(inward, "z", MIDDLE)
        outward_two = lax.ppermute(middle_one, "z", OUTWARD)
        outward_three = lax.ppermute(middle_two, "z", OUTWARD)
        last_in, last_mid, last_out = inward, middle_one, outward_two
        near = jnp.where(inner, inward, outward_one)
        far_one = jnp.where(inner, middle_one, outward_two)
        far_two = jnp.where(inner, middle_two, outward_three)
        low = place < 2
        end = (place == 0) | (place == 3)
        first = jnp.where(end, own, near)
        second = jnp.where(end, near, own)
        result.append(
            jnp.concatenate(
                [
                    jnp.where(low, first, far_two),
                    jnp.where(low, second, far_one),
                    jnp.where(low, far_one, second),
                    jnp.where(low, far_two, first),
                ],
                1,
            )
        )
    return result


def scatter_line(pieces):
    if len(pieces) == 1:
        return lax.psum_scatter(pieces[0], "z", scatter_dimension=1, tiled=True)
    own, near, far_one, far_two = pieces

    def add(*terms):
        return sum(term.astype(F32) for term in terms).astype(BF16)

    inward_three = lax.ppermute(far_two, "z", INWARD)
    inward_two = lax.ppermute(far_one, "z", INWARD)
    inward_one = lax.ppermute(near, "z", INWARD)
    middle_two = lax.ppermute(add(far_two, inward_three), "z", MIDDLE)
    middle_one = lax.ppermute(add(far_one, inward_two), "z", MIDDLE)
    outward = lax.ppermute(add(near, middle_two), "z", OUTWARD)
    return add(own, inward_one, middle_one, outward)


def shards(
    tokens_in,
    key_mask,
    expert_ids,
    expert_slots,
    norm1_gain,
    norm1_shift,
    qkv_weight,
    qv_bias,
    out_weight,
    out_bias,
    norm2_gain,
    norm2_shift,
    router_weight,
    up_weight,
    up_bias,
    down_weight,
    down_bias,
    out_grad,
):
    length = lax.axis_size("z")
    quarter = lax.axis_size("t")
    core = lax.axis_index("t") % 2
    chip_y = lax.axis_index("t") // 2
    expert = lax.axis_index("x") * quarter + lax.axis_index("t")
    piece, sequence, model = tokens_in.shape
    experts, part, units = up_weight.shape
    dp = model // part
    width = qkv_weight.shape[2]
    tokens = piece * sequence
    blocks = units // CHUNK
    spans = [(0, 1), (1, 3), (3, 5), (5, 6)] if blocks == 6 else [(0, blocks)]

    smalls = jnp.concatenate(
        [
            norm1_gain[None],
            norm1_shift[None],
            qv_bias,
            out_bias[None],
            norm2_gain[None],
            norm2_shift[None],
            down_bias,
            router_weight.T,
            up_bias.reshape(experts * quarter, part),
        ],
        0,
    ).astype(BF16)
    small_rows = smalls.shape[0]
    pad = -(small_rows * part) % (16 * model)
    small_block = jnp.pad(smalls.reshape(-1), (0, pad)).reshape(-1, model)
    pack = jnp.concatenate(
        [
            jnp.concatenate(
                [qkv_weight[0], qkv_weight[1], qkv_weight[2], out_weight.T], 1
            ).astype(BF16),
            small_block,
        ],
        0,
    )
    packs = lax.all_gather(pack, EVERY, axis=0, tiled=False)
    packs = packs.reshape(quarter, dp, pack.shape[0], model)
    wq, wk, wv, wo = [
        packs[:, :, :part, k * width : (k + 1) * width].reshape(quarter, model, width)
        for k in range(4)
    ]
    vectors = packs[0, :, part:].reshape(dp, -1)[:, : small_rows * part]
    vectors = vectors.reshape(dp, small_rows, part).transpose(1, 0, 2)
    lines = vectors[: 7 + 2 * experts].reshape(-1, model).astype(F32)
    bias_pairs = lines[2:4].reshape(2, quarter, width).transpose(1, 0, 2)
    bias_down = lines[7 : 7 + experts]
    router = lines[7 + experts :].astype(BF16)
    bias_up = vectors[7 + 2 * experts :].reshape(experts, quarter, dp, part)
    bias_up = bias_up.transpose(0, 2, 1, 3).reshape(experts, quarter, units)
    bias_up = lax.dynamic_index_in_dim(bias_up, expert, 0, keepdims=False).astype(F32)

    parts = []
    event = None
    for first, last in spans:
        some = jnp.stack(
            [
                up_weight[:, :, first * CHUNK : last * CHUNK].astype(BF16),
                down_weight[:, first * CHUNK : last * CHUNK].astype(BF16).transpose(0, 2, 1),
            ],
            1,
        )
        some = lax.all_to_all(tie(some, event), PLANE, 0, 0, tiled=True)
        event = some
        some = some.reshape(2, quarter, 2, part, (last - first) * CHUNK)
        some = some.transpose(2, 0, 3, 1, 4)
        parts.append(some.reshape(2, 2 * part, quarter * (last - first) * CHUNK))

    first_group = chip_y * 3
    group_tokens = GROUP_IMG * sequence
    position = (expert_ids * CAP + expert_slots).reshape(-1, group_tokens, 2)
    position_full = lax.dynamic_index_in_dim(position, first_group + 2 * core, 0, keepdims=False)
    position_half = lax.dynamic_index_in_dim(position, first_group + 1, 0, keepdims=False)
    slots_full = jnp.arange(experts * CAP, dtype=jnp.int32)
    half = CAP // 2
    slots_half = (
        jnp.arange(experts, dtype=jnp.int32)[:, None] * CAP
        + core * half
        + jnp.arange(half, dtype=jnp.int32)
    ).reshape(-1)
    match_full = slots_full[:, None, None] == position_full.T[None]
    match_half = slots_half[:, None, None] == position_half.T[None]
    hot_full = (match_full[:, 0] | match_full[:, 1]).astype(BF16)
    hot_half = (match_half[:, 0] | match_half[:, 1]).astype(BF16)
    swap = [(k, k ^ 1) for k in range(quarter)]

    def both_groups(values):
        lent = jnp.where(core == 0, values[2], values[0])
        other = lax.ppermute(lent, "t", swap)
        full = jnp.where(core == 0, values[:2], values[1:])
        shared = jnp.where(core == 0, jnp.stack([lent, other]), jnp.stack([other, lent]))
        return (
            full.reshape(group_tokens, -1),
            shared.reshape(group_tokens, -1),
        )

    def join_rows(full, shared):
        full = full.reshape((experts, CAP) + full.shape[1:])
        shared = shared.reshape((experts, half) + shared.shape[1:])
        return jnp.concatenate([full, shared], 1)

    def dispatch(full, shared, after=None):
        rows = join_rows(dot(hot_full, full).astype(BF16), dot(hot_half, shared).astype(BF16))
        rows = tie(rows, after)
        return lax.all_to_all(rows, PLANE, 0, 0, tiled=True).reshape(-1, model)

    def combine(rows):
        back = lax.all_to_all(
            rows.reshape(experts, CAP + half, model), PLANE, 0, 0, tiled=True
        )
        full = dot(hot_full, back[:, :CAP].reshape(-1, model), 0, 0)
        shared = dot(hot_half, back[:, CAP:].reshape(-1, model), 0, 0)
        full = full.reshape(GROUP_IMG, sequence, model)
        shared = shared.reshape(GROUP_IMG, sequence, model)
        mine = jnp.where(core == 0, shared[0], shared[1])
        theirs = jnp.where(core == 0, shared[1], shared[0])
        mine = mine + lax.ppermute(theirs, "t", swap)
        return jnp.where(
            core == 0,
            jnp.concatenate([full, mine[None]]),
            jnp.concatenate([mine[None], full]),
        )

    grad_full, grad_shared = both_groups(out_grad)
    incoming = dispatch(grad_full, grad_shared, event)

    local_start = lax.axis_index("t") * piece
    mask_here = lax.dynamic_slice_in_dim(key_mask, local_start, piece, 0)[:, None]
    n1, n2, residual, q, k, v, attended, lse = attend_forward(
        tokens_in, mask_here, wq, wk, wv, wo, lines, bias_pairs
    )
    normed_two = n2.reshape(tokens, model)

    normed_full, normed_shared = both_groups(n2)

    def chances_of(rows):
        return jax.nn.softmax(dot(rows, router, 1, 1), -1)

    probabilities = chances_of(normed_two)
    hot_ids = expert_ids[..., None] == jnp.arange(experts, dtype=jnp.int32)
    hot_here = lax.dynamic_slice_in_dim(hot_ids, local_start, piece, 0).astype(F32)
    hot_here = jnp.sum(hot_here.reshape(tokens, 2, experts), 1)
    share_here = hot_here * probabilities

    def slot_gates(match, rows, position_here):
        chance = chances_of(rows)
        hot = (position_here // CAP)[..., None] == jnp.arange(experts, dtype=jnp.int32)
        gates = jnp.sum(hot.astype(F32) * chance[:, None], -1)
        return jnp.sum(jnp.where(match, gates.T[None], 0.0), (1, 2))

    gates_sent = join_rows(
        slot_gates(match_full, normed_full, position_full),
        slot_gates(match_half, normed_shared, position_half),
    )
    chosen = dispatch(normed_full, normed_shared, incoming)
    slot_gate = lax.all_to_all(gates_sent, PLANE, 0, 0, tiled=True).reshape(-1, 1)

    incoming_f = incoming.astype(F32)
    out_part = (incoming_f * slot_gate).astype(BF16)
    place = lax.axis_index("z")
    pieces, piece_type = (4, BF16) if length == 4 else (1, F32)
    order = jnp.asarray(ORDER if length == 4 else [[0]] * length, jnp.int32)
    order = lax.dynamic_index_in_dim(order, place, 0, keepdims=False)
    sums = None
    bias_parts = []
    reduced = []
    for (first, last), both in zip(spans, gather_lines(parts, length)):
        bias_one = bias_up[:, first * CHUNK : last * CHUNK].reshape(1, -1)
        produced, pulled, bias_part, *grads = expert_chunk(
            order, chosen, out_part, both, bias_one, sums, pieces, piece_type
        )
        sums = (produced, pulled)
        bias_parts.append(bias_part.reshape(quarter, -1))
        reduced.append(scatter_line(grads).astype(BF16))

    gate_part = jnp.sum(incoming_f * produced, -1)
    gate_back = lax.all_to_all(
        gate_part.reshape(experts, CAP + half), PLANE, 0, 0, tiled=True
    )
    norm_two_grad = combine(pulled.astype(BF16))

    def slots_to_tokens(match, parts_here):
        parts_here = parts_here.reshape(experts, -1)
        match = (match[:, 0] | match[:, 1]).reshape(experts, -1, group_tokens)
        return jnp.sum(jnp.where(match, parts_here[..., None], 0.0), 1).T

    prob_full = slots_to_tokens(match_full, gate_back[:, :CAP])
    prob_shared = slots_to_tokens(match_half, gate_back[:, CAP:])
    prob_full = prob_full.reshape(GROUP_IMG, sequence, experts)
    prob_shared = prob_shared.reshape(GROUP_IMG, sequence, experts)
    mine = jnp.where(core == 0, prob_shared[0], prob_shared[1])
    theirs = jnp.where(core == 0, prob_shared[1], prob_shared[0])
    mine = mine + lax.ppermute(theirs, "t", swap)
    chance_grad = jnp.where(
        core == 0,
        jnp.concatenate([prob_full, mine[None]]),
        jnp.concatenate([mine[None], prob_full]),
    ).reshape(tokens, experts)
    grad_rows = out_grad.reshape(tokens, model)
    bias_dot = dot(grad_rows, bias_down.astype(BF16), 1, 1)
    chance_grad = chance_grad + hot_here * bias_dot
    logit_grad = probabilities * (
        chance_grad - jnp.sum(probabilities * chance_grad, -1, keepdims=True)
    )
    logit_grad = logit_grad.astype(BF16)
    router_grad = dot(logit_grad, normed_two, 0, 0)
    down_bias_grad = lax.dot_general(
        share_here, grad_rows.astype(F32), (((0,), (0,)), ((), ())), precision=HIGHEST
    )

    norm_two_grad = norm_two_grad + dot(logit_grad, router).reshape(norm_two_grad.shape)
    input_grad, dwq, dwk, dwv, dwo, line_sums, pair_sums = attend_backward(
        norm_two_grad, out_grad, tokens_in, residual, mask_here, wq, wk, wv, wo, lines,
        n1, q, k, v, attended, lse,
    )
    mixture = combine(tie((produced * slot_gate).astype(BF16), norm_two_grad))
    bias_term = jnp.dot(share_here, bias_down, precision=HIGHEST).reshape(residual.shape)
    output = (residual + mixture + bias_term).astype(BF16)

    bias_rows = jnp.concatenate(bias_parts, 1).reshape(dp, quarter, part)
    bias_rows = jnp.where(
        jnp.arange(experts)[:, None, None, None] == expert, bias_rows[None], 0.0
    )
    bias_rows = bias_rows.transpose(0, 2, 1, 3).reshape(experts * quarter, dp, part)
    line_grads = jnp.concatenate(
        [
            line_sums[0:2],
            pair_sums[:, 0].reshape(1, model),
            pair_sums[:, 1].reshape(1, model),
            line_sums[4:7],
            down_bias_grad,
            router_grad,
        ],
        0,
    ).reshape(-1, dp, part)
    sum_type = BF16 if length == 4 else F32
    vector_grads = jnp.concatenate([line_grads, bias_rows], 0).astype(sum_type)
    vector_grads = vector_grads.transpose(1, 0, 2).reshape(dp, small_rows * part)
    vector_grads = jnp.pad(vector_grads, ((0, 0), (0, pad))).reshape(dp, -1, model)
    pack_grads = jnp.concatenate(
        [
            jnp.concatenate([dwq, dwk, dwv, dwo], -1)
            .astype(sum_type)
            .reshape(quarter, dp, part, model),
            jnp.broadcast_to(vector_grads[None], (quarter,) + vector_grads.shape),
        ],
        2,
    )
    pack_grads = pack_grads.reshape((quarter * dp,) + pack_grads.shape[2:])
    pack_grad = lax.psum_scatter(pack_grads, EVERY, scatter_dimension=0, tiled=False)
    pack_grad = pack_grad.astype(F32)
    qkv_out = pack_grad[:part, : 3 * width].reshape(part, 3, width).transpose(1, 0, 2)
    out_weight_grad = pack_grad[:part, 3 * width :].T
    small_grads = pack_grad[part:].reshape(-1)[: small_rows * part].reshape(small_rows, part)

    ups, downs = [], []
    event = norm_two_grad
    for some in reduced:
        some = some.reshape(2, 2, part, quarter, -1)
        some = some.transpose(1, 3, 0, 2, 4).reshape(experts, 2, part, -1)
        some = lax.all_to_all(some, PLANE, 0, 0, tiled=True).astype(F32)
        ups.append(some[:, 0])
        downs.append(some[:, 1])
    up_grad = jnp.concatenate(ups, -1)
    down_grad = jnp.concatenate(downs, -1).transpose(0, 2, 1)
    return (
        output,
        input_grad,
        small_grads[0],
        small_grads[1],
        qkv_out,
        small_grads[2:4],
        out_weight_grad,
        small_grads[4],
        small_grads[5],
        small_grads[6],
        small_grads[7 + experts : 7 + 2 * experts].T,
        up_grad,
        small_grads[7 + 2 * experts :].reshape(experts, -1),
        down_grad,
        small_grads[7 : 7 + experts],
    )


def solution(mesh):
    dp, tensor = mesh.devices.shape
    planes = jax.sharding.Mesh(mesh.devices.reshape(dp // 2, 2, tensor), ("z", "x", "t"))
    rows = ("z", "x")
    images = P(("z", "x", "t"), None, None)
    return jax.shard_map(
        shards,
        mesh=planes,
        in_specs=(
            images,
            P(rows, None),
            P(rows, None, None),
            P(rows, None, None),
            P(rows),
            P(rows),
            P(None, rows, "t"),
            P(None, rows),
            P("t", rows),
            P(rows),
            P(rows),
            P(rows),
            P(rows, None),
            P(None, rows, "t"),
            P(None, rows),
            P(None, "t", rows),
            P(None, rows),
            images,
        ),
        out_specs=(
            images,
            images,
            P(rows),
            P(rows),
            P(None, rows, "t"),
            P(None, rows),
            P("t", rows),
            P(rows),
            P(rows),
            P(rows),
            P(rows, None),
            P(None, rows, "t"),
            P(None, rows),
            P(None, "t", rows),
            P(None, rows),
        ),
        check_vma=False,
    )
```

```python
import functools
import jax
import jax.numpy as jnp
from jax import lax
from jax.experimental import pallas as pl
from jax.experimental.pallas import tpu as pltpu
from jax.sharding import PartitionSpec as P

HD = 64
EPSILON = 1e-06
NEGATIVE = -1e30
F32 = jnp.float32
BF16 = jnp.bfloat16


def dot(left, right, left_dim=1, right_dim=0):
    return lax.dot_general(
        left, right, (((left_dim,), (right_dim,)), ((), ())), preferred_element_type=F32
    )


def norm_forward(values, gains, shifts):
    middle = jnp.mean(values, -1, keepdims=True)
    centred = values - middle
    inverse = lax.rsqrt(jnp.mean(centred * centred, -1, keepdims=True) + EPSILON)
    unit_rows = centred * inverse
    return (unit_rows * gains + shifts, unit_rows, inverse)


def norm_backward(grad_rows, unit_rows, inverse, gains):
    scaled = grad_rows * gains
    return inverse * (
        scaled
        - jnp.mean(scaled, -1, keepdims=True)
        - unit_rows * jnp.mean(scaled * unit_rows, -1, keepdims=True)
    )


def head_masks(width):
    lane = lax.broadcasted_iota(jnp.int32, (1, width), 1)
    return [(lane // HD == k) for k in range(width // HD)]


def arrange(w_ref, *parts):
    width = parts[0].shape[2]
    for t in range(w_ref.shape[0]):
        packed = w_ref[t]
        for k, ref in enumerate(parts):
            ref[t] = packed[:, k * width : (k + 1) * width]


def put_rows(ref, values):
    rows, columns = values.shape
    spare = jnp.zeros((ref.shape[0] - rows, columns), values.dtype)
    ref[...] = jnp.concatenate([values, spare], 0).astype(ref.dtype)


def attend_forward_kernel(
    place_ref, tokens_ref, mask_ref, lines_ref, bias_ref, *refs,
):
    (
        n1_ref, n2_ref, h_ref, q_ref, k_ref, v_ref, o_ref, lse_ref,
        wq_ref, wk_ref, wv_ref, wo_ref, all_ref, sem,
    ) = refs[-14:]
    packs = refs[:-14]

    @pl.when(pl.program_id(0) == 0)
    def _():
        if len(packs) == 1:
            pltpu.make_async_copy(packs[0], all_ref, sem).start()
        else:
            z, x, y, c = [place_ref[k] for k in range(4)]
            part = all_ref.shape[1] // 8
            for index, ref in enumerate(packs):
                dx, dy, dc = index & 1, (index >> 1) & 1, index >> 2
                t = (y ^ dy) * 2 + (c ^ dc)
                for back in range(4):
                    row = (((z - back) & 3) * 2 + (x ^ dx)) * part
                    pltpu.make_async_copy(
                        ref.at[back, pl.ds(0, part)],
                        all_ref.at[t, pl.ds(pl.multiple_of(row, 32), part)],
                        sem,
                    ).start()
        pltpu.make_async_copy(all_ref, all_ref, sem).wait()
        arrange(all_ref, wq_ref, wk_ref, wv_ref, wo_ref)

    x = tokens_ref[0].astype(F32)
    n1, _, _ = norm_forward(x, lines_ref[0:1, :], lines_ref[1:2, :])
    put_rows(n1_ref.at[0], n1)
    n1 = n1.astype(BF16)
    width = wq_ref.shape[2]
    masks = head_masks(width)
    keys = mask_ref[0] > 0
    total = x + lines_ref[4:5, :]
    for t in range(wq_ref.shape[0]):
        q = (dot(n1, wq_ref[t]) + bias_ref[t, 0:1, :]).astype(BF16)
        k = dot(n1, wk_ref[t]).astype(BF16)
        v = (dot(n1, wv_ref[t]) + bias_ref[t, 1:2, :]).astype(BF16)
        q_ref[0, t] = q
        k_ref[0, t] = k
        v_ref[0, t] = v
        scaled = q * jnp.asarray(HD ** (-0.5), BF16)
        o = jnp.zeros(q.shape, F32)
        for h, here in enumerate(masks):
            s = dot(jnp.where(here, scaled, jnp.zeros_like(scaled)), k, 1, 1)
            s = jnp.where(keys, s, NEGATIVE)
            largest = jnp.max(s, -1, keepdims=True)
            e = jnp.exp(s - largest)
            total_e = jnp.sum(e, -1, keepdims=True)
            p = (e / total_e).astype(BF16)
            o = jnp.where(here, dot(p, v), o)
            index = t * len(masks) + h
            lse_ref[0, :, index : index + 1] = largest + jnp.log(total_e)
        put_rows(o_ref.at[0, t], o)
        total = total + dot(o.astype(BF16), wo_ref[t], 1, 1)
    h_ref[0] = total
    n2, _, _ = norm_forward(total, lines_ref[5:6, :], lines_ref[6:7, :])
    n2_ref[0] = n2.astype(BF16)


def whole(shape):
    return pl.BlockSpec(shape, lambda b: (0,) * len(shape))


def by_image(shape):
    return pl.BlockSpec((1,) + shape[1:], lambda b: (b,) + (0,) * (len(shape) - 1))


def padded(rows):
    return -(-rows // 16) * 16


def attend_forward(place, tokens_in, mask, lines, bias_pairs, packs, width):
    images, sequence, model = tokens_in.shape
    quarter = model // width
    rows = (images, sequence, model)
    heads = (images, quarter, sequence, width)
    columns = (quarter, model, width)
    outs = [
        ((images, padded(sequence), model), BF16), (rows, BF16), (rows, F32), (heads, BF16), (heads, BF16),
        (heads, BF16), ((images, quarter, padded(sequence), width), BF16), ((images, sequence, 128), F32),
        (columns, BF16), (columns, BF16), (columns, BF16), (columns, BF16),
    ]
    place_spec = lambda spec: pl.BlockSpec(spec.block_shape, lambda b, p: spec.index_map(b))
    in_specs = [by_image(tokens_in.shape), by_image(mask.shape), whole(lines.shape), whole(bias_pairs.shape)]
    out_specs = [by_image(s) for s, _ in outs[:8]] + [whole(s) for s, _ in outs[8:]]
    return pl.pallas_call(
        attend_forward_kernel,
        grid_spec=pltpu.PrefetchScalarGridSpec(
            num_scalar_prefetch=1,
            grid=(images,),
            in_specs=[place_spec(s) for s in in_specs]
            + [pl.BlockSpec(memory_space=pl.ANY)] * len(packs),
            out_specs=[place_spec(s) for s in out_specs],
            scratch_shapes=[pltpu.VMEM((quarter, model, 4 * width), BF16), pltpu.SemaphoreType.DMA(())],
        ),
        out_shape=[jax.ShapeDtypeStruct(s, d) for s, d in outs],
        compiler_params=pltpu.CompilerParams(vmem_limit_bytes=56 * 2**20),
        cost_estimate=pl.CostEstimate(flops=3 * 10**9, bytes_accessed=6 * 10**7, transcendentals=2 * 10**6),
        name="attend_forward",
    )(place, tokens_in, mask, lines, bias_pairs, *packs)


def attend_backward_kernel(
    n2_grad_ref, grad_ref, h_ref, mask_ref, wo_ref, lines_ref, q_ref, k_ref, v_ref, lse_ref,
    h_grad_ref, hb_ref, dq_ref, dk_ref, dv_ref, vec_ref, pair_ref,
):
    @pl.when(pl.program_id(0) == 0)
    def _():
        vec_ref[...] = jnp.zeros_like(vec_ref)
        pair_ref[...] = jnp.zeros_like(pair_ref)

    n2_grad = n2_grad_ref[0]
    _, unit_two, inverse_two = norm_forward(h_ref[0], lines_ref[5:6, :], lines_ref[6:7, :])
    vec_ref[1:2, :] += jnp.sum(n2_grad * unit_two, 0, keepdims=True)
    vec_ref[2:3, :] += jnp.sum(n2_grad, 0, keepdims=True)
    h_grad = grad_ref[0].astype(F32) + norm_backward(
        n2_grad, unit_two, inverse_two, lines_ref[5:6, :]
    )
    vec_ref[0:1, :] += jnp.sum(h_grad, 0, keepdims=True)
    h_grad_ref[0] = h_grad
    put_rows(hb_ref.at[0], h_grad)
    hb = h_grad.astype(BF16)
    width = wo_ref.shape[2]
    masks = head_masks(width)
    keys = mask_ref[0] > 0
    scale = HD ** (-0.5)
    for t in range(wo_ref.shape[0]):
        do = dot(hb, wo_ref[t]).astype(BF16)
        q, k, v = q_ref[0, t], k_ref[0, t], v_ref[0, t]
        zero = jnp.zeros_like(q)
        scaled = q * jnp.asarray(scale, BF16)
        dq = jnp.zeros(q.shape, F32)
        dk = jnp.zeros(q.shape, F32)
        dv = jnp.zeros(q.shape, F32)
        for h, here in enumerate(masks):
            index = t * len(masks) + h
            s = dot(jnp.where(here, scaled, zero), k, 1, 1)
            s = jnp.where(keys, s, NEGATIVE)
            p = jnp.exp(s - lse_ref[0, :, index : index + 1])
            dp = dot(jnp.where(here, do, zero), v, 1, 1)
            ds = p * (dp - jnp.sum(p * dp, -1, keepdims=True))
            ds = ds.astype(BF16)
            dv = jnp.where(here, dot(p.astype(BF16), do, 0, 0), dv)
            dq = jnp.where(here, dot(ds, k), dq)
            dk = jnp.where(here, dot(ds, q, 0, 0), dk)
        dq = (dq * scale).astype(BF16).astype(F32)
        dv = dv.astype(BF16).astype(F32)
        pair_ref[t, 0:1, :] += jnp.sum(dq, 0, keepdims=True)
        pair_ref[t, 1:2, :] += jnp.sum(dv, 0, keepdims=True)
        put_rows(dq_ref.at[0, t], dq)
        put_rows(dk_ref.at[0, t], dk * scale)
        put_rows(dv_ref.at[0, t], dv)


def attend_backward(n2_grad, out_grad, h, mask, wo, lines, q, k, v, lse):
    ins = (n2_grad, out_grad, h, mask, wo, lines, q, k, v, lse)
    shared = {4, 5}
    images, sequence, model = n2_grad.shape
    quarter, _, width = wo.shape
    heads = ((images, quarter, padded(sequence), width), BF16)
    outs = [
        (n2_grad.shape, F32), ((images, padded(sequence), model), BF16), heads, heads, heads,
        ((8, model), F32), ((quarter, 8, width), F32),
    ]
    return pl.pallas_call(
        attend_backward_kernel,
        grid=(images,),
        in_specs=[whole(a.shape) if i in shared else by_image(a.shape) for i, a in enumerate(ins)],
        out_specs=[by_image(s) for s, _ in outs[:5]] + [whole(s) for s, _ in outs[5:]],
        out_shape=[jax.ShapeDtypeStruct(s, d) for s, d in outs],
        compiler_params=pltpu.CompilerParams(vmem_limit_bytes=56 * 2**20),
        cost_estimate=pl.CostEstimate(flops=4 * 10**9, bytes_accessed=7 * 10**7, transcendentals=2 * 10**6),
        name="attend_backward",
    )(*ins)


def attend_weights_kernel(n1_ref, hb_ref, dq_ref, dk_ref, dv_ref, o_ref, *refs):
    out_ref = refs[-1]
    width = dq_ref.shape[3]
    n1 = n1_ref[...].reshape(-1, n1_ref.shape[2])
    hb = hb_ref[...].reshape(-1, n1_ref.shape[2])
    for k, (left, ref) in enumerate(((n1, dq_ref), (n1, dk_ref), (n1, dv_ref), (hb, o_ref))):
        sums = dot(left, ref[...].reshape(-1, width), 0, 0).astype(out_ref.dtype)
        columns = slice(k * width, (k + 1) * width)
        if len(refs) == 1:
            out_ref[0, :, columns] = sums
            continue
        part = sums.shape[0] // 8
        for z in range(4):
            for x in range(2):
                start = (z * 2 + x) * part
                out_ref[0, x, 0, z, :part, columns] = sums[start : start + part]
    if len(refs) == 2:
        for z in range(4):
            for x in range(2):
                out_ref[0, x, 0, z, part:, :] = refs[0][z * 2 + x]


def attend_weights(n1, hb, dq, dk, dv, o, extra):
    images, quarter, rows, width = dq.shape
    model = n1.shape[2]
    heads = pl.BlockSpec((images, 1, rows, width), lambda t: (0, t, 0, 0))
    if extra is None:
        out_spec = pl.BlockSpec((1, model, 4 * width), lambda t: (t, 0, 0))
        out_shape = jax.ShapeDtypeStruct((quarter, model, 4 * width), F32)
    else:
        depth = model // 8 + extra.shape[1]
        out_spec = pl.BlockSpec(
            (1, 2, 1, 4, depth, model), lambda t: (t % 2, 0, t // 2, 0, 0, 0)
        )
        out_shape = jax.ShapeDtypeStruct((2, 2, 2, 4, depth, model), BF16)
    extras = [] if extra is None else [extra]
    return pl.pallas_call(
        attend_weights_kernel,
        grid=(quarter,),
        in_specs=[whole(n1.shape), whole(hb.shape)] + [heads] * 4 + [whole(e.shape) for e in extras],
        out_specs=out_spec,
        out_shape=out_shape,
        compiler_params=pltpu.CompilerParams(vmem_limit_bytes=56 * 2**20),
        cost_estimate=pl.CostEstimate(flops=3 * 10**9, bytes_accessed=3 * 10**7, transcendentals=0),
        name="attend_weights",
    )(n1, hb, dq, dk, dv, o, *extras)


def input_backward_kernel(
    h_grad_ref, tokens_ref, wq_ref, wk_ref, wv_ref, lines_ref, dq_ref, dk_ref, dv_ref,
    input_grad_ref, vec_ref,
):
    @pl.when(pl.program_id(0) == 0)
    def _():
        vec_ref[...] = jnp.zeros_like(vec_ref)

    rows = tokens_ref.shape[1]
    n1_grad = jnp.zeros((dq_ref.shape[2], tokens_ref.shape[2]), F32)
    for t in range(wq_ref.shape[0]):
        for grads, weights in ((dq_ref, wq_ref), (dk_ref, wk_ref), (dv_ref, wv_ref)):
            n1_grad += dot(grads[0, t], weights[t], 1, 1)
    n1_grad = n1_grad[:rows]
    _, unit_one, inverse_one = norm_forward(
        tokens_ref[0].astype(F32), lines_ref[0:1, :], lines_ref[1:2, :]
    )
    vec_ref[0:1, :] += jnp.sum(n1_grad * unit_one, 0, keepdims=True)
    vec_ref[1:2, :] += jnp.sum(n1_grad, 0, keepdims=True)
    input_grad_ref[0] = h_grad_ref[0] + norm_backward(
        n1_grad, unit_one, inverse_one, lines_ref[0:1, :]
    )


def input_backward(h_grad, tokens_in, wq, wk, wv, lines, dq, dk, dv):
    ins = (h_grad, tokens_in, wq, wk, wv, lines, dq, dk, dv)
    outs = [(h_grad.shape, F32), ((8, wq.shape[1]), F32)]
    return pl.pallas_call(
        input_backward_kernel,
        grid=(h_grad.shape[0],),
        in_specs=[whole(a.shape) if 2 <= i <= 5 else by_image(a.shape) for i, a in enumerate(ins)],
        out_specs=[by_image(outs[0][0]), whole(outs[1][0])],
        out_shape=[jax.ShapeDtypeStruct(s, d) for s, d in outs],
        compiler_params=pltpu.CompilerParams(vmem_limit_bytes=56 * 2**20),
        cost_estimate=pl.CostEstimate(flops=3 * 10**9, bytes_accessed=3 * 10**7, transcendentals=0),
        name="input_backward",
    )(*ins)


def pack_experts_kernel(up_ref, down_ref, *refs):
    up = up_ref[0].astype(BF16)
    down = down_ref[0].T.astype(BF16)
    start = 0
    for ref in refs:
        stop = start + ref.shape[3]
        ref[0, 0] = up[:, start:stop]
        ref[0, 1] = down[:, start:stop]
        start = stop


def pack_experts(up, down, sizes):
    experts, part, units = up.shape
    outs = [(experts, 2, part, size) for size in sizes]
    return pl.pallas_call(
        pack_experts_kernel,
        grid=(experts,),
        in_specs=[by_image(up.shape), by_image(down.shape)],
        out_specs=[by_image(s) for s in outs],
        out_shape=[jax.ShapeDtypeStruct(s, BF16) for s in outs],
        compiler_params=pltpu.CompilerParams(vmem_limit_bytes=32 * 2**20),
        cost_estimate=pl.CostEstimate(flops=0, bytes_accessed=8 * 10**6, transcendentals=0),
        name="pack_experts",
    )(up, down)


def to_column(line):
    return jnp.broadcast_to(line, (128, 256)).T[:, :1]


def to_line(column):
    return jnp.broadcast_to(column, (256, 128)).T[:1, :]


def expert_kernel(first, last, count, order_ref, x_ref, g_ref, b_ref, *refs):
    pieces, refs = refs[:count], refs[count:]
    if not first:
        (y_in, p_in), refs = refs[:2], refs[2:]
    (y_out, p_out, bias_ref), refs = refs[:3], refs[3:]
    acc_ref, w_ref, sem = refs[-3:]
    grads = refs[:-3]
    step = pl.program_id(0)
    model = w_ref.shape[1]

    @pl.when(step == 0)
    def _():
        if count == 1:
            pltpu.make_async_copy(pieces[0], w_ref, sem).start()
        else:
            part, units = pieces[0].shape[2:]
            end = order_ref[4] == 1

            def load(ref, slot):
                for p in range(8):
                    row = pl.multiple_of(slot * (2 * part) + (p // 4) * part, 32)
                    pltpu.make_async_copy(
                        ref.at[p],
                        w_ref.at[:, pl.ds(row, part), pl.ds((p % 4) * units, units)],
                        sem,
                    ).start()

            load(pieces[0], order_ref[0])
            for k in range(1, 4):
                pl.when(end)(functools.partial(load, pieces[k], order_ref[k]))
                pl.when(jnp.logical_not(end))(functools.partial(load, pieces[k + 3], order_ref[k]))
        acc_ref[...] = jnp.zeros_like(acc_ref)
        bias_ref[...] = jnp.zeros_like(bias_ref)
        pltpu.make_async_copy(w_ref, w_ref, sem).wait()

    sources, slots, _ = g_ref.shape
    x = x_ref[:, :slots].reshape(-1, model)
    g_raw = g_ref[...].reshape(-1, model)
    gates = []
    for k in range(sources):
        parts = x_ref[k, slots : slots + 16, :256].astype(F32)
        gates.append(to_column(parts[0:1] + parts[1:2])[:slots])
    gate = jnp.concatenate(gates, 0)
    g = (g_raw.astype(F32) * gate).astype(BF16)
    hidden = dot(x, w_ref[0]) + b_ref[...]
    cdf = 0.5 * (1.0 + lax.erf(hidden * (0.5 ** 0.5)))
    active = (hidden * cdf).astype(BF16)
    slope = cdf + hidden * (jnp.exp(-0.5 * hidden * hidden) * 0.3989422804014327)
    hidden_grad = (dot(g, w_ref[1]) * slope).astype(BF16)
    y = dot(active, w_ref[1], 1, 1)
    p = dot(hidden_grad, w_ref[0], 1, 1)
    if not first:
        y = y_in[...].reshape(-1, model) + y
        p = p_in[...].reshape(-1, model) + p
    if not last:
        y_out[...] = y.reshape(sources, slots, model)
        p_out[...] = p.reshape(sources, slots, model)
    else:
        y_out[...] = (y * gate).astype(BF16).reshape(sources, slots, model)
        p_out[:, :slots] = p.astype(BF16).reshape(sources, slots, model)
        gate_grad = jnp.sum(g_raw.astype(F32) * y, -1, keepdims=True)
        for k in range(sources):
            own = gate_grad[k * slots : (k + 1) * slots]
            line = to_line(jnp.concatenate([own, jnp.zeros((256 - slots, 1), F32)], 0))
            high = line.astype(BF16)
            low = (line - high.astype(F32)).astype(BF16)
            block = jnp.concatenate([high, low, jnp.zeros((14, 256), BF16)], 0)
            p_out[k, slots:] = jnp.concatenate([block, jnp.zeros((16, model - 256), BF16)], 1)
    bias_ref[...] += jnp.sum(hidden_grad.astype(F32), 0, keepdims=True)
    acc_ref[0] += dot(x, hidden_grad, 0, 0)
    acc_ref[1] += dot(g, active, 0, 0)

    @pl.when(step == pl.num_programs(0) - 1)
    def _():
        if len(grads) == 1:
            grads[0][...] = acc_ref[...]
        else:
            own_ref, rest_ref, near_ref = grads
            part, units = own_ref.shape[2:]
            for k in range(4):
                for q in range(8):
                    row = pl.multiple_of(order_ref[k] * (2 * part) + (q // 4) * part, 32)
                    columns = slice((q % 4) * units, (q % 4 + 1) * units)
                    block = acc_ref[:, pl.ds(row, part), columns].astype(BF16)
                    if k == 0:
                        own_ref[q] = block
                    else:
                        rest_ref[k - 1, q] = block
                    if k == 1:
                        near_ref[q] = block


def expert_chunk(order, x, g, b, sums, pieces, last):
    experts, slots, model = g.shape
    units = b.shape[1]
    first = sums is None
    step = 2
    block = lambda rows: pl.BlockSpec((step, rows, model), lambda i, o: (i, 0, 0))
    full = lambda shape: pl.BlockSpec(shape, lambda i, o: (0,) * len(shape))
    ins = [x, g, b] + list(pieces) + ([] if first else list(sums))
    in_specs = [block(x.shape[1]), block(slots), full(b.shape)]
    in_specs += [pl.BlockSpec(memory_space=pl.ANY)] * len(pieces)
    in_specs += [] if first else [block(slots)] * 2
    rows = (experts, slots, model)
    if last:
        outs = [(rows, BF16), (x.shape, BF16)]
    else:
        outs = [(rows, F32), (rows, F32)]
    out_specs = [block(s[1]) for s, _ in outs]
    outs.append((b.shape, F32))
    if len(pieces) == 1:
        outs.append(((2, model, units), F32))
    else:
        shape = pieces[0].shape
        outs += [(shape, BF16), ((3,) + shape, BF16), (shape, BF16)]
    out_specs += [full(s) for s, _ in outs[2:]]
    base = 4 + len(pieces)
    return pl.pallas_call(
        functools.partial(expert_kernel, first, last, len(pieces)),
        grid_spec=pltpu.PrefetchScalarGridSpec(
            num_scalar_prefetch=1,
            grid=(experts // step,),
            in_specs=in_specs,
            out_specs=out_specs,
            scratch_shapes=[
                pltpu.VMEM((2, model, units), F32),
                pltpu.VMEM((2, model, units), BF16),
                pltpu.SemaphoreType.DMA(()),
            ],
        ),
        out_shape=[jax.ShapeDtypeStruct(s, d) for s, d in outs],
        input_output_aliases={} if first or last else {base: 0, base + 1: 1},
        compiler_params=pltpu.CompilerParams(vmem_limit_bytes=58 * 2**20),
        cost_estimate=pl.CostEstimate(
            flops=12 * experts * slots * model * units, bytes_accessed=3 * 10**7,
            transcendentals=2 * experts * slots * units,
        ),
        name="expert_chunk",
    )(order, *ins)


CAP = 128
GROUP_IMG = 2
CHUNK = 128
HIGHEST = lax.Precision.HIGHEST
TENSOR = ("y", "c")
PLANE = ("x", "y", "c")
EVERY = ("y", "c", "z", "x")
INWARD = [(0, 1), (3, 2)]
MIDDLE = [(1, 2), (2, 1)]
OUTWARD = [(1, 0), (2, 3)]
ORDER = ((0, 1, 2, 3), (1, 0, 2, 3), (2, 3, 1, 0), (3, 2, 1, 0))


def tie(values, *events):
    events = [e for e in events if e is not None]
    if not events:
        return values
    return lax.optimization_barrier((values, *events))[0]


class Line:
    def __init__(self, own, length):
        self.own, self.length = own, length

    def start(self, *events):
        if self.length != 4:
            self.full = lax.all_gather(self.own, "z", axis=1, tiled=True)
            return
        own = tie(self.own, *events)
        self.inward = lax.ppermute(own, "z", INWARD)
        self.outward_one = lax.ppermute(own, "z", OUTWARD)
        self.middle_one = lax.ppermute(own, "z", MIDDLE)
        self.outward_two = lax.ppermute(own, "z", [(1, 3), (2, 0)])
        self.middle_two = lax.ppermute(self.inward, "z", MIDDLE)
        self.outward_three = lax.ppermute(self.middle_two, "z", OUTWARD)

    def early(self):
        if self.length != 4:
            return []
        return [self.inward, self.middle_one, self.outward_one]

    def result(self):
        if self.length != 4:
            return [self.full]
        return [
            self.own, self.outward_one, self.outward_two, self.outward_three,
            self.inward, self.middle_one, self.middle_two,
        ]


def add(*terms):
    return sum(term.astype(F32) for term in terms).astype(BF16)


class Reduce:
    def __init__(self, grads):
        self.grads = grads
        if len(grads) == 1:
            self.total = lax.psum_scatter(grads[0], "z", scatter_dimension=1, tiled=True)
            return
        own, rest, near = grads
        self.inward = lax.ppermute(rest, "z", INWARD)
        self.outward_one = lax.ppermute(near, "z", OUTWARD)
        self.two = add(rest[1], self.inward[1])
        self.three = add(rest[2], self.inward[2])

    def finish(self, *events):
        if len(self.grads) > 1:
            outward_two = lax.ppermute(tie(self.three, *events), "z", [(1, 3), (2, 0)])
            middle = lax.ppermute(tie(self.two, *events), "z", MIDDLE)
            self.total = add(
                self.grads[0], self.inward[0], self.outward_one, outward_two, middle
            )

    def early(self):
        return [self.three, self.two] if len(self.grads) > 1 else []


def gather_packs(pack):
    below = [pack] + [
        lax.ppermute(pack, "z", [(k, (k + far) % 4) for k in range(4)]) for far in (1, 2, 3)
    ]
    column = jnp.stack(below)
    swap = [(0, 1), (1, 0)]
    over_x = lax.ppermute(column, "x", swap)
    over_y = lax.ppermute(column, "y", swap)
    over_both = lax.ppermute(column, ("x", "y"), [(0, 3), (1, 2), (2, 1), (3, 0)])
    four = [column, over_x, over_y, over_both]
    return four + [lax.ppermute(each, "c", swap) for each in four]


def shards(
    tokens_in,
    key_mask,
    expert_ids,
    expert_slots,
    norm1_gain,
    norm1_shift,
    qkv_weight,
    qv_bias,
    out_weight,
    out_bias,
    norm2_gain,
    norm2_shift,
    router_weight,
    up_weight,
    up_bias,
    down_weight,
    down_bias,
    out_grad,
):
    length = lax.axis_size("z")
    core = lax.axis_index("c")
    chip_y = lax.axis_index("y")
    quarter = lax.axis_size("y") * 2
    expert = (lax.axis_index("x") * lax.axis_size("y") + chip_y) * 2 + core
    piece, sequence, model = tokens_in.shape
    experts, part, units = up_weight.shape
    dp = model // part
    width = qkv_weight.shape[2]
    tokens = piece * sequence
    blocks = units // CHUNK
    spans = [(0, 1), (1, 3), (3, 5), (5, 6)] if blocks == 6 else [(0, blocks)]

    smalls = jnp.concatenate(
        [
            norm1_gain[None],
            norm1_shift[None],
            qv_bias,
            out_bias[None],
            norm2_gain[None],
            norm2_shift[None],
            down_bias,
            router_weight.T,
            up_bias.reshape(experts * quarter, part),
        ],
        0,
    ).astype(BF16)
    small_rows = smalls.shape[0]
    pad = -(small_rows * part) % (16 * model)
    small_block = jnp.pad(smalls.reshape(-1), (0, pad)).reshape(-1, model)
    pack = jnp.concatenate(
        [
            jnp.concatenate(
                [qkv_weight[0], qkv_weight[1], qkv_weight[2], out_weight.T], 1
            ).astype(BF16),
            small_block,
        ],
        0,
    )
    place = [lax.axis_index(name) for name in ("z", "x", "y", "c")]
    if length == 4:
        packs = gather_packs(pack)
        by_x = jnp.stack([packs[0][:, part:], packs[1][:, part:]]).reshape(2, 4, -1)
        pick_x = (place[1] ^ jnp.arange(2))[:, None] == jnp.arange(2)
        pick_z = (place[0] - jnp.arange(4)[:, None]) % 4 == jnp.arange(4)
        pick = pick_z[:, None, None, :] & pick_x[None, :, :, None]
        vectors = dot(pick.reshape(8, 8).astype(BF16), by_x.reshape(8, -1)).astype(BF16)
    else:
        packs = lax.all_gather(pack, EVERY, axis=0, tiled=False)
        packs = packs.reshape(quarter, dp, pack.shape[0], model)
        vectors = packs[0, :, part:].reshape(dp, -1)
        packs = [packs[:, :, :part].reshape(quarter, model, model)]
    vectors = vectors[:, : small_rows * part].reshape(dp, small_rows, part).transpose(1, 0, 2)
    lines = vectors[: 7 + 2 * experts].reshape(-1, model).astype(F32)
    bias_pairs = lines[2:4].reshape(2, quarter, width).transpose(1, 0, 2)
    bias_down = lines[7 : 7 + experts]
    router = lines[7 + experts :].astype(BF16)
    bias_up = vectors[7 + 2 * experts :].reshape(experts, quarter, dp, part)
    bias_up = bias_up.transpose(0, 2, 1, 3).reshape(experts, quarter, units)
    bias_up = lax.dynamic_index_in_dim(bias_up, expert, 0, keepdims=False).astype(F32)

    head = spans[0][1] * CHUNK
    sizes = [head, units - head] if units > head else [head]
    packed = pack_experts(up_weight, down_weight, sizes)
    event = None
    parts = []
    for some in packed:
        some = lax.all_to_all(tie(some, event), PLANE, 0, 0, tiled=True)
        event = some
        starts = [CHUNK * f for f, _ in spans[1:]] if parts else [0]
        stops = [CHUNK * l for _, l in spans[1:]] if parts else [head]
        base = starts[0]
        parts += [some[..., f - base : l - base] for f, l in zip(starts, stops)]
    if length != 4:
        parts = [
            one.reshape(2, quarter, 2, part, -1).transpose(2, 0, 3, 1, 4).reshape(2, 2 * part, -1)
            for one in parts
        ]

    first_group = chip_y * 3
    group_tokens = GROUP_IMG * sequence
    position = (expert_ids * CAP + expert_slots).reshape(-1, group_tokens, 2)
    position_full = lax.dynamic_index_in_dim(position, first_group + 2 * core, 0, keepdims=False)
    position_half = lax.dynamic_index_in_dim(position, first_group + 1, 0, keepdims=False)
    slots_full = jnp.arange(experts * CAP, dtype=jnp.int32)
    half = CAP // 2
    slots_half = (
        jnp.arange(experts, dtype=jnp.int32)[:, None] * CAP
        + core * half
        + jnp.arange(half, dtype=jnp.int32)
    ).reshape(-1)
    match_full = slots_full[:, None, None] == position_full.T[None]
    match_half = slots_half[:, None, None] == position_half.T[None]
    hot_full = (match_full[:, 0] | match_full[:, 1]).astype(BF16)
    hot_half = (match_half[:, 0] | match_half[:, 1]).astype(BF16)
    swap = [(0, 1), (1, 0)]

    def both_groups(values):
        lent = jnp.where(core == 0, values[2], values[0])
        other = lax.ppermute(lent, "c", swap)
        full = jnp.where(core == 0, values[:2], values[1:])
        shared = jnp.where(core == 0, jnp.stack([lent, other]), jnp.stack([other, lent]))
        return (
            full.reshape(group_tokens, -1),
            shared.reshape(group_tokens, -1),
        )

    def join_rows(full, shared):
        full = full.reshape((experts, CAP) + full.shape[1:])
        shared = shared.reshape((experts, half) + shared.shape[1:])
        return jnp.concatenate([full, shared], 1)

    def lines_of(values):
        high = values.astype(BF16)
        low = (values - high.astype(F32)).astype(BF16)
        both = jnp.stack([high, low], 1)
        return jnp.pad(both, ((0, 0), (0, 14), (0, model - both.shape[2])))

    def values_of(rows):
        both = rows[:, CAP + half : CAP + half + 2, : CAP + half].astype(F32)
        return both[:, 0] + both[:, 1]

    def swap_experts(rows, *events):
        return lax.all_to_all(tie(rows, *events), PLANE, 0, 0, tiled=True)

    def dispatch(full, shared):
        return join_rows(dot(hot_full, full).astype(BF16), dot(hot_half, shared).astype(BF16))

    def combine(back):
        full = dot(hot_full, back[:, :CAP].reshape(-1, model), 0, 0)
        shared = dot(hot_half, back[:, CAP : CAP + half].reshape(-1, model), 0, 0)
        full = full.reshape(GROUP_IMG, sequence, model)
        shared = shared.reshape(GROUP_IMG, sequence, model)
        mine = jnp.where(core == 0, shared[0], shared[1])
        theirs = jnp.where(core == 0, shared[1], shared[0])
        mine = mine + lax.ppermute(theirs, "c", swap)
        return jnp.where(
            core == 0,
            jnp.concatenate([full, mine[None]]),
            jnp.concatenate([mine[None], full]),
        )

    lines_z = [Line(own, length) for own in parts]
    for k in range(2):
        if k < len(lines_z):
            lines_z[k].start(*(lines_z[k - 1].early() if k else []))
    grad_full, grad_shared = both_groups(out_grad)
    incoming = swap_experts(dispatch(grad_full, grad_shared), event)

    local_start = (chip_y * 2 + core) * piece
    mask_here = lax.dynamic_slice_in_dim(key_mask, local_start, piece, 0)[:, None]
    before = [event] + lines_z[0].early() + (lines_z[1].early() if len(lines_z) > 1 else [])
    n1, n2, residual, q, k, v, attended, lse, wq, wk, wv, wo = attend_forward(
        jnp.stack(place).astype(jnp.int32), tie(tokens_in, *before), mask_here, lines, bias_pairs,
        packs, width,
    )
    for line in lines_z[2:]:
        line.start(n2)
    normed_two = n2.reshape(tokens, model)

    normed_full, normed_shared = both_groups(n2)

    def chances_of(rows):
        return jax.nn.softmax(dot(rows, router, 1, 1), -1)

    probabilities = chances_of(normed_two)
    hot_ids = expert_ids[..., None] == jnp.arange(experts, dtype=jnp.int32)
    hot_here = lax.dynamic_slice_in_dim(hot_ids, local_start, piece, 0).astype(F32)
    hot_here = jnp.sum(hot_here.reshape(tokens, 2, experts), 1)
    share_here = hot_here * probabilities

    def slot_gates(match, rows, position_here):
        chance = chances_of(rows)
        hot = (position_here // CAP)[..., None] == jnp.arange(experts, dtype=jnp.int32)
        gates = jnp.sum(hot.astype(F32) * chance[:, None], -1)
        return jnp.sum(jnp.where(match, gates.T[None], 0.0), (1, 2))

    gates_sent = join_rows(
        slot_gates(match_full, normed_full, position_full),
        slot_gates(match_half, normed_shared, position_half),
    )
    chosen = swap_experts(
        jnp.concatenate([dispatch(normed_full, normed_shared), lines_of(gates_sent)], 1), incoming
    )

    order = jnp.asarray(
        [ORDER[k] + (int(k in (0, 3)),) for k in range(4)] if length == 4 else [[0] * 5] * length,
        jnp.int32,
    )
    order = lax.dynamic_index_in_dim(order, place[0], 0, keepdims=False)
    sums = None
    bias_parts = []
    reduced = []
    for index, (first, last) in enumerate(spans):
        both = lines_z[index].result()
        events = []
        if index >= 2:
            events += reduced[index - 2].early()
        if index == 1:
            for line in lines_z[2:]:
                events += line.early()
        bias_one = bias_up[:, first * CHUNK : last * CHUNK].reshape(1, -1)
        final = index == len(spans) - 1
        *sums, bias_part = (
            outs := expert_chunk(order, chosen, incoming, tie(bias_one, *events), sums, both, final)
        )[:3]
        bias_parts.append(bias_part.reshape(quarter, -1))
        reduced.append(Reduce(outs[3:]))
        if index >= 2:
            reduced[index - 2].finish()

    mixed, pulled = sums
    back = swap_experts(pulled)
    gate_back = values_of(back)
    norm_two_grad = combine(back)

    def slots_to_tokens(match, parts_here):
        parts_here = parts_here.reshape(experts, -1)
        match = (match[:, 0] | match[:, 1]).reshape(experts, -1, group_tokens)
        return jnp.sum(jnp.where(match, parts_here[..., None], 0.0), 1).T

    prob_full = slots_to_tokens(match_full, gate_back[:, :CAP])
    prob_shared = slots_to_tokens(match_half, gate_back[:, CAP:])
    prob_full = prob_full.reshape(GROUP_IMG, sequence, experts)
    prob_shared = prob_shared.reshape(GROUP_IMG, sequence, experts)
    mine = jnp.where(core == 0, prob_shared[0], prob_shared[1])
    theirs = jnp.where(core == 0, prob_shared[1], prob_shared[0])
    mine = mine + lax.ppermute(theirs, "c", swap)
    chance_grad = jnp.where(
        core == 0,
        jnp.concatenate([prob_full, mine[None]]),
        jnp.concatenate([mine[None], prob_full]),
    ).reshape(tokens, experts)
    grad_rows = out_grad.reshape(tokens, model)
    bias_dot = dot(grad_rows, bias_down.astype(BF16), 1, 1)
    chance_grad = chance_grad + hot_here * bias_dot
    logit_grad = probabilities * (
        chance_grad - jnp.sum(probabilities * chance_grad, -1, keepdims=True)
    )
    logit_grad = logit_grad.astype(BF16)
    router_grad = dot(logit_grad, normed_two, 0, 0)
    down_bias_grad = lax.dot_general(
        share_here, grad_rows.astype(F32), (((0,), (0,)), ((), ())), precision=HIGHEST
    )

    norm_two_grad = norm_two_grad + dot(logit_grad, router).reshape(norm_two_grad.shape)
    h_grad, hb, dq, dk, dv, line_sums, pair_sums = attend_backward(
        norm_two_grad, out_grad, residual, mask_here, wo, lines, q, k, v, lse
    )
    input_grad, line_ones = input_backward(h_grad, tokens_in, wq, wk, wv, lines, dq, dk, dv)
    for some in reduced[-2:] if len(reduced) > 1 else reduced:
        some.finish()

    bias_rows = jnp.concatenate(bias_parts, 1).reshape(dp, quarter, part)
    bias_rows = jnp.where(
        jnp.arange(experts)[:, None, None, None] == expert, bias_rows[None], 0.0
    )
    bias_rows = bias_rows.transpose(0, 2, 1, 3).reshape(experts * quarter, dp, part)
    line_grads = jnp.concatenate(
        [
            line_ones[:2],
            pair_sums[:, 0].reshape(1, model),
            pair_sums[:, 1].reshape(1, model),
            line_sums[:3],
            down_bias_grad,
            router_grad,
        ],
        0,
    ).reshape(-1, dp, part)
    sum_type = BF16 if length == 4 else F32
    vector_grads = jnp.concatenate([line_grads, bias_rows], 0).astype(sum_type)
    vector_grads = vector_grads.transpose(1, 0, 2).reshape(dp, small_rows * part)
    vector_grads = jnp.pad(vector_grads, ((0, 0), (0, pad))).reshape(dp, -1, model)

    if length == 4:
        pack_grads = attend_weights(n1, hb, dq, dk, dv, attended, vector_grads)
    else:
        pack_grads = attend_weights(n1, hb, dq, dk, dv, attended, None)
        pack_grads = pack_grads.reshape(quarter, dp, part, model)
        vector_grads = jnp.broadcast_to(vector_grads[None], (quarter,) + vector_grads.shape)
        pack_grads = jnp.concatenate([pack_grads, vector_grads], 2)
        pack_grads = pack_grads.reshape(quarter // 2, 2, dp // 2, 2, -1, model)
        pack_grads = pack_grads.transpose(1, 3, 0, 2, 4, 5)
    mine = lax.dynamic_index_in_dim(pack_grads, core, 0, keepdims=False)
    theirs = lax.dynamic_index_in_dim(pack_grads, 1 - core, 0, keepdims=False)
    theirs = lax.ppermute(theirs, "c", swap)
    pack_grads = (mine.astype(F32) + theirs.astype(F32)).astype(sum_type)
    pack_grads = pack_grads.reshape((-1,) + pack_grads.shape[2:])
    pack_grads = lax.all_to_all(pack_grads, ("x", "y"), 0, 0, tiled=True)
    pack_grads = jnp.sum(pack_grads.astype(F32), 0).astype(sum_type)
    if length == 4:
        pack_grads = lax.all_to_all(pack_grads, "z", 0, 0, tiled=True)
        pack_grad = jnp.sum(pack_grads.astype(F32), 0)
    else:
        pack_grad = lax.psum_scatter(pack_grads, "z", scatter_dimension=0, tiled=False)
    qkv_out = pack_grad[:part, : 3 * width].reshape(part, 3, width).transpose(1, 0, 2)
    out_weight_grad = pack_grad[:part, 3 * width :].T
    small_grads = pack_grad[part:].reshape(-1)[: small_rows * part].reshape(small_rows, part)

    mixture = combine(swap_experts(mixed, back))
    bias_term = jnp.dot(share_here, bias_down, precision=HIGHEST).reshape(residual.shape)
    output = (residual + mixture + bias_term).astype(BF16)

    ups, downs = [], []
    totals = [one.total for one in reduced]
    if length != 4:
        totals = [
            one.reshape(2, 2, part, quarter, -1).transpose(1, 3, 0, 2, 4).reshape(experts, 2, part, -1)
            for one in totals
        ]
    for some in (totals[:2], totals[2:]):
        if some:
            some = some[0] if len(some) == 1 else jnp.concatenate(some, -1)
            some = lax.all_to_all(some.astype(BF16), PLANE, 0, 0, tiled=True).astype(F32)
            ups.append(some[:, 0])
            downs.append(some[:, 1])
    up_grad = jnp.concatenate(ups, -1)
    down_grad = jnp.concatenate(downs, -1).transpose(0, 2, 1)
    return (
        output,
        input_grad,
        small_grads[0],
        small_grads[1],
        qkv_out,
        small_grads[2:4],
        out_weight_grad,
        small_grads[4],
        small_grads[5],
        small_grads[6],
        small_grads[7 + experts : 7 + 2 * experts].T,
        up_grad,
        small_grads[7 + 2 * experts :].reshape(experts, -1),
        down_grad,
        small_grads[7 : 7 + experts],
    )


def solution(mesh):
    dp, tensor = mesh.devices.shape
    planes = jax.sharding.Mesh(
        mesh.devices.reshape(dp // 2, 2, tensor // 2, 2), ("z", "x", "y", "c")
    )
    rows = ("z", "x")
    images = P(("z", "x", "y", "c"), None, None)
    return jax.shard_map(
        shards,
        mesh=planes,
        in_specs=(
            images,
            P(rows, None),
            P(rows, None, None),
            P(rows, None, None),
            P(rows),
            P(rows),
            P(None, rows, TENSOR),
            P(None, rows),
            P(TENSOR, rows),
            P(rows),
            P(rows),
            P(rows),
            P(rows, None),
            P(None, rows, TENSOR),
            P(None, rows),
            P(None, TENSOR, rows),
            P(None, rows),
            images,
        ),
        out_specs=(
            images,
            images,
            P(rows),
            P(rows),
            P(None, rows, TENSOR),
            P(None, rows),
            P(TENSOR, rows),
            P(rows),
            P(rows),
            P(rows),
            P(rows, None),
            P(None, rows, TENSOR),
            P(None, rows),
            P(None, TENSOR, rows),
            P(None, rows),
        ),
        check_vma=False,
    )
```

```python
import functools
import jax
import jax.numpy as jnp
from jax import lax
from jax.experimental import pallas as pl
from jax.experimental.pallas import tpu as pltpu
from jax.sharding import PartitionSpec as P

HD = 64
EPSILON = 1e-06
NEGATIVE = -1e30
F32 = jnp.float32
BF16 = jnp.bfloat16


def dot(left, right, left_dim=1, right_dim=0):
    return lax.dot_general(
        left, right, (((left_dim,), (right_dim,)), ((), ())), preferred_element_type=F32
    )


def norm_forward(values, gains, shifts):
    middle = jnp.mean(values, -1, keepdims=True)
    centred = values - middle
    inverse = lax.rsqrt(jnp.mean(centred * centred, -1, keepdims=True) + EPSILON)
    unit_rows = centred * inverse
    return (unit_rows * gains + shifts, unit_rows, inverse)


def norm_backward(grad_rows, unit_rows, inverse, gains):
    scaled = grad_rows * gains
    return inverse * (
        scaled
        - jnp.mean(scaled, -1, keepdims=True)
        - unit_rows * jnp.mean(scaled * unit_rows, -1, keepdims=True)
    )


def head_masks(width):
    lane = lax.broadcasted_iota(jnp.int32, (1, width), 1)
    return [(lane // HD == k) for k in range(width // HD)]


def arrange(w_ref, *parts):
    width = parts[0].shape[2]
    for t in range(w_ref.shape[0]):
        packed = w_ref[t]
        for k, ref in enumerate(parts):
            ref[t] = packed[:, k * width : (k + 1) * width]


def put_rows(ref, values):
    rows, columns = values.shape
    spare = jnp.zeros((ref.shape[0] - rows, columns), values.dtype)
    ref[...] = jnp.concatenate([values, spare], 0).astype(ref.dtype)


def attend_forward_kernel(
    place_ref, tokens_ref, mask_ref, lines_ref, bias_ref, *refs,
):
    (
        n1_ref, n2_ref, h_ref, q_ref, k_ref, v_ref, o_ref, lse_ref,
        wq_ref, wk_ref, wv_ref, wo_ref, all_ref, sem,
    ) = refs[-14:]
    packs = refs[:-14]

    @pl.when(pl.program_id(0) == 0)
    def _():
        if len(packs) == 1:
            pltpu.make_async_copy(packs[0], all_ref, sem).start()
        else:
            z, x, y, c = [place_ref[k] for k in range(4)]
            part = all_ref.shape[1] // 8
            for index, ref in enumerate(packs):
                dx, dy, dc = index & 1, (index >> 1) & 1, index >> 2
                t = (y ^ dy) * 2 + (c ^ dc)
                for back in range(4):
                    row = (((z - back) & 3) * 2 + (x ^ dx)) * part
                    pltpu.make_async_copy(
                        ref.at[back, pl.ds(0, part)],
                        all_ref.at[t, pl.ds(pl.multiple_of(row, 32), part)],
                        sem,
                    ).start()
        pltpu.make_async_copy(all_ref, all_ref, sem).wait()
        arrange(all_ref, wq_ref, wk_ref, wv_ref, wo_ref)

    x = tokens_ref[0].astype(F32)
    n1, _, _ = norm_forward(x, lines_ref[0:1, :], lines_ref[1:2, :])
    put_rows(n1_ref.at[0], n1)
    n1 = n1.astype(BF16)
    width = wq_ref.shape[2]
    masks = head_masks(width)
    keys = mask_ref[0] > 0
    total = x + lines_ref[4:5, :]
    for t in range(wq_ref.shape[0]):
        q = (dot(n1, wq_ref[t]) + bias_ref[t, 0:1, :]).astype(BF16)
        k = dot(n1, wk_ref[t]).astype(BF16)
        v = (dot(n1, wv_ref[t]) + bias_ref[t, 1:2, :]).astype(BF16)
        q_ref[0, t] = q
        k_ref[0, t] = k
        v_ref[0, t] = v
        scaled = q * jnp.asarray(HD ** (-0.5), BF16)
        o = jnp.zeros(q.shape, F32)
        for h, here in enumerate(masks):
            s = dot(jnp.where(here, scaled, jnp.zeros_like(scaled)), k, 1, 1)
            s = jnp.where(keys, s, NEGATIVE)
            largest = jnp.max(s, -1, keepdims=True)
            e = jnp.exp(s - largest)
            total_e = jnp.sum(e, -1, keepdims=True)
            p = (e / total_e).astype(BF16)
            o = jnp.where(here, dot(p, v), o)
            index = t * len(masks) + h
            lse_ref[0, :, index : index + 1] = largest + jnp.log(total_e)
        put_rows(o_ref.at[0, t], o)
        total = total + dot(o.astype(BF16), wo_ref[t], 1, 1)
    h_ref[0] = total
    n2, _, _ = norm_forward(total, lines_ref[5:6, :], lines_ref[6:7, :])
    n2_ref[0] = n2.astype(BF16)


def whole(shape):
    return pl.BlockSpec(shape, lambda b: (0,) * len(shape))


def by_image(shape):
    return pl.BlockSpec((1,) + shape[1:], lambda b: (b,) + (0,) * (len(shape) - 1))


def padded(rows):
    return -(-rows // 16) * 16


def attend_forward(place, tokens_in, mask, lines, bias_pairs, packs, width):
    images, sequence, model = tokens_in.shape
    quarter = model // width
    rows = (images, sequence, model)
    heads = (images, quarter, sequence, width)
    columns = (quarter, model, width)
    outs = [
        ((images, padded(sequence), model), BF16), (rows, BF16), (rows, F32), (heads, BF16), (heads, BF16),
        (heads, BF16), ((images, quarter, padded(sequence), width), BF16), ((images, sequence, 128), F32),
        (columns, BF16), (columns, BF16), (columns, BF16), (columns, BF16),
    ]
    place_spec = lambda spec: pl.BlockSpec(spec.block_shape, lambda b, p: spec.index_map(b))
    in_specs = [by_image(tokens_in.shape), by_image(mask.shape), whole(lines.shape), whole(bias_pairs.shape)]
    out_specs = [by_image(s) for s, _ in outs[:8]] + [whole(s) for s, _ in outs[8:]]
    return pl.pallas_call(
        attend_forward_kernel,
        grid_spec=pltpu.PrefetchScalarGridSpec(
            num_scalar_prefetch=1,
            grid=(images,),
            in_specs=[place_spec(s) for s in in_specs]
            + [pl.BlockSpec(memory_space=pl.ANY)] * len(packs),
            out_specs=[place_spec(s) for s in out_specs],
            scratch_shapes=[pltpu.VMEM((quarter, model, 4 * width), BF16), pltpu.SemaphoreType.DMA(())],
        ),
        out_shape=[jax.ShapeDtypeStruct(s, d) for s, d in outs],
        compiler_params=pltpu.CompilerParams(vmem_limit_bytes=56 * 2**20),
        cost_estimate=pl.CostEstimate(flops=2 * 10**9, bytes_accessed=4 * 10**6, transcendentals=0),
        name="attend_forward",
    )(place, tokens_in, mask, lines, bias_pairs, *packs)


def attend_backward_kernel(
    n2_grad_ref, grad_ref, h_ref, mask_ref, wo_ref, lines_ref, q_ref, k_ref, v_ref, lse_ref,
    h_grad_ref, hb_ref, dq_ref, dk_ref, dv_ref, vec_ref, pair_ref,
):
    @pl.when(pl.program_id(0) == 0)
    def _():
        vec_ref[...] = jnp.zeros_like(vec_ref)
        pair_ref[...] = jnp.zeros_like(pair_ref)

    n2_grad = n2_grad_ref[0]
    _, unit_two, inverse_two = norm_forward(h_ref[0], lines_ref[5:6, :], lines_ref[6:7, :])
    vec_ref[1:2, :] += jnp.sum(n2_grad * unit_two, 0, keepdims=True)
    vec_ref[2:3, :] += jnp.sum(n2_grad, 0, keepdims=True)
    h_grad = grad_ref[0].astype(F32) + norm_backward(
        n2_grad, unit_two, inverse_two, lines_ref[5:6, :]
    )
    vec_ref[0:1, :] += jnp.sum(h_grad, 0, keepdims=True)
    h_grad_ref[0] = h_grad
    put_rows(hb_ref.at[0], h_grad)
    hb = h_grad.astype(BF16)
    width = wo_ref.shape[2]
    masks = head_masks(width)
    keys = mask_ref[0] > 0
    scale = HD ** (-0.5)
    for t in range(wo_ref.shape[0]):
        do = dot(hb, wo_ref[t]).astype(BF16)
        q, k, v = q_ref[0, t], k_ref[0, t], v_ref[0, t]
        zero = jnp.zeros_like(q)
        scaled = q * jnp.asarray(scale, BF16)
        dq = jnp.zeros(q.shape, F32)
        dk = jnp.zeros(q.shape, F32)
        dv = jnp.zeros(q.shape, F32)
        for h, here in enumerate(masks):
            index = t * len(masks) + h
            s = dot(jnp.where(here, scaled, zero), k, 1, 1)
            s = jnp.where(keys, s, NEGATIVE)
            p = jnp.exp(s - lse_ref[0, :, index : index + 1])
            dp = dot(jnp.where(here, do, zero), v, 1, 1)
            ds = p * (dp - jnp.sum(p * dp, -1, keepdims=True))
            ds = ds.astype(BF16)
            dv = jnp.where(here, dot(p.astype(BF16), do, 0, 0), dv)
            dq = jnp.where(here, dot(ds, k), dq)
            dk = jnp.where(here, dot(ds, q, 0, 0), dk)
        dq = (dq * scale).astype(BF16).astype(F32)
        dv = dv.astype(BF16).astype(F32)
        pair_ref[t, 0:1, :] += jnp.sum(dq, 0, keepdims=True)
        pair_ref[t, 1:2, :] += jnp.sum(dv, 0, keepdims=True)
        put_rows(dq_ref.at[0, t], dq)
        put_rows(dk_ref.at[0, t], dk * scale)
        put_rows(dv_ref.at[0, t], dv)


def attend_backward(n2_grad, out_grad, h, mask, wo, lines, q, k, v, lse):
    ins = (n2_grad, out_grad, h, mask, wo, lines, q, k, v, lse)
    shared = {4, 5}
    images, sequence, model = n2_grad.shape
    quarter, _, width = wo.shape
    heads = ((images, quarter, padded(sequence), width), BF16)
    outs = [
        (n2_grad.shape, F32), ((images, padded(sequence), model), BF16), heads, heads, heads,
        ((8, model), F32), ((quarter, 8, width), F32),
    ]
    return pl.pallas_call(
        attend_backward_kernel,
        grid=(images,),
        in_specs=[whole(a.shape) if i in shared else by_image(a.shape) for i, a in enumerate(ins)],
        out_specs=[by_image(s) for s, _ in outs[:5]] + [whole(s) for s, _ in outs[5:]],
        out_shape=[jax.ShapeDtypeStruct(s, d) for s, d in outs],
        compiler_params=pltpu.CompilerParams(vmem_limit_bytes=56 * 2**20),
        cost_estimate=pl.CostEstimate(flops=0, bytes_accessed=0, transcendentals=0),
        name="attend_backward",
    )(*ins)


def attend_weights_kernel(n1_ref, hb_ref, dq_ref, dk_ref, dv_ref, o_ref, *refs):
    out_ref = refs[-1]
    width = dq_ref.shape[3]
    n1 = n1_ref[...].reshape(-1, n1_ref.shape[2])
    hb = hb_ref[...].reshape(-1, n1_ref.shape[2])
    for k, (left, ref) in enumerate(((n1, dq_ref), (n1, dk_ref), (n1, dv_ref), (hb, o_ref))):
        sums = dot(left, ref[...].reshape(-1, width), 0, 0).astype(out_ref.dtype)
        columns = slice(k * width, (k + 1) * width)
        if len(refs) == 1:
            out_ref[0, :, columns] = sums
            continue
        part = sums.shape[0] // 8
        for z in range(4):
            for x in range(2):
                start = (z * 2 + x) * part
                out_ref[0, x, 0, z, :part, columns] = sums[start : start + part]
    if len(refs) == 2:
        for z in range(4):
            for x in range(2):
                out_ref[0, x, 0, z, part:, :] = refs[0][z * 2 + x]


def attend_weights(n1, hb, dq, dk, dv, o, extra):
    images, quarter, rows, width = dq.shape
    model = n1.shape[2]
    heads = pl.BlockSpec((images, 1, rows, width), lambda t: (0, t, 0, 0))
    if extra is None:
        out_spec = pl.BlockSpec((1, model, 4 * width), lambda t: (t, 0, 0))
        out_shape = jax.ShapeDtypeStruct((quarter, model, 4 * width), F32)
    else:
        depth = model // 8 + extra.shape[1]
        out_spec = pl.BlockSpec(
            (1, 2, 1, 4, depth, model), lambda t: (t % 2, 0, t // 2, 0, 0, 0)
        )
        out_shape = jax.ShapeDtypeStruct((2, 2, 2, 4, depth, model), BF16)
    extras = [] if extra is None else [extra]
    return pl.pallas_call(
        attend_weights_kernel,
        grid=(quarter,),
        in_specs=[whole(n1.shape), whole(hb.shape)] + [heads] * 4 + [whole(e.shape) for e in extras],
        out_specs=out_spec,
        out_shape=out_shape,
        compiler_params=pltpu.CompilerParams(vmem_limit_bytes=56 * 2**20),
        cost_estimate=pl.CostEstimate(flops=0, bytes_accessed=0, transcendentals=0),
        name="attend_weights",
    )(n1, hb, dq, dk, dv, o, *extras)


def input_backward_kernel(
    h_grad_ref, tokens_ref, wq_ref, wk_ref, wv_ref, lines_ref, dq_ref, dk_ref, dv_ref,
    input_grad_ref, vec_ref,
):
    @pl.when(pl.program_id(0) == 0)
    def _():
        vec_ref[...] = jnp.zeros_like(vec_ref)

    rows = tokens_ref.shape[1]
    n1_grad = jnp.zeros((dq_ref.shape[2], tokens_ref.shape[2]), F32)
    for t in range(wq_ref.shape[0]):
        for grads, weights in ((dq_ref, wq_ref), (dk_ref, wk_ref), (dv_ref, wv_ref)):
            n1_grad += dot(grads[0, t], weights[t], 1, 1)
    n1_grad = n1_grad[:rows]
    _, unit_one, inverse_one = norm_forward(
        tokens_ref[0].astype(F32), lines_ref[0:1, :], lines_ref[1:2, :]
    )
    vec_ref[0:1, :] += jnp.sum(n1_grad * unit_one, 0, keepdims=True)
    vec_ref[1:2, :] += jnp.sum(n1_grad, 0, keepdims=True)
    input_grad_ref[0] = h_grad_ref[0] + norm_backward(
        n1_grad, unit_one, inverse_one, lines_ref[0:1, :]
    )


def input_backward(h_grad, tokens_in, wq, wk, wv, lines, dq, dk, dv):
    ins = (h_grad, tokens_in, wq, wk, wv, lines, dq, dk, dv)
    outs = [(h_grad.shape, F32), ((8, wq.shape[1]), F32)]
    return pl.pallas_call(
        input_backward_kernel,
        grid=(h_grad.shape[0],),
        in_specs=[whole(a.shape) if 2 <= i <= 5 else by_image(a.shape) for i, a in enumerate(ins)],
        out_specs=[by_image(outs[0][0]), whole(outs[1][0])],
        out_shape=[jax.ShapeDtypeStruct(s, d) for s, d in outs],
        compiler_params=pltpu.CompilerParams(vmem_limit_bytes=56 * 2**20),
        cost_estimate=pl.CostEstimate(flops=0, bytes_accessed=0, transcendentals=0),
        name="input_backward",
    )(*ins)


def pack_experts_kernel(up_ref, down_ref, *refs):
    up = up_ref[0].astype(BF16)
    down = down_ref[0].T.astype(BF16)
    start = 0
    for ref in refs:
        stop = start + ref.shape[3]
        ref[0, 0] = up[:, start:stop]
        ref[0, 1] = down[:, start:stop]
        start = stop


def pack_experts(up, down, sizes):
    experts, part, units = up.shape
    outs = [(experts, 2, part, size) for size in sizes]
    return pl.pallas_call(
        pack_experts_kernel,
        grid=(experts,),
        in_specs=[by_image(up.shape), by_image(down.shape)],
        out_specs=[by_image(s) for s in outs],
        out_shape=[jax.ShapeDtypeStruct(s, BF16) for s in outs],
        compiler_params=pltpu.CompilerParams(vmem_limit_bytes=32 * 2**20),
        cost_estimate=pl.CostEstimate(flops=0, bytes_accessed=8 * 10**6, transcendentals=0),
        name="pack_experts",
    )(up, down)


def to_column(line):
    return jnp.broadcast_to(line, (128, 256)).T[:, :1]


def to_line(column):
    return jnp.broadcast_to(column, (256, 128)).T[:1, :]


def expert_kernel(first, last, order_ref, x_ref, g_ref, b_ref, shards_ref, *refs):
    if not first:
        (y_in, p_in), refs = refs[:2], refs[2:]
    (y_out, p_out, bias_ref), refs = refs[:3], refs[3:]
    acc_ref, w_ref, sem = refs[-3:]
    grads = refs[:-3]
    step = pl.program_id(0)
    model = w_ref.shape[1]

    @pl.when(step == 0)
    def _():
        if len(shards_ref.shape) == 3:
            pltpu.make_async_copy(shards_ref, w_ref, sem).start()
        else:
            part, units = shards_ref.shape[3:]
            for z in range(4):
                for p in range(8):
                    row = (z * 2 + p // 4) * part
                    pltpu.make_async_copy(
                        shards_ref.at[z, p],
                        w_ref.at[:, pl.ds(row, part), pl.ds((p % 4) * units, units)],
                        sem,
                    ).start()
        acc_ref[...] = jnp.zeros_like(acc_ref)
        bias_ref[...] = jnp.zeros_like(bias_ref)
        pltpu.make_async_copy(w_ref, w_ref, sem).wait()

    sources, slots, _ = g_ref.shape
    x = x_ref[:, :slots].reshape(-1, model)
    g_raw = g_ref[...].reshape(-1, model)
    gates = []
    for k in range(sources):
        parts = x_ref[k, slots : slots + 16, :256].astype(F32)
        gates.append(to_column(parts[0:1] + parts[1:2])[:slots])
    gate = jnp.concatenate(gates, 0)
    g = (g_raw.astype(F32) * gate).astype(BF16)
    hidden = dot(x, w_ref[0]) + b_ref[...]
    cdf = 0.5 * (1.0 + lax.erf(hidden * (0.5 ** 0.5)))
    active = (hidden * cdf).astype(BF16)
    slope = cdf + hidden * (jnp.exp(-0.5 * hidden * hidden) * 0.3989422804014327)
    hidden_grad = (dot(g, w_ref[1]) * slope).astype(BF16)
    y = dot(active, w_ref[1], 1, 1)
    p = dot(hidden_grad, w_ref[0], 1, 1)
    if not first:
        y = y_in[...].reshape(-1, model) + y
        p = p_in[...].reshape(-1, model) + p
    if not last:
        y_out[...] = y.reshape(sources, slots, model)
        p_out[...] = p.reshape(sources, slots, model)
    else:
        y_out[...] = (y * gate).astype(BF16).reshape(sources, slots, model)
        p_out[:, :slots] = p.astype(BF16).reshape(sources, slots, model)
        gate_grad = jnp.sum(g_raw.astype(F32) * y, -1, keepdims=True)
        for k in range(sources):
            own = gate_grad[k * slots : (k + 1) * slots]
            line = to_line(jnp.concatenate([own, jnp.zeros((256 - slots, 1), F32)], 0))
            high = line.astype(BF16)
            low = (line - high.astype(F32)).astype(BF16)
            block = jnp.concatenate([high, low, jnp.zeros((14, 256), BF16)], 0)
            p_out[k, slots:] = jnp.concatenate([block, jnp.zeros((16, model - 256), BF16)], 1)
    bias_ref[...] += jnp.sum(hidden_grad.astype(F32), 0, keepdims=True)
    acc_ref[0] += dot(x, hidden_grad, 0, 0)
    acc_ref[1] += dot(g, active, 0, 0)

    @pl.when(step == pl.num_programs(0) - 1)
    def _():
        if len(grads) == 1:
            grads[0][...] = acc_ref[...]
        else:
            own_ref, near_ref, rest_ref = grads[:3]
            part, units = own_ref.shape[2:]
            for k in range(4):
                for q in range(8):
                    row = pl.multiple_of(order_ref[k] * (2 * part) + (q // 4) * part, 32)
                    columns = slice((q % 4) * units, (q % 4 + 1) * units)
                    block = acc_ref[:, pl.ds(row, part), columns].astype(BF16)
                    if k == 0:
                        own_ref[q] = block
                    elif k == 3 and len(grads) == 4:
                        grads[3][q] = block
                    else:
                        rest_ref[k - 1, q] = block
                    if k == 1:
                        near_ref[q] = block


def expert_chunk(order, x, g, b, sums, shards, last):
    experts, slots, model = g.shape
    units = b.shape[1]
    first = sums is None
    step = 2
    block = lambda rows: pl.BlockSpec((step, rows, model), lambda i, o: (i, 0, 0))
    full = lambda shape: pl.BlockSpec(shape, lambda i, o: (0,) * len(shape))
    ins = [x, g, b, shards] + ([] if first else list(sums))
    in_specs = [block(x.shape[1]), block(slots), full(b.shape)]
    in_specs.append(pl.BlockSpec(memory_space=pl.ANY))
    in_specs += [] if first else [block(slots)] * 2
    rows = (experts, slots, model)
    if last:
        outs = [(rows, BF16), (x.shape, BF16)]
    else:
        outs = [(rows, F32), (rows, F32)]
    out_specs = [block(s[1]) for s, _ in outs]
    outs.append((b.shape, F32))
    if len(shards.shape) == 3:
        outs.append(((2, model, units), F32))
    else:
        shape = shards.shape[1:]
        outs += [(shape, BF16), (shape, BF16)]
        outs += [((2,) + shape, BF16), (shape, BF16)] if first else [((3,) + shape, BF16)]
    out_specs += [full(s) for s, _ in outs[2:]]
    base = 5
    return pl.pallas_call(
        functools.partial(expert_kernel, first, last),
        grid_spec=pltpu.PrefetchScalarGridSpec(
            num_scalar_prefetch=1,
            grid=(experts // step,),
            in_specs=in_specs,
            out_specs=out_specs,
            scratch_shapes=[
                pltpu.VMEM((2, model, units), F32),
                pltpu.VMEM((2, model, units), BF16),
                pltpu.SemaphoreType.DMA(()),
            ],
        ),
        out_shape=[jax.ShapeDtypeStruct(s, d) for s, d in outs],
        input_output_aliases={} if first or last else {base: 0, base + 1: 1},
        compiler_params=pltpu.CompilerParams(vmem_limit_bytes=58 * 2**20),
        cost_estimate=pl.CostEstimate(
            flops=2 * experts * slots * model * units, bytes_accessed=4 * 10**6, transcendentals=0
        ),
        name="expert_chunk",
    )(order, *ins)


CAP = 128
GROUP_IMG = 2
CHUNK = 128
HIGHEST = lax.Precision.HIGHEST
TENSOR = ("y", "c")
PLANE = ("x", "y", "c")
EVERY = ("y", "c", "z", "x")
INWARD = [(0, 1), (3, 2)]
MIDDLE = [(1, 2), (2, 1)]
OUTWARD = [(1, 0), (2, 3)]
ACROSS = [(1, 3), (2, 0)]
ORDER = ((0, 1, 2, 3), (1, 0, 2, 3), (2, 3, 1, 0), (3, 2, 1, 0))


def tie(values, *events):
    events = [e for e in events if e is not None]
    if not events:
        return values
    return lax.optimization_barrier((values, *events))[0]


def add(*terms):
    return sum(term.astype(F32) for term in terms).astype(BF16)


class Reduce:
    def __init__(self, grads):
        self.grads = grads
        if len(grads) == 1:
            self.total = lax.psum_scatter(grads[0], "z", scatter_dimension=1, tiled=True)
            return
        own, near, *rest = grads
        self.inward = [lax.ppermute(one, "z", INWARD) for one in rest]

    def forward_far(self, *events):
        if len(self.grads) == 1:
            return self.total
        inward = tie(self.inward[-1], *events)
        far, inward = [one[2] if one.shape[0] == 3 else one for one in (self.grads[-1], inward)]
        three = add(far, inward)
        self.outward_two = lax.ppermute(three, "z", ACROSS)
        return three

    def forward(self, *events):
        if len(self.grads) == 1:
            return self.total
        near = self.grads[1]
        self.inward[0] = tie(self.inward[0], *events)
        two = add(self.grads[2][1], self.inward[0][1])
        self.middle = lax.ppermute(two, "z", MIDDLE)
        self.outward_one = lax.ppermute(tie(near, *events), "z", OUTWARD)
        return two

    def finish(self):
        if len(self.grads) > 1:
            self.total = add(
                self.grads[0], self.inward[0][0], self.outward_one, self.outward_two, self.middle
            )
        return self.total


def gather_packs(pack):
    below = [pack] + [
        lax.ppermute(pack, "z", [(k, (k + far) % 4) for k in range(4)]) for far in (1, 2, 3)
    ]
    column = jnp.stack(below)
    swap = [(0, 1), (1, 0)]
    over_x = lax.ppermute(column, "x", swap)
    over_y = lax.ppermute(column, "y", swap)
    over_both = lax.ppermute(column, ("x", "y"), [(0, 3), (1, 2), (2, 1), (3, 0)])
    four = [column, over_x, over_y, over_both]
    return four + [lax.ppermute(each, "c", swap) for each in four], below[1:]


def shards(
    tokens_in,
    key_mask,
    expert_ids,
    expert_slots,
    norm1_gain,
    norm1_shift,
    qkv_weight,
    qv_bias,
    out_weight,
    out_bias,
    norm2_gain,
    norm2_shift,
    router_weight,
    up_weight,
    up_bias,
    down_weight,
    down_bias,
    out_grad,
):
    length = lax.axis_size("z")
    core = lax.axis_index("c")
    chip_y = lax.axis_index("y")
    quarter = lax.axis_size("y") * 2
    expert = (lax.axis_index("x") * lax.axis_size("y") + chip_y) * 2 + core
    piece, sequence, model = tokens_in.shape
    experts, part, units = up_weight.shape
    dp = model // part
    width = qkv_weight.shape[2]
    tokens = piece * sequence
    blocks = units // CHUNK
    spans = [(0, 3), (3, 5), (5, 6)] if blocks == 6 else [(0, blocks)]

    head = spans[0][1] * CHUNK
    sizes = [head, units - head] if units > head else [head]
    packed = pack_experts(up_weight, down_weight, sizes)
    qkv_weight, norm1_gain = tie((qkv_weight, norm1_gain), packed[0])

    smalls = jnp.concatenate(
        [
            norm1_gain[None],
            norm1_shift[None],
            qv_bias,
            out_bias[None],
            norm2_gain[None],
            norm2_shift[None],
            down_bias,
            router_weight.T,
            up_bias.reshape(experts * quarter, part),
        ],
        0,
    ).astype(BF16)
    small_rows = smalls.shape[0]
    pad = -(small_rows * part) % (16 * model)
    small_block = jnp.pad(smalls.reshape(-1), (0, pad)).reshape(-1, model)
    pack = jnp.concatenate(
        [
            jnp.concatenate(
                [qkv_weight[0], qkv_weight[1], qkv_weight[2], out_weight.T], 1
            ).astype(BF16),
            small_block,
        ],
        0,
    )
    place = [lax.axis_index(name) for name in ("z", "x", "y", "c")]
    if length == 4:
        packs, below = gather_packs(pack)
        by_x = jnp.stack([packs[0][:, part:], packs[1][:, part:]]).reshape(2, 4, -1)
        pick_x = (place[1] ^ jnp.arange(2))[:, None] == jnp.arange(2)
        pick_z = (place[0] - jnp.arange(4)[:, None]) % 4 == jnp.arange(4)
        pick = pick_z[:, None, None, :] & pick_x[None, :, :, None]
        vectors = dot(pick.reshape(8, 8).astype(BF16), by_x.reshape(8, -1)).astype(BF16)
    else:
        packs = lax.all_gather(pack, EVERY, axis=0, tiled=False)
        packs = packs.reshape(quarter, dp, pack.shape[0], model)
        vectors = packs[0, :, part:].reshape(dp, -1)
        packs = [packs[:, :, :part].reshape(quarter, model, model)]
    event = []
    parts = []
    for some in packed:
        some = lax.all_to_all(tie(some, *event), PLANE, 0, 0, tiled=True)
        event = [some, packs[len(packs) // 2]]
        starts = [CHUNK * f for f, _ in spans[1:]] if parts else [0]
        stops = [CHUNK * l for _, l in spans[1:]] if parts else [head]
        base = starts[0]
        parts += [some[..., f - base : l - base] for f, l in zip(starts, stops)]
    if length != 4:
        parts = [
            one.reshape(2, quarter, 2, part, -1).transpose(2, 0, 3, 1, 4).reshape(2, 2 * part, -1)
            for one in parts
        ]

    vectors = vectors[:, : small_rows * part].reshape(dp, small_rows, part).transpose(1, 0, 2)
    lines = vectors[: 7 + 2 * experts].reshape(-1, model).astype(F32)
    bias_pairs = lines[2:4].reshape(2, quarter, width).transpose(1, 0, 2)
    bias_down = lines[7 : 7 + experts]
    router = lines[7 + experts :].astype(BF16)
    bias_up = vectors[7 + 2 * experts :].reshape(experts, quarter, dp, part)
    bias_up = bias_up.transpose(0, 2, 1, 3).reshape(experts, quarter, units)
    bias_up = lax.dynamic_index_in_dim(bias_up, expert, 0, keepdims=False).astype(F32)

    first_group = chip_y * 3
    group_tokens = GROUP_IMG * sequence
    position = (expert_ids * CAP + expert_slots).reshape(-1, group_tokens, 2)
    position_full = lax.dynamic_index_in_dim(position, first_group + 2 * core, 0, keepdims=False)
    position_half = lax.dynamic_index_in_dim(position, first_group + 1, 0, keepdims=False)
    slots_full = jnp.arange(experts * CAP, dtype=jnp.int32)
    half = CAP // 2
    slots_half = (
        jnp.arange(experts, dtype=jnp.int32)[:, None] * CAP
        + core * half
        + jnp.arange(half, dtype=jnp.int32)
    ).reshape(-1)
    match_full = slots_full[:, None, None] == position_full.T[None]
    match_half = slots_half[:, None, None] == position_half.T[None]
    hot_full = (match_full[:, 0] | match_full[:, 1]).astype(BF16)
    hot_half = (match_half[:, 0] | match_half[:, 1]).astype(BF16)
    swap = [(0, 1), (1, 0)]

    def both_groups(values):
        lent = jnp.where(core == 0, values[2], values[0])
        other = lax.ppermute(lent, "c", swap)
        full = jnp.where(core == 0, values[:2], values[1:])
        shared = jnp.where(core == 0, jnp.stack([lent, other]), jnp.stack([other, lent]))
        return (
            full.reshape(group_tokens, -1),
            shared.reshape(group_tokens, -1),
        )

    def join_rows(full, shared):
        full = full.reshape((experts, CAP) + full.shape[1:])
        shared = shared.reshape((experts, half) + shared.shape[1:])
        return jnp.concatenate([full, shared], 1)

    def lines_of(values):
        high = values.astype(BF16)
        low = (values - high.astype(F32)).astype(BF16)
        both = jnp.stack([high, low], 1)
        return jnp.pad(both, ((0, 0), (0, 14), (0, model - both.shape[2])))

    def values_of(rows):
        both = rows[:, CAP + half : CAP + half + 2, : CAP + half].astype(F32)
        return both[:, 0] + both[:, 1]

    def swap_experts(rows, *events):
        return lax.all_to_all(tie(rows, *events), PLANE, 0, 0, tiled=True)

    def dispatch(full, shared):
        return join_rows(dot(hot_full, full).astype(BF16), dot(hot_half, shared).astype(BF16))

    def combine(back):
        full = dot(hot_full, back[:, :CAP].reshape(-1, model), 0, 0)
        shared = dot(hot_half, back[:, CAP : CAP + half].reshape(-1, model), 0, 0)
        full = full.reshape(GROUP_IMG, sequence, model)
        shared = shared.reshape(GROUP_IMG, sequence, model)
        mine = jnp.where(core == 0, shared[0], shared[1])
        theirs = jnp.where(core == 0, shared[1], shared[0])
        mine = mine + lax.ppermute(theirs, "c", swap)
        return jnp.where(
            core == 0,
            jnp.concatenate([full, mine[None]]),
            jnp.concatenate([mine[None], full]),
        )

    if length == 4:
        parts[0] = tie(parts[0], *below)
    full_parts = [
        lax.all_gather(one, "z", axis=0, tiled=False)
        if length == 4
        else lax.all_gather(one, "z", axis=1, tiled=True)
        for one in parts
    ]
    grad_full, grad_shared = both_groups(out_grad)
    incoming = swap_experts(dispatch(grad_full, grad_shared), packs[-1], parts[-1])

    local_start = (chip_y * 2 + core) * piece
    mask_here = lax.dynamic_slice_in_dim(key_mask, local_start, piece, 0)[:, None]
    n1, n2, residual, q, k, v, attended, lse, wq, wk, wv, wo = attend_forward(
        jnp.stack(place).astype(jnp.int32),
        tokens_in, mask_here, lines, bias_pairs,
        packs, width,
    )
    n2 = tie(n2, incoming)
    normed_two = n2.reshape(tokens, model)

    normed_full, normed_shared = both_groups(n2)

    def chances_of(rows):
        return jax.nn.softmax(dot(rows, router, 1, 1), -1)

    probabilities = chances_of(normed_two)
    hot_ids = expert_ids[..., None] == jnp.arange(experts, dtype=jnp.int32)
    hot_here = lax.dynamic_slice_in_dim(hot_ids, local_start, piece, 0).astype(F32)
    hot_here = jnp.sum(hot_here.reshape(tokens, 2, experts), 1)
    share_here = hot_here * probabilities

    def slot_gates(match, rows, position_here):
        chance = chances_of(rows)
        hot = (position_here // CAP)[..., None] == jnp.arange(experts, dtype=jnp.int32)
        gates = jnp.sum(hot.astype(F32) * chance[:, None], -1)
        return jnp.sum(jnp.where(match, gates.T[None], 0.0), (1, 2))

    gates_sent = join_rows(
        slot_gates(match_full, normed_full, position_full),
        slot_gates(match_half, normed_shared, position_half),
    )
    chosen = swap_experts(
        jnp.concatenate([dispatch(normed_full, normed_shared), lines_of(gates_sent)], 1),
        incoming,
    )

    order = jnp.asarray(
        [ORDER[k] + (int(k in (0, 3)),) for k in range(4)] if length == 4 else [[0] * 5] * length,
        jnp.int32,
    )
    order = lax.dynamic_index_in_dim(order, place[0], 0, keepdims=False)
    sums = None
    bias_parts = []
    reduced = []
    count = len(spans)
    for index, (first, last) in enumerate(spans):
        bias_one = bias_up[:, first * CHUNK : last * CHUNK].reshape(1, -1)
        final = index == count - 1
        events = []
        if count == 3 and index == 2:
            events.append(reduced[0].forward_far())
        *sums, bias_part = (
            outs := expert_chunk(
                order, chosen, incoming, tie(bias_one, *events), sums, full_parts[index], final
            )
        )[:3]
        bias_parts.append(bias_part.reshape(quarter, -1))
        reduced.append(Reduce(outs[3:]))

    mixed, pulled = sums
    back = swap_experts(pulled)
    gate_back = values_of(back)
    norm_two_grad = combine(back)
    mixed = swap_experts(mixed, back)
    if count == 3:
        norm_two_grad = tie(norm_two_grad, reduced[0].forward(back))

    def slots_to_tokens(match, parts_here):
        parts_here = parts_here.reshape(experts, -1)
        match = (match[:, 0] | match[:, 1]).reshape(experts, -1, group_tokens)
        return jnp.sum(jnp.where(match, parts_here[..., None], 0.0), 1).T

    prob_full = slots_to_tokens(match_full, gate_back[:, :CAP])
    prob_shared = slots_to_tokens(match_half, gate_back[:, CAP:])
    prob_full = prob_full.reshape(GROUP_IMG, sequence, experts)
    prob_shared = prob_shared.reshape(GROUP_IMG, sequence, experts)
    mine = jnp.where(core == 0, prob_shared[0], prob_shared[1])
    theirs = jnp.where(core == 0, prob_shared[1], prob_shared[0])
    mine = mine + lax.ppermute(theirs, "c", swap)
    chance_grad = jnp.where(
        core == 0,
        jnp.concatenate([prob_full, mine[None]]),
        jnp.concatenate([mine[None], prob_full]),
    ).reshape(tokens, experts)
    grad_rows = out_grad.reshape(tokens, model)
    bias_dot = dot(grad_rows, bias_down.astype(BF16), 1, 1)
    chance_grad = chance_grad + hot_here * bias_dot
    logit_grad = probabilities * (
        chance_grad - jnp.sum(probabilities * chance_grad, -1, keepdims=True)
    )
    logit_grad = logit_grad.astype(BF16)
    router_grad = dot(logit_grad, normed_two, 0, 0)
    down_bias_grad = lax.dot_general(
        share_here, grad_rows.astype(F32), (((0,), (0,)), ((), ())), precision=HIGHEST
    )

    norm_two_grad = norm_two_grad + dot(logit_grad, router).reshape(norm_two_grad.shape)
    h_grad, hb, dq, dk, dv, line_sums, pair_sums = attend_backward(
        norm_two_grad, out_grad, residual, mask_here, wo, lines, q, k, v, lse
    )
    input_grad, line_ones = input_backward(h_grad, tokens_in, wq, wk, wv, lines, dq, dk, dv)
    if count == 3:
        hb = tie(
            hb, mixed, reduced[0].finish(), reduced[1].forward(hb), reduced[1].forward_far(hb)
        )

    bias_rows = jnp.concatenate(bias_parts, 1).reshape(dp, quarter, part)
    bias_rows = jnp.where(
        jnp.arange(experts)[:, None, None, None] == expert, bias_rows[None], 0.0
    )
    bias_rows = bias_rows.transpose(0, 2, 1, 3).reshape(experts * quarter, dp, part)
    line_grads = jnp.concatenate(
        [
            line_ones[:2],
            pair_sums[:, 0].reshape(1, model),
            pair_sums[:, 1].reshape(1, model),
            line_sums[:3],
            down_bias_grad,
            router_grad,
        ],
        0,
    ).reshape(-1, dp, part)
    sum_type = BF16 if length == 4 else F32
    vector_grads = jnp.concatenate([line_grads, bias_rows], 0).astype(sum_type)
    vector_grads = vector_grads.transpose(1, 0, 2).reshape(dp, small_rows * part)
    vector_grads = jnp.pad(vector_grads, ((0, 0), (0, pad))).reshape(dp, -1, model)

    if length == 4:
        pack_grads = attend_weights(n1, hb, dq, dk, dv, attended, vector_grads)
    else:
        pack_grads = attend_weights(n1, hb, dq, dk, dv, attended, None)
        pack_grads = pack_grads.reshape(quarter, dp, part, model)
        vector_grads = jnp.broadcast_to(vector_grads[None], (quarter,) + vector_grads.shape)
        pack_grads = jnp.concatenate([pack_grads, vector_grads], 2)
        pack_grads = pack_grads.reshape(quarter // 2, 2, dp // 2, 2, -1, model)
        pack_grads = pack_grads.transpose(1, 3, 0, 2, 4, 5)
    mine = lax.dynamic_index_in_dim(pack_grads, core, 0, keepdims=False)
    theirs = lax.dynamic_index_in_dim(pack_grads, 1 - core, 0, keepdims=False)
    theirs = lax.ppermute(theirs, "c", swap)
    pack_grads = (mine.astype(F32) + theirs.astype(F32)).astype(sum_type)
    pack_grads = pack_grads.reshape((-1,) + pack_grads.shape[2:])
    if count == 3:
        pack_grads = tie(
            pack_grads,
            reduced[2].forward(pack_grads),
            reduced[2].forward_far(pack_grads),
            reduced[1].finish(),
        )
    pack_grads = lax.all_to_all(pack_grads, ("x", "y"), 0, 0, tiled=True)
    pack_grads = jnp.sum(pack_grads.astype(F32), 0).astype(sum_type)
    if count == 3:
        reduced[2].finish()
    if length == 4:
        pack_grad = lax.dynamic_index_in_dim(pack_grads, place[0], 0, keepdims=False).astype(F32)
        for far in (1, 2, 3):
            some = lax.dynamic_index_in_dim(pack_grads, (place[0] + far) % 4, 0, keepdims=False)
            some = lax.ppermute(some, "z", [(k, (k + far) % 4) for k in range(4)])
            pack_grad = pack_grad + some.astype(F32)
    else:
        pack_grad = lax.psum_scatter(pack_grads, "z", scatter_dimension=0, tiled=False)
    qkv_out = pack_grad[:part, : 3 * width].reshape(part, 3, width).transpose(1, 0, 2)
    out_weight_grad = pack_grad[:part, 3 * width :].T
    small_grads = pack_grad[part:].reshape(-1)[: small_rows * part].reshape(small_rows, part)

    mixture = combine(mixed)
    bias_term = jnp.dot(share_here, bias_down, precision=HIGHEST).reshape(residual.shape)
    output = (residual + mixture + bias_term).astype(BF16)

    ups, downs = [], []
    totals = [one.total for one in reduced]
    if length != 4:
        totals = [
            one.reshape(2, 2, part, quarter, -1).transpose(1, 3, 0, 2, 4).reshape(experts, 2, part, -1)
            for one in totals
        ]
    for some, event in ((totals[:1], mixed), (totals[1:2], pack_grads), (totals[2:], pack_grads)):
        if some:
            some = some[0] if len(some) == 1 else jnp.concatenate(some, -1)
            some = lax.all_to_all(tie(some.astype(BF16), event), PLANE, 0, 0, tiled=True).astype(F32)
            ups.append(some[:, 0])
            downs.append(some[:, 1])
    up_grad = jnp.concatenate(ups, -1)
    down_grad = jnp.concatenate(downs, -1).transpose(0, 2, 1)
    return (
        output,
        input_grad,
        small_grads[0],
        small_grads[1],
        qkv_out,
        small_grads[2:4],
        out_weight_grad,
        small_grads[4],
        small_grads[5],
        small_grads[6],
        small_grads[7 + experts : 7 + 2 * experts].T,
        up_grad,
        small_grads[7 + 2 * experts :].reshape(experts, -1),
        down_grad,
        small_grads[7 : 7 + experts],
    )


def solution(mesh):
    dp, tensor = mesh.devices.shape
    planes = jax.sharding.Mesh(
        mesh.devices.reshape(dp // 2, 2, tensor // 2, 2), ("z", "x", "y", "c")
    )
    rows = ("z", "x")
    images = P(("z", "x", "y", "c"), None, None)
    return jax.shard_map(
        shards,
        mesh=planes,
        in_specs=(
            images,
            P(rows, None),
            P(rows, None, None),
            P(rows, None, None),
            P(rows),
            P(rows),
            P(None, rows, TENSOR),
            P(None, rows),
            P(TENSOR, rows),
            P(rows),
            P(rows),
            P(rows),
            P(rows, None),
            P(None, rows, TENSOR),
            P(None, rows),
            P(None, TENSOR, rows),
            P(None, rows),
            images,
        ),
        out_specs=(
            images,
            images,
            P(rows),
            P(rows),
            P(None, rows, TENSOR),
            P(None, rows),
            P(TENSOR, rows),
            P(rows),
            P(rows),
            P(rows),
            P(rows, None),
            P(None, rows, TENSOR),
            P(None, rows),
            P(None, TENSOR, rows),
            P(None, rows),
        ),
        check_vma=False,
    )
```

```python
import functools
import jax
import jax.numpy as jnp
from jax import lax
from jax.experimental import pallas as pl
from jax.experimental.pallas import tpu as pltpu
from jax.sharding import PartitionSpec as P

HD = 64
EPSILON = 1e-06
NEGATIVE = -1e30
F32 = jnp.float32
BF16 = jnp.bfloat16


def dot(left, right, left_dim=1, right_dim=0):
    return lax.dot_general(
        left, right, (((left_dim,), (right_dim,)), ((), ())), preferred_element_type=F32
    )


def norm_forward(values, gains, shifts):
    middle = jnp.mean(values, -1, keepdims=True)
    centred = values - middle
    inverse = lax.rsqrt(jnp.mean(centred * centred, -1, keepdims=True) + EPSILON)
    unit_rows = centred * inverse
    return (unit_rows * gains + shifts, unit_rows, inverse)


def norm_backward(grad_rows, unit_rows, inverse, gains):
    scaled = grad_rows * gains
    return inverse * (
        scaled
        - jnp.mean(scaled, -1, keepdims=True)
        - unit_rows * jnp.mean(scaled * unit_rows, -1, keepdims=True)
    )


def head_masks(width):
    lane = lax.broadcasted_iota(jnp.int32, (1, width), 1)
    return [(lane // HD == k) for k in range(width // HD)]


def arrange(w_ref, *parts):
    width = parts[0].shape[2]
    for t in range(w_ref.shape[0]):
        packed = w_ref[t]
        for k, ref in enumerate(parts):
            ref[t] = packed[:, k * width : (k + 1) * width]


def put_rows(ref, values):
    rows, columns = values.shape
    spare = jnp.zeros((ref.shape[0] - rows, columns), values.dtype)
    ref[...] = jnp.concatenate([values, spare], 0).astype(ref.dtype)


def attend_forward_kernel(
    place_ref, tokens_ref, mask_ref, lines_ref, bias_ref, *refs,
):
    (
        n1_ref, n2_ref, h_ref, q_ref, k_ref, v_ref, o_ref, lse_ref,
        wq_ref, wk_ref, wv_ref, wo_ref, all_ref, sem,
    ) = refs[-14:]
    packs = refs[:-14]

    @pl.when(pl.program_id(0) == 0)
    def _():
        if len(packs) == 1:
            pltpu.make_async_copy(packs[0], all_ref, sem).start()
        else:
            z, x, y, c = [place_ref[k] for k in range(4)]
            part = all_ref.shape[1] // 8
            for index, ref in enumerate(packs):
                dx, dy, dc = index & 1, (index >> 1) & 1, index >> 2
                t = (y ^ dy) * 2 + (c ^ dc)
                for back in range(4):
                    row = (((z - back) & 3) * 2 + (x ^ dx)) * part
                    pltpu.make_async_copy(
                        ref.at[back, pl.ds(0, part)],
                        all_ref.at[t, pl.ds(pl.multiple_of(row, 32), part)],
                        sem,
                    ).start()
        pltpu.make_async_copy(all_ref, all_ref, sem).wait()
        arrange(all_ref, wq_ref, wk_ref, wv_ref, wo_ref)

    x = tokens_ref[0].astype(F32)
    n1, _, _ = norm_forward(x, lines_ref[0:1, :], lines_ref[1:2, :])
    put_rows(n1_ref.at[0], n1)
    n1 = n1.astype(BF16)
    width = wq_ref.shape[2]
    masks = head_masks(width)
    keys = mask_ref[0] > 0
    total = x + lines_ref[4:5, :]
    for t in range(wq_ref.shape[0]):
        q = (dot(n1, wq_ref[t]) + bias_ref[t, 0:1, :]).astype(BF16)
        k = dot(n1, wk_ref[t]).astype(BF16)
        v = (dot(n1, wv_ref[t]) + bias_ref[t, 1:2, :]).astype(BF16)
        q_ref[0, t] = q
        k_ref[0, t] = k
        v_ref[0, t] = v
        scaled = q * jnp.asarray(HD ** (-0.5), BF16)
        o = jnp.zeros(q.shape, F32)
        for h, here in enumerate(masks):
            s = dot(jnp.where(here, scaled, jnp.zeros_like(scaled)), k, 1, 1)
            s = jnp.where(keys, s, NEGATIVE)
            largest = jnp.max(s, -1, keepdims=True)
            e = jnp.exp(s - largest)
            total_e = jnp.sum(e, -1, keepdims=True)
            p = (e / total_e).astype(BF16)
            o = jnp.where(here, dot(p, v), o)
            index = t * len(masks) + h
            lse_ref[0, :, index : index + 1] = largest + jnp.log(total_e)
        put_rows(o_ref.at[0, t], o)
        total = total + dot(o.astype(BF16), wo_ref[t], 1, 1)
    h_ref[0] = total
    n2, _, _ = norm_forward(total, lines_ref[5:6, :], lines_ref[6:7, :])
    n2_ref[0] = n2.astype(BF16)


def whole(shape):
    return pl.BlockSpec(shape, lambda b: (0,) * len(shape))


def by_image(shape):
    return pl.BlockSpec((1,) + shape[1:], lambda b: (b,) + (0,) * (len(shape) - 1))


def padded(rows):
    return -(-rows // 16) * 16


def attend_forward(place, tokens_in, mask, lines, bias_pairs, packs, width):
    images, sequence, model = tokens_in.shape
    quarter = model // width
    rows = (images, sequence, model)
    heads = (images, quarter, sequence, width)
    columns = (quarter, model, width)
    outs = [
        ((images, padded(sequence), model), BF16), (rows, BF16), (rows, F32), (heads, BF16), (heads, BF16),
        (heads, BF16), ((images, quarter, padded(sequence), width), BF16), ((images, sequence, 128), F32),
        (columns, BF16), (columns, BF16), (columns, BF16), (columns, BF16),
    ]
    place_spec = lambda spec: pl.BlockSpec(spec.block_shape, lambda b, p: spec.index_map(b))
    in_specs = [by_image(tokens_in.shape), by_image(mask.shape), whole(lines.shape), whole(bias_pairs.shape)]
    out_specs = [by_image(s) for s, _ in outs[:8]] + [whole(s) for s, _ in outs[8:]]
    return pl.pallas_call(
        attend_forward_kernel,
        grid_spec=pltpu.PrefetchScalarGridSpec(
            num_scalar_prefetch=1,
            grid=(images,),
            in_specs=[place_spec(s) for s in in_specs]
            + [pl.BlockSpec(memory_space=pl.ANY)] * len(packs),
            out_specs=[place_spec(s) for s in out_specs],
            scratch_shapes=[pltpu.VMEM((quarter, model, 4 * width), BF16), pltpu.SemaphoreType.DMA(())],
        ),
        out_shape=[jax.ShapeDtypeStruct(s, d) for s, d in outs],
        compiler_params=pltpu.CompilerParams(vmem_limit_bytes=56 * 2**20),
        cost_estimate=pl.CostEstimate(flops=2 * 10**9, bytes_accessed=4 * 10**6, transcendentals=0),
        name="attend_forward",
    )(place, tokens_in, mask, lines, bias_pairs, *packs)


def attend_backward_kernel(
    n2_grad_ref, grad_ref, h_ref, mask_ref, wo_ref, lines_ref, q_ref, k_ref, v_ref, lse_ref,
    h_grad_ref, hb_ref, dq_ref, dk_ref, dv_ref, vec_ref, pair_ref,
):
    @pl.when(pl.program_id(0) == 0)
    def _():
        vec_ref[...] = jnp.zeros_like(vec_ref)
        pair_ref[...] = jnp.zeros_like(pair_ref)

    n2_grad = n2_grad_ref[0]
    _, unit_two, inverse_two = norm_forward(h_ref[0], lines_ref[5:6, :], lines_ref[6:7, :])
    vec_ref[1:2, :] += jnp.sum(n2_grad * unit_two, 0, keepdims=True)
    vec_ref[2:3, :] += jnp.sum(n2_grad, 0, keepdims=True)
    h_grad = grad_ref[0].astype(F32) + norm_backward(
        n2_grad, unit_two, inverse_two, lines_ref[5:6, :]
    )
    vec_ref[0:1, :] += jnp.sum(h_grad, 0, keepdims=True)
    h_grad_ref[0] = h_grad
    put_rows(hb_ref.at[0], h_grad)
    hb = h_grad.astype(BF16)
    width = wo_ref.shape[2]
    masks = head_masks(width)
    keys = mask_ref[0] > 0
    scale = HD ** (-0.5)
    for t in range(wo_ref.shape[0]):
        do = dot(hb, wo_ref[t]).astype(BF16)
        q, k, v = q_ref[0, t], k_ref[0, t], v_ref[0, t]
        zero = jnp.zeros_like(q)
        scaled = q * jnp.asarray(scale, BF16)
        dq = jnp.zeros(q.shape, F32)
        dk = jnp.zeros(q.shape, F32)
        dv = jnp.zeros(q.shape, F32)
        for h, here in enumerate(masks):
            index = t * len(masks) + h
            s = dot(jnp.where(here, scaled, zero), k, 1, 1)
            s = jnp.where(keys, s, NEGATIVE)
            p = jnp.exp(s - lse_ref[0, :, index : index + 1])
            dp = dot(jnp.where(here, do, zero), v, 1, 1)
            ds = p * (dp - jnp.sum(p * dp, -1, keepdims=True))
            ds = ds.astype(BF16)
            dv = jnp.where(here, dot(p.astype(BF16), do, 0, 0), dv)
            dq = jnp.where(here, dot(ds, k), dq)
            dk = jnp.where(here, dot(ds, q, 0, 0), dk)
        dq = (dq * scale).astype(BF16).astype(F32)
        dv = dv.astype(BF16).astype(F32)
        pair_ref[t, 0:1, :] += jnp.sum(dq, 0, keepdims=True)
        pair_ref[t, 1:2, :] += jnp.sum(dv, 0, keepdims=True)
        put_rows(dq_ref.at[0, t], dq)
        put_rows(dk_ref.at[0, t], dk * scale)
        put_rows(dv_ref.at[0, t], dv)


def attend_backward(n2_grad, out_grad, h, mask, wo, lines, q, k, v, lse):
    ins = (n2_grad, out_grad, h, mask, wo, lines, q, k, v, lse)
    shared = {4, 5}
    images, sequence, model = n2_grad.shape
    quarter, _, width = wo.shape
    heads = ((images, quarter, padded(sequence), width), BF16)
    outs = [
        (n2_grad.shape, F32), ((images, padded(sequence), model), BF16), heads, heads, heads,
        ((8, model), F32), ((quarter, 8, width), F32),
    ]
    return pl.pallas_call(
        attend_backward_kernel,
        grid=(images,),
        in_specs=[whole(a.shape) if i in shared else by_image(a.shape) for i, a in enumerate(ins)],
        out_specs=[by_image(s) for s, _ in outs[:5]] + [whole(s) for s, _ in outs[5:]],
        out_shape=[jax.ShapeDtypeStruct(s, d) for s, d in outs],
        compiler_params=pltpu.CompilerParams(vmem_limit_bytes=56 * 2**20),
        cost_estimate=pl.CostEstimate(flops=0, bytes_accessed=0, transcendentals=0),
        name="attend_backward",
    )(*ins)


def attend_weights_kernel(n1_ref, hb_ref, dq_ref, dk_ref, dv_ref, o_ref, *refs):
    out_ref = refs[-1]
    width = dq_ref.shape[3]
    n1 = n1_ref[...].reshape(-1, n1_ref.shape[2])
    hb = hb_ref[...].reshape(-1, n1_ref.shape[2])
    for k, (left, ref) in enumerate(((n1, dq_ref), (n1, dk_ref), (n1, dv_ref), (hb, o_ref))):
        sums = dot(left, ref[...].reshape(-1, width), 0, 0).astype(out_ref.dtype)
        columns = slice(k * width, (k + 1) * width)
        if len(refs) == 1:
            out_ref[0, :, columns] = sums
            continue
        part = sums.shape[0] // 8
        for z in range(4):
            for x in range(2):
                start = (z * 2 + x) * part
                out_ref[0, x, 0, z, :part, columns] = sums[start : start + part]
    if len(refs) == 2:
        for z in range(4):
            for x in range(2):
                out_ref[0, x, 0, z, part:, :] = refs[0][z * 2 + x]


def attend_weights(n1, hb, dq, dk, dv, o, extra):
    images, quarter, rows, width = dq.shape
    model = n1.shape[2]
    heads = pl.BlockSpec((images, 1, rows, width), lambda t: (0, t, 0, 0))
    if extra is None:
        out_spec = pl.BlockSpec((1, model, 4 * width), lambda t: (t, 0, 0))
        out_shape = jax.ShapeDtypeStruct((quarter, model, 4 * width), F32)
    else:
        depth = model // 8 + extra.shape[1]
        out_spec = pl.BlockSpec(
            (1, 2, 1, 4, depth, model), lambda t: (t % 2, 0, t // 2, 0, 0, 0)
        )
        out_shape = jax.ShapeDtypeStruct((2, 2, 2, 4, depth, model), BF16)
    extras = [] if extra is None else [extra]
    return pl.pallas_call(
        attend_weights_kernel,
        grid=(quarter,),
        in_specs=[whole(n1.shape), whole(hb.shape)] + [heads] * 4 + [whole(e.shape) for e in extras],
        out_specs=out_spec,
        out_shape=out_shape,
        compiler_params=pltpu.CompilerParams(vmem_limit_bytes=56 * 2**20),
        cost_estimate=pl.CostEstimate(flops=0, bytes_accessed=0, transcendentals=0),
        name="attend_weights",
    )(n1, hb, dq, dk, dv, o, *extras)


def input_backward_kernel(
    h_grad_ref, tokens_ref, wq_ref, wk_ref, wv_ref, lines_ref, dq_ref, dk_ref, dv_ref,
    input_grad_ref, vec_ref,
):
    @pl.when(pl.program_id(0) == 0)
    def _():
        vec_ref[...] = jnp.zeros_like(vec_ref)

    rows = tokens_ref.shape[1]
    n1_grad = jnp.zeros((dq_ref.shape[2], tokens_ref.shape[2]), F32)
    for t in range(wq_ref.shape[0]):
        for grads, weights in ((dq_ref, wq_ref), (dk_ref, wk_ref), (dv_ref, wv_ref)):
            n1_grad += dot(grads[0, t], weights[t], 1, 1)
    n1_grad = n1_grad[:rows]
    _, unit_one, inverse_one = norm_forward(
        tokens_ref[0].astype(F32), lines_ref[0:1, :], lines_ref[1:2, :]
    )
    vec_ref[0:1, :] += jnp.sum(n1_grad * unit_one, 0, keepdims=True)
    vec_ref[1:2, :] += jnp.sum(n1_grad, 0, keepdims=True)
    input_grad_ref[0] = h_grad_ref[0] + norm_backward(
        n1_grad, unit_one, inverse_one, lines_ref[0:1, :]
    )


def input_backward(h_grad, tokens_in, wq, wk, wv, lines, dq, dk, dv):
    ins = (h_grad, tokens_in, wq, wk, wv, lines, dq, dk, dv)
    outs = [(h_grad.shape, F32), ((8, wq.shape[1]), F32)]
    return pl.pallas_call(
        input_backward_kernel,
        grid=(h_grad.shape[0],),
        in_specs=[whole(a.shape) if 2 <= i <= 5 else by_image(a.shape) for i, a in enumerate(ins)],
        out_specs=[by_image(outs[0][0]), whole(outs[1][0])],
        out_shape=[jax.ShapeDtypeStruct(s, d) for s, d in outs],
        compiler_params=pltpu.CompilerParams(vmem_limit_bytes=56 * 2**20),
        cost_estimate=pl.CostEstimate(flops=0, bytes_accessed=0, transcendentals=0),
        name="input_backward",
    )(*ins)


def pack_experts_kernel(up_ref, down_ref, *refs):
    up = up_ref[0].astype(BF16)
    down = down_ref[0].T.astype(BF16)
    start = 0
    for ref in refs:
        stop = start + ref.shape[3]
        ref[0, 0] = up[:, start:stop]
        ref[0, 1] = down[:, start:stop]
        start = stop


def pack_experts(up, down, sizes):
    experts, part, units = up.shape
    outs = [(experts, 2, part, size) for size in sizes]
    return pl.pallas_call(
        pack_experts_kernel,
        grid=(experts,),
        in_specs=[by_image(up.shape), by_image(down.shape)],
        out_specs=[by_image(s) for s in outs],
        out_shape=[jax.ShapeDtypeStruct(s, BF16) for s in outs],
        compiler_params=pltpu.CompilerParams(vmem_limit_bytes=32 * 2**20),
        cost_estimate=pl.CostEstimate(flops=0, bytes_accessed=8 * 10**6, transcendentals=0),
        name="pack_experts",
    )(up, down)


def to_column(line):
    return jnp.broadcast_to(line, (128, 256)).T[:, :1]


def to_line(column):
    return jnp.broadcast_to(column, (256, 128)).T[:1, :]


def expert_kernel(first, last, x_ref, g_ref, b_ref, shards_ref, *refs):
    if not first:
        (y_in, p_in), refs = refs[:2], refs[2:]
    (y_out, p_out, bias_ref), refs = refs[:3], refs[3:]
    acc_ref, w_ref, sem = refs[-3:]
    grads_ref = refs[0]
    step = pl.program_id(0)
    model = w_ref.shape[1]

    @pl.when(step == 0)
    def _():
        if len(shards_ref.shape) == 3:
            pltpu.make_async_copy(shards_ref, w_ref, sem).start()
        else:
            part, units = shards_ref.shape[3:]
            for z in range(4):
                for p in range(8):
                    row = (z * 2 + p // 4) * part
                    pltpu.make_async_copy(
                        shards_ref.at[z, p],
                        w_ref.at[:, pl.ds(row, part), pl.ds((p % 4) * units, units)],
                        sem,
                    ).start()
        acc_ref[...] = jnp.zeros_like(acc_ref)
        bias_ref[...] = jnp.zeros_like(bias_ref)
        pltpu.make_async_copy(w_ref, w_ref, sem).wait()

    sources, slots, _ = g_ref.shape
    x = x_ref[:, :slots].reshape(-1, model)
    g_raw = g_ref[...].reshape(-1, model)
    gates = []
    for k in range(sources):
        parts = x_ref[k, slots : slots + 16, :256].astype(F32)
        gates.append(to_column(parts[0:1] + parts[1:2])[:slots])
    gate = jnp.concatenate(gates, 0)
    g = (g_raw.astype(F32) * gate).astype(BF16)
    hidden = dot(x, w_ref[0]) + b_ref[...]
    cdf = 0.5 * (1.0 + lax.erf(hidden * (0.5 ** 0.5)))
    active = (hidden * cdf).astype(BF16)
    slope = cdf + hidden * (jnp.exp(-0.5 * hidden * hidden) * 0.3989422804014327)
    hidden_grad = (dot(g, w_ref[1]) * slope).astype(BF16)
    y = dot(active, w_ref[1], 1, 1)
    p = dot(hidden_grad, w_ref[0], 1, 1)
    if not first:
        y = y_in[...].reshape(-1, model) + y
        p = p_in[...].reshape(-1, model) + p
    if not last:
        y_out[...] = y.reshape(sources, slots, model)
        p_out[...] = p.reshape(sources, slots, model)
    else:
        y_out[...] = (y * gate).astype(BF16).reshape(sources, slots, model)
        p_out[:, :slots] = p.astype(BF16).reshape(sources, slots, model)
        gate_grad = jnp.sum(g_raw.astype(F32) * y, -1, keepdims=True)
        for k in range(sources):
            own = gate_grad[k * slots : (k + 1) * slots]
            line = to_line(jnp.concatenate([own, jnp.zeros((256 - slots, 1), F32)], 0))
            high = line.astype(BF16)
            low = (line - high.astype(F32)).astype(BF16)
            block = jnp.concatenate([high, low, jnp.zeros((14, 256), BF16)], 0)
            p_out[k, slots:] = jnp.concatenate([block, jnp.zeros((16, model - 256), BF16)], 1)
    bias_ref[...] += jnp.sum(hidden_grad.astype(F32), 0, keepdims=True)
    acc_ref[0] += dot(x, hidden_grad, 0, 0)
    acc_ref[1] += dot(g, active, 0, 0)

    @pl.when(step == pl.num_programs(0) - 1)
    def _():
        if len(shards_ref.shape) == 3:
            grads_ref[...] = acc_ref[...]
        else:
            part, units = shards_ref.shape[3:]
            for z in range(4):
                for q in range(8):
                    row = (z * 2 + q // 4) * part
                    columns = slice((q % 4) * units, (q % 4 + 1) * units)
                    grads_ref[z, q] = acc_ref[:, row : row + part, columns].astype(BF16)


def expert_chunk(x, g, b, sums, shards, last):
    experts, slots, model = g.shape
    units = b.shape[1]
    first = sums is None
    step = 2
    block = lambda rows: pl.BlockSpec((step, rows, model), lambda i: (i, 0, 0))
    full = whole
    ins = [x, g, b, shards] + ([] if first else list(sums))
    in_specs = [block(x.shape[1]), block(slots), full(b.shape)]
    in_specs.append(pl.BlockSpec(memory_space=pl.ANY))
    in_specs += [] if first else [block(slots)] * 2
    rows = (experts, slots, model)
    if last:
        outs = [(rows, BF16), (x.shape, BF16)]
    else:
        outs = [(rows, F32), (rows, F32)]
    out_specs = [block(s[1]) for s, _ in outs]
    outs.append((b.shape, F32))
    if len(shards.shape) == 3:
        outs.append(((2, model, units), F32))
    else:
        outs.append((shards.shape, BF16))
    out_specs += [full(s) for s, _ in outs[2:]]
    base = 4
    return pl.pallas_call(
        functools.partial(expert_kernel, first, last),
        grid=(experts // step,),
        in_specs=in_specs,
        out_specs=out_specs,
        scratch_shapes=[
            pltpu.VMEM((2, model, units), F32),
            pltpu.VMEM((2, model, units), BF16),
            pltpu.SemaphoreType.DMA(()),
        ],
        out_shape=[jax.ShapeDtypeStruct(s, d) for s, d in outs],
        input_output_aliases={} if first or last else {base: 0, base + 1: 1},
        compiler_params=pltpu.CompilerParams(vmem_limit_bytes=58 * 2**20),
        cost_estimate=pl.CostEstimate(
            flops=2 * experts * slots * model * units, bytes_accessed=4 * 10**6, transcendentals=0
        ),
        name="expert_chunk",
    )(*ins)


CAP = 128
GROUP_IMG = 2
CHUNK = 128
HIGHEST = lax.Precision.HIGHEST
TENSOR = ("y", "c")
PLANE = ("x", "y", "c")
EVERY = ("y", "c", "z", "x")


def tie(values, *events):
    events = [e for e in events if e is not None]
    if not events:
        return values
    return lax.optimization_barrier((values, *events))[0]


def gather_packs(pack):
    below = [pack] + [
        lax.ppermute(pack, "z", [(k, (k + far) % 4) for k in range(4)]) for far in (1, 2, 3)
    ]
    column = jnp.stack(below)
    swap = [(0, 1), (1, 0)]
    over_x = lax.ppermute(column, "x", swap)
    over_y = lax.ppermute(column, "y", swap)
    over_both = lax.ppermute(column, ("x", "y"), [(0, 3), (1, 2), (2, 1), (3, 0)])
    four = [column, over_x, over_y, over_both]
    return four + [lax.ppermute(each, "c", swap) for each in four], below[1:]


def shards(
    tokens_in,
    key_mask,
    expert_ids,
    expert_slots,
    norm1_gain,
    norm1_shift,
    qkv_weight,
    qv_bias,
    out_weight,
    out_bias,
    norm2_gain,
    norm2_shift,
    router_weight,
    up_weight,
    up_bias,
    down_weight,
    down_bias,
    out_grad,
):
    length = lax.axis_size("z")
    core = lax.axis_index("c")
    chip_y = lax.axis_index("y")
    quarter = lax.axis_size("y") * 2
    expert = (lax.axis_index("x") * lax.axis_size("y") + chip_y) * 2 + core
    piece, sequence, model = tokens_in.shape
    experts, part, units = up_weight.shape
    dp = model // part
    width = qkv_weight.shape[2]
    tokens = piece * sequence
    blocks = units // CHUNK
    spans = [(0, 3), (3, 5), (5, 6)] if blocks == 6 else [(0, blocks)]

    head = spans[0][1] * CHUNK
    sizes = [head, units - head] if units > head else [head]
    packed = pack_experts(up_weight, down_weight, sizes)
    qkv_weight, norm1_gain = tie((qkv_weight, norm1_gain), packed[0])

    smalls = jnp.concatenate(
        [
            norm1_gain[None],
            norm1_shift[None],
            qv_bias,
            out_bias[None],
            norm2_gain[None],
            norm2_shift[None],
            down_bias,
            router_weight.T,
            up_bias.reshape(experts * quarter, part),
        ],
        0,
    ).astype(BF16)
    small_rows = smalls.shape[0]
    pad = -(small_rows * part) % (16 * model)
    small_block = jnp.pad(smalls.reshape(-1), (0, pad)).reshape(-1, model)
    pack = jnp.concatenate(
        [
            jnp.concatenate(
                [qkv_weight[0], qkv_weight[1], qkv_weight[2], out_weight.T], 1
            ).astype(BF16),
            small_block,
        ],
        0,
    )
    place = [lax.axis_index(name) for name in ("z", "x", "y", "c")]
    if length == 4:
        packs, below = gather_packs(pack)
        by_x = jnp.stack([packs[0][:, part:], packs[1][:, part:]]).reshape(2, 4, -1)
        pick_x = (place[1] ^ jnp.arange(2))[:, None] == jnp.arange(2)
        pick_z = (place[0] - jnp.arange(4)[:, None]) % 4 == jnp.arange(4)
        pick = pick_z[:, None, None, :] & pick_x[None, :, :, None]
        vectors = dot(pick.reshape(8, 8).astype(BF16), by_x.reshape(8, -1)).astype(BF16)
    else:
        packs = lax.all_gather(pack, EVERY, axis=0, tiled=False)
        packs = packs.reshape(quarter, dp, pack.shape[0], model)
        vectors = packs[0, :, part:].reshape(dp, -1)
        packs = [packs[:, :, :part].reshape(quarter, model, model)]
    event = []
    parts = []
    for some in packed:
        some = lax.all_to_all(tie(some, *event), PLANE, 0, 0, tiled=True)
        event = [some, packs[len(packs) // 2]]
        starts = [CHUNK * f for f, _ in spans[1:]] if parts else [0]
        stops = [CHUNK * l for _, l in spans[1:]] if parts else [head]
        base = starts[0]
        parts += [some[..., f - base : l - base] for f, l in zip(starts, stops)]
    if length != 4:
        parts = [
            one.reshape(2, quarter, 2, part, -1).transpose(2, 0, 3, 1, 4).reshape(2, 2 * part, -1)
            for one in parts
        ]

    vectors = vectors[:, : small_rows * part].reshape(dp, small_rows, part).transpose(1, 0, 2)
    lines = vectors[: 7 + 2 * experts].reshape(-1, model).astype(F32)
    bias_pairs = lines[2:4].reshape(2, quarter, width).transpose(1, 0, 2)
    bias_down = lines[7 : 7 + experts]
    router = lines[7 + experts :].astype(BF16)
    bias_up = vectors[7 + 2 * experts :].reshape(experts, quarter, dp, part)
    bias_up = bias_up.transpose(0, 2, 1, 3).reshape(experts, quarter, units)
    bias_up = lax.dynamic_index_in_dim(bias_up, expert, 0, keepdims=False).astype(F32)

    first_group = chip_y * 3
    group_tokens = GROUP_IMG * sequence
    position = (expert_ids * CAP + expert_slots).reshape(-1, group_tokens, 2)
    position_full = lax.dynamic_index_in_dim(position, first_group + 2 * core, 0, keepdims=False)
    position_half = lax.dynamic_index_in_dim(position, first_group + 1, 0, keepdims=False)
    slots_full = jnp.arange(experts * CAP, dtype=jnp.int32)
    half = CAP // 2
    slots_half = (
        jnp.arange(experts, dtype=jnp.int32)[:, None] * CAP
        + core * half
        + jnp.arange(half, dtype=jnp.int32)
    ).reshape(-1)
    match_full = slots_full[:, None, None] == position_full.T[None]
    match_half = slots_half[:, None, None] == position_half.T[None]
    hot_full = (match_full[:, 0] | match_full[:, 1]).astype(BF16)
    hot_half = (match_half[:, 0] | match_half[:, 1]).astype(BF16)
    swap = [(0, 1), (1, 0)]

    def both_groups(values):
        lent = jnp.where(core == 0, values[2], values[0])
        other = lax.ppermute(lent, "c", swap)
        full = jnp.where(core == 0, values[:2], values[1:])
        shared = jnp.where(core == 0, jnp.stack([lent, other]), jnp.stack([other, lent]))
        return (
            full.reshape(group_tokens, -1),
            shared.reshape(group_tokens, -1),
        )

    def join_rows(full, shared):
        full = full.reshape((experts, CAP) + full.shape[1:])
        shared = shared.reshape((experts, half) + shared.shape[1:])
        return jnp.concatenate([full, shared], 1)

    def lines_of(values):
        high = values.astype(BF16)
        low = (values - high.astype(F32)).astype(BF16)
        both = jnp.stack([high, low], 1)
        return jnp.pad(both, ((0, 0), (0, 14), (0, model - both.shape[2])))

    def values_of(rows):
        both = rows[:, CAP + half : CAP + half + 2, : CAP + half].astype(F32)
        return both[:, 0] + both[:, 1]

    def swap_experts(rows, *events):
        return lax.all_to_all(tie(rows, *events), PLANE, 0, 0, tiled=True)

    def dispatch(full, shared):
        return join_rows(dot(hot_full, full).astype(BF16), dot(hot_half, shared).astype(BF16))

    def combine(back):
        full = dot(hot_full, back[:, :CAP].reshape(-1, model), 0, 0)
        shared = dot(hot_half, back[:, CAP : CAP + half].reshape(-1, model), 0, 0)
        full = full.reshape(GROUP_IMG, sequence, model)
        shared = shared.reshape(GROUP_IMG, sequence, model)
        mine = jnp.where(core == 0, shared[0], shared[1])
        theirs = jnp.where(core == 0, shared[1], shared[0])
        mine = mine + lax.ppermute(theirs, "c", swap)
        return jnp.where(
            core == 0,
            jnp.concatenate([full, mine[None]]),
            jnp.concatenate([mine[None], full]),
        )

    if length == 4:
        parts[0] = tie(parts[0], *below)
    full_parts = [
        lax.all_gather(one, "z", axis=0, tiled=False)
        if length == 4
        else lax.all_gather(one, "z", axis=1, tiled=True)
        for one in parts
    ]
    grad_full, grad_shared = both_groups(out_grad)
    incoming = swap_experts(dispatch(grad_full, grad_shared), packs[-1], parts[-1])

    local_start = (chip_y * 2 + core) * piece
    mask_here = lax.dynamic_slice_in_dim(key_mask, local_start, piece, 0)[:, None]
    n1, n2, residual, q, k, v, attended, lse, wq, wk, wv, wo = attend_forward(
        jnp.stack(place).astype(jnp.int32),
        tokens_in, mask_here, lines, bias_pairs,
        packs, width,
    )
    n2 = tie(n2, incoming)
    normed_two = n2.reshape(tokens, model)

    normed_full, normed_shared = both_groups(n2)

    def chances_of(rows):
        return jax.nn.softmax(dot(rows, router, 1, 1), -1)

    probabilities = chances_of(normed_two)
    hot_ids = expert_ids[..., None] == jnp.arange(experts, dtype=jnp.int32)
    hot_here = lax.dynamic_slice_in_dim(hot_ids, local_start, piece, 0).astype(F32)
    hot_here = jnp.sum(hot_here.reshape(tokens, 2, experts), 1)
    share_here = hot_here * probabilities

    def slot_gates(match, rows, position_here):
        chance = chances_of(rows)
        hot = (position_here // CAP)[..., None] == jnp.arange(experts, dtype=jnp.int32)
        gates = jnp.sum(hot.astype(F32) * chance[:, None], -1)
        return jnp.sum(jnp.where(match, gates.T[None], 0.0), (1, 2))

    gates_sent = join_rows(
        slot_gates(match_full, normed_full, position_full),
        slot_gates(match_half, normed_shared, position_half),
    )
    chosen = swap_experts(
        jnp.concatenate([dispatch(normed_full, normed_shared), lines_of(gates_sent)], 1),
        incoming,
    )

    sums = None
    bias_parts = []
    reduced = []
    count = len(spans)
    for index, (first, last) in enumerate(spans):
        bias_one = bias_up[:, first * CHUNK : last * CHUNK].reshape(1, -1)
        final = index == count - 1
        *sums, bias_part, grads = expert_chunk(
            chosen, incoming, bias_one, sums, full_parts[index], final
        )
        bias_parts.append(bias_part.reshape(quarter, -1))
        if length == 4:
            reduced.append(lax.psum_scatter(grads, "z", scatter_dimension=0, tiled=False))
        else:
            reduced.append(lax.psum_scatter(grads, "z", scatter_dimension=1, tiled=True))

    mixed, pulled = sums
    back = swap_experts(pulled)
    gate_back = values_of(back)
    norm_two_grad = combine(back)
    mixed = swap_experts(mixed, back)

    def slots_to_tokens(match, parts_here):
        parts_here = parts_here.reshape(experts, -1)
        match = (match[:, 0] | match[:, 1]).reshape(experts, -1, group_tokens)
        return jnp.sum(jnp.where(match, parts_here[..., None], 0.0), 1).T

    prob_full = slots_to_tokens(match_full, gate_back[:, :CAP])
    prob_shared = slots_to_tokens(match_half, gate_back[:, CAP:])
    prob_full = prob_full.reshape(GROUP_IMG, sequence, experts)
    prob_shared = prob_shared.reshape(GROUP_IMG, sequence, experts)
    mine = jnp.where(core == 0, prob_shared[0], prob_shared[1])
    theirs = jnp.where(core == 0, prob_shared[1], prob_shared[0])
    mine = mine + lax.ppermute(theirs, "c", swap)
    chance_grad = jnp.where(
        core == 0,
        jnp.concatenate([prob_full, mine[None]]),
        jnp.concatenate([mine[None], prob_full]),
    ).reshape(tokens, experts)
    grad_rows = out_grad.reshape(tokens, model)
    bias_dot = dot(grad_rows, bias_down.astype(BF16), 1, 1)
    chance_grad = chance_grad + hot_here * bias_dot
    logit_grad = probabilities * (
        chance_grad - jnp.sum(probabilities * chance_grad, -1, keepdims=True)
    )
    logit_grad = logit_grad.astype(BF16)
    router_grad = dot(logit_grad, normed_two, 0, 0)
    down_bias_grad = lax.dot_general(
        share_here, grad_rows.astype(F32), (((0,), (0,)), ((), ())), precision=HIGHEST
    )

    norm_two_grad = norm_two_grad + dot(logit_grad, router).reshape(norm_two_grad.shape)
    h_grad, hb, dq, dk, dv, line_sums, pair_sums = attend_backward(
        norm_two_grad, out_grad, residual, mask_here, wo, lines, q, k, v, lse
    )
    h_grad = tie(h_grad, mixed)
    input_grad, line_ones = input_backward(h_grad, tokens_in, wq, wk, wv, lines, dq, dk, dv)
    bias_rows = jnp.concatenate(bias_parts, 1).reshape(dp, quarter, part)
    bias_rows = jnp.where(
        jnp.arange(experts)[:, None, None, None] == expert, bias_rows[None], 0.0
    )
    bias_rows = bias_rows.transpose(0, 2, 1, 3).reshape(experts * quarter, dp, part)
    line_grads = jnp.concatenate(
        [
            line_ones[:2],
            pair_sums[:, 0].reshape(1, model),
            pair_sums[:, 1].reshape(1, model),
            line_sums[:3],
            down_bias_grad,
            router_grad,
        ],
        0,
    ).reshape(-1, dp, part)
    sum_type = BF16 if length == 4 else F32
    vector_grads = jnp.concatenate([line_grads, bias_rows], 0).astype(sum_type)
    vector_grads = vector_grads.transpose(1, 0, 2).reshape(dp, small_rows * part)
    vector_grads = jnp.pad(vector_grads, ((0, 0), (0, pad))).reshape(dp, -1, model)

    if length == 4:
        pack_grads = attend_weights(n1, hb, dq, dk, dv, attended, vector_grads)
    else:
        pack_grads = attend_weights(n1, hb, dq, dk, dv, attended, None)
        pack_grads = pack_grads.reshape(quarter, dp, part, model)
        vector_grads = jnp.broadcast_to(vector_grads[None], (quarter,) + vector_grads.shape)
        pack_grads = jnp.concatenate([pack_grads, vector_grads], 2)
        pack_grads = pack_grads.reshape(quarter // 2, 2, dp // 2, 2, -1, model)
        pack_grads = pack_grads.transpose(1, 3, 0, 2, 4, 5)
    mine = lax.dynamic_index_in_dim(pack_grads, core, 0, keepdims=False)
    theirs = lax.dynamic_index_in_dim(pack_grads, 1 - core, 0, keepdims=False)
    theirs = lax.ppermute(theirs, "c", swap)
    pack_grads = (mine.astype(F32) + theirs.astype(F32)).astype(sum_type)
    pack_grads = pack_grads.reshape((-1,) + pack_grads.shape[2:])
    pack_grads = lax.all_to_all(pack_grads, ("x", "y"), 0, 0, tiled=True)
    pack_grads = jnp.sum(pack_grads.astype(F32), 0).astype(sum_type)
    if length == 4:
        pack_grad = lax.dynamic_index_in_dim(pack_grads, place[0], 0, keepdims=False).astype(F32)
        for far in (1, 2, 3):
            some = lax.dynamic_index_in_dim(pack_grads, (place[0] + far) % 4, 0, keepdims=False)
            some = lax.ppermute(some, "z", [(k, (k + far) % 4) for k in range(4)])
            pack_grad = pack_grad + some.astype(F32)
    else:
        pack_grad = lax.psum_scatter(pack_grads, "z", scatter_dimension=0, tiled=False)
    qkv_out = pack_grad[:part, : 3 * width].reshape(part, 3, width).transpose(1, 0, 2)
    out_weight_grad = pack_grad[:part, 3 * width :].T
    small_grads = pack_grad[part:].reshape(-1)[: small_rows * part].reshape(small_rows, part)

    mixture = combine(mixed)
    bias_term = jnp.dot(share_here, bias_down, precision=HIGHEST).reshape(residual.shape)
    output = (residual + mixture + bias_term).astype(BF16)

    ups, downs = [], []
    totals = reduced
    if length != 4:
        totals = [
            one.reshape(2, 2, part, quarter, -1).transpose(1, 3, 0, 2, 4).reshape(experts, 2, part, -1)
            for one in totals
        ]
    for some, event in ((totals[:1], mixed), (totals[1:2], pack_grads), (totals[2:], pack_grads)):
        if some:
            some = some[0] if len(some) == 1 else jnp.concatenate(some, -1)
            some = lax.all_to_all(tie(some.astype(BF16), event), PLANE, 0, 0, tiled=True).astype(F32)
            ups.append(some[:, 0])
            downs.append(some[:, 1])
    up_grad = jnp.concatenate(ups, -1)
    down_grad = jnp.concatenate(downs, -1).transpose(0, 2, 1)
    return (
        output,
        input_grad,
        small_grads[0],
        small_grads[1],
        qkv_out,
        small_grads[2:4],
        out_weight_grad,
        small_grads[4],
        small_grads[5],
        small_grads[6],
        small_grads[7 + experts : 7 + 2 * experts].T,
        up_grad,
        small_grads[7 + 2 * experts :].reshape(experts, -1),
        down_grad,
        small_grads[7 : 7 + experts],
    )


def solution(mesh):
    dp, tensor = mesh.devices.shape
    planes = jax.sharding.Mesh(
        mesh.devices.reshape(dp // 2, 2, tensor // 2, 2), ("z", "x", "y", "c")
    )
    rows = ("z", "x")
    images = P(("z", "x", "y", "c"), None, None)
    return jax.shard_map(
        shards,
        mesh=planes,
        in_specs=(
            images,
            P(rows, None),
            P(rows, None, None),
            P(rows, None, None),
            P(rows),
            P(rows),
            P(None, rows, TENSOR),
            P(None, rows),
            P(TENSOR, rows),
            P(rows),
            P(rows),
            P(rows),
            P(rows, None),
            P(None, rows, TENSOR),
            P(None, rows),
            P(None, TENSOR, rows),
            P(None, rows),
            images,
        ),
        out_specs=(
            images,
            images,
            P(rows),
            P(rows),
            P(None, rows, TENSOR),
            P(None, rows),
            P(TENSOR, rows),
            P(rows),
            P(rows),
            P(rows),
            P(rows, None),
            P(None, rows, TENSOR),
            P(None, rows),
            P(None, TENSOR, rows),
            P(None, rows),
        ),
        check_vma=False,
    )
```

```python
import functools
import jax
import jax.numpy as jnp
from jax import lax
from jax.experimental import pallas as pl
from jax.experimental.pallas import tpu as pltpu
from jax.sharding import PartitionSpec as P

HD = 64
EPSILON = 1e-06
NEGATIVE = -1e30
F32 = jnp.float32
BF16 = jnp.bfloat16


def dot(left, right, left_dim=1, right_dim=0):
    return lax.dot_general(
        left, right, (((left_dim,), (right_dim,)), ((), ())), preferred_element_type=F32
    )


def norm_forward(values, gains, shifts):
    middle = jnp.mean(values, -1, keepdims=True)
    centred = values - middle
    inverse = lax.rsqrt(jnp.mean(centred * centred, -1, keepdims=True) + EPSILON)
    unit_rows = centred * inverse
    return (unit_rows * gains + shifts, unit_rows, inverse)


def norm_backward(grad_rows, unit_rows, inverse, gains):
    scaled = grad_rows * gains
    return inverse * (
        scaled
        - jnp.mean(scaled, -1, keepdims=True)
        - unit_rows * jnp.mean(scaled * unit_rows, -1, keepdims=True)
    )


def head_masks(width):
    lane = lax.broadcasted_iota(jnp.int32, (1, width), 1)
    return [(lane // HD == k) for k in range(width // HD)]


def arrange(w_ref, *parts):
    width = parts[0].shape[2]
    for t in range(w_ref.shape[0]):
        packed = w_ref[t]
        for k, ref in enumerate(parts):
            ref[t] = packed[:, k * width : (k + 1) * width]


def put_rows(ref, values):
    rows, columns = values.shape
    spare = jnp.zeros((ref.shape[0] - rows, columns), values.dtype)
    ref[...] = jnp.concatenate([values, spare], 0).astype(ref.dtype)


def attend_forward_kernel(
    place_ref, tokens_ref, mask_ref, lines_ref, bias_ref, *refs,
):
    (
        n1_ref, n2_ref, h_ref, q_ref, k_ref, v_ref, o_ref, lse_ref,
        wq_ref, wk_ref, wv_ref, wo_ref, all_ref, sem,
    ) = refs[-14:]
    packs = refs[:-14]

    @pl.when(pl.program_id(0) == 0)
    def _():
        if len(packs) == 1:
            pltpu.make_async_copy(packs[0], all_ref, sem).start()
        else:
            z, x, y, c = [place_ref[k] for k in range(4)]
            part = all_ref.shape[1] // 8
            for index, ref in enumerate(packs):
                dx, dy, dc = index & 1, (index >> 1) & 1, index >> 2
                t = (y ^ dy) * 2 + (c ^ dc)
                for back in range(4):
                    row = (((z - back) & 3) * 2 + (x ^ dx)) * part
                    pltpu.make_async_copy(
                        ref.at[back, pl.ds(0, part)],
                        all_ref.at[t, pl.ds(pl.multiple_of(row, 32), part)],
                        sem,
                    ).start()
        pltpu.make_async_copy(all_ref, all_ref, sem).wait()
        arrange(all_ref, wq_ref, wk_ref, wv_ref, wo_ref)

    x = tokens_ref[0].astype(F32)
    n1, _, _ = norm_forward(x, lines_ref[0:1, :], lines_ref[1:2, :])
    put_rows(n1_ref.at[0], n1)
    n1 = n1.astype(BF16)
    width = wq_ref.shape[2]
    masks = head_masks(width)
    keys = mask_ref[0] > 0
    total = x + lines_ref[4:5, :]
    for t in range(wq_ref.shape[0]):
        q = (dot(n1, wq_ref[t]) + bias_ref[t, 0:1, :]).astype(BF16)
        k = dot(n1, wk_ref[t]).astype(BF16)
        v = (dot(n1, wv_ref[t]) + bias_ref[t, 1:2, :]).astype(BF16)
        q_ref[0, t] = q
        k_ref[0, t] = k
        v_ref[0, t] = v
        scaled = q * jnp.asarray(HD ** (-0.5), BF16)
        o = jnp.zeros(q.shape, F32)
        for h, here in enumerate(masks):
            s = dot(jnp.where(here, scaled, jnp.zeros_like(scaled)), k, 1, 1)
            s = jnp.where(keys, s, NEGATIVE)
            largest = jnp.max(s, -1, keepdims=True)
            e = jnp.exp(s - largest)
            total_e = jnp.sum(e, -1, keepdims=True)
            p = (e / total_e).astype(BF16)
            o = jnp.where(here, dot(p, v), o)
            index = t * len(masks) + h
            lse_ref[0, :, index : index + 1] = largest + jnp.log(total_e)
        put_rows(o_ref.at[0, t], o)
        total = total + dot(o.astype(BF16), wo_ref[t], 1, 1)
    h_ref[0] = total
    n2, _, _ = norm_forward(total, lines_ref[5:6, :], lines_ref[6:7, :])
    n2_ref[0] = n2.astype(BF16)


def whole(shape):
    return pl.BlockSpec(shape, lambda b: (0,) * len(shape))


def by_image(shape):
    return pl.BlockSpec((1,) + shape[1:], lambda b: (b,) + (0,) * (len(shape) - 1))


def padded(rows):
    return -(-rows // 16) * 16


def attend_forward(place, tokens_in, mask, lines, bias_pairs, packs, width):
    images, sequence, model = tokens_in.shape
    quarter = model // width
    rows = (images, sequence, model)
    heads = (images, quarter, sequence, width)
    columns = (quarter, model, width)
    outs = [
        ((images, padded(sequence), model), BF16), (rows, BF16), (rows, F32), (heads, BF16), (heads, BF16),
        (heads, BF16), ((images, quarter, padded(sequence), width), BF16), ((images, sequence, 128), F32),
        (columns, BF16), (columns, BF16), (columns, BF16), (columns, BF16),
    ]
    place_spec = lambda spec: pl.BlockSpec(spec.block_shape, lambda b, p: spec.index_map(b))
    in_specs = [by_image(tokens_in.shape), by_image(mask.shape), whole(lines.shape), whole(bias_pairs.shape)]
    out_specs = [by_image(s) for s, _ in outs[:8]] + [whole(s) for s, _ in outs[8:]]
    return pl.pallas_call(
        attend_forward_kernel,
        grid_spec=pltpu.PrefetchScalarGridSpec(
            num_scalar_prefetch=1,
            grid=(images,),
            in_specs=[place_spec(s) for s in in_specs]
            + [pl.BlockSpec(memory_space=pl.ANY)] * len(packs),
            out_specs=[place_spec(s) for s in out_specs],
            scratch_shapes=[pltpu.VMEM((quarter, model, 4 * width), BF16), pltpu.SemaphoreType.DMA(())],
        ),
        out_shape=[jax.ShapeDtypeStruct(s, d) for s, d in outs],
        compiler_params=pltpu.CompilerParams(vmem_limit_bytes=56 * 2**20),
        cost_estimate=pl.CostEstimate(flops=2 * 10**9, bytes_accessed=4 * 10**6, transcendentals=0),
        name="attend_forward",
    )(place, tokens_in, mask, lines, bias_pairs, *packs)


def attend_backward_kernel(
    n2_grad_ref, grad_ref, h_ref, mask_ref, wo_ref, lines_ref, q_ref, k_ref, v_ref, lse_ref,
    h_grad_ref, hb_ref, dq_ref, dk_ref, dv_ref, vec_ref, pair_ref,
):
    @pl.when(pl.program_id(0) == 0)
    def _():
        vec_ref[...] = jnp.zeros_like(vec_ref)
        pair_ref[...] = jnp.zeros_like(pair_ref)

    n2_grad = n2_grad_ref[0]
    _, unit_two, inverse_two = norm_forward(h_ref[0], lines_ref[5:6, :], lines_ref[6:7, :])
    vec_ref[1:2, :] += jnp.sum(n2_grad * unit_two, 0, keepdims=True)
    vec_ref[2:3, :] += jnp.sum(n2_grad, 0, keepdims=True)
    h_grad = grad_ref[0].astype(F32) + norm_backward(
        n2_grad, unit_two, inverse_two, lines_ref[5:6, :]
    )
    vec_ref[0:1, :] += jnp.sum(h_grad, 0, keepdims=True)
    h_grad_ref[0] = h_grad
    put_rows(hb_ref.at[0], h_grad)
    hb = h_grad.astype(BF16)
    width = wo_ref.shape[2]
    masks = head_masks(width)
    keys = mask_ref[0] > 0
    scale = HD ** (-0.5)
    for t in range(wo_ref.shape[0]):
        do = dot(hb, wo_ref[t]).astype(BF16)
        q, k, v = q_ref[0, t], k_ref[0, t], v_ref[0, t]
        zero = jnp.zeros_like(q)
        scaled = q * jnp.asarray(scale, BF16)
        dq = jnp.zeros(q.shape, F32)
        dk = jnp.zeros(q.shape, F32)
        dv = jnp.zeros(q.shape, F32)
        for h, here in enumerate(masks):
            index = t * len(masks) + h
            s = dot(jnp.where(here, scaled, zero), k, 1, 1)
            s = jnp.where(keys, s, NEGATIVE)
            p = jnp.exp(s - lse_ref[0, :, index : index + 1])
            dp = dot(jnp.where(here, do, zero), v, 1, 1)
            ds = p * (dp - jnp.sum(p * dp, -1, keepdims=True))
            ds = ds.astype(BF16)
            dv = jnp.where(here, dot(p.astype(BF16), do, 0, 0), dv)
            dq = jnp.where(here, dot(ds, k), dq)
            dk = jnp.where(here, dot(ds, q, 0, 0), dk)
        dq = (dq * scale).astype(BF16).astype(F32)
        dv = dv.astype(BF16).astype(F32)
        pair_ref[t, 0:1, :] += jnp.sum(dq, 0, keepdims=True)
        pair_ref[t, 1:2, :] += jnp.sum(dv, 0, keepdims=True)
        put_rows(dq_ref.at[0, t], dq)
        put_rows(dk_ref.at[0, t], dk * scale)
        put_rows(dv_ref.at[0, t], dv)


def attend_backward(n2_grad, out_grad, h, mask, wo, lines, q, k, v, lse):
    ins = (n2_grad, out_grad, h, mask, wo, lines, q, k, v, lse)
    shared = {4, 5}
    images, sequence, model = n2_grad.shape
    quarter, _, width = wo.shape
    heads = ((images, quarter, padded(sequence), width), BF16)
    outs = [
        (n2_grad.shape, F32), ((images, padded(sequence), model), BF16), heads, heads, heads,
        ((8, model), F32), ((quarter, 8, width), F32),
    ]
    return pl.pallas_call(
        attend_backward_kernel,
        grid=(images,),
        in_specs=[whole(a.shape) if i in shared else by_image(a.shape) for i, a in enumerate(ins)],
        out_specs=[by_image(s) for s, _ in outs[:5]] + [whole(s) for s, _ in outs[5:]],
        out_shape=[jax.ShapeDtypeStruct(s, d) for s, d in outs],
        compiler_params=pltpu.CompilerParams(vmem_limit_bytes=56 * 2**20),
        cost_estimate=pl.CostEstimate(flops=0, bytes_accessed=0, transcendentals=0),
        name="attend_backward",
    )(*ins)


def attend_weights_kernel(n1_ref, hb_ref, dq_ref, dk_ref, dv_ref, o_ref, *refs):
    out_ref = refs[-1]
    width = dq_ref.shape[3]
    n1 = n1_ref[...].reshape(-1, n1_ref.shape[2])
    hb = hb_ref[...].reshape(-1, n1_ref.shape[2])
    for k, (left, ref) in enumerate(((n1, dq_ref), (n1, dk_ref), (n1, dv_ref), (hb, o_ref))):
        sums = dot(left, ref[...].reshape(-1, width), 0, 0).astype(out_ref.dtype)
        columns = slice(k * width, (k + 1) * width)
        if len(refs) == 1:
            out_ref[0, :, columns] = sums
            continue
        part = sums.shape[0] // 8
        for z in range(4):
            for x in range(2):
                start = (z * 2 + x) * part
                out_ref[0, x, 0, z, :part, columns] = sums[start : start + part]
    if len(refs) == 2:
        for z in range(4):
            for x in range(2):
                out_ref[0, x, 0, z, part:, :] = refs[0][z * 2 + x]


def attend_weights(n1, hb, dq, dk, dv, o, extra):
    images, quarter, rows, width = dq.shape
    model = n1.shape[2]
    heads = pl.BlockSpec((images, 1, rows, width), lambda t: (0, t, 0, 0))
    if extra is None:
        out_spec = pl.BlockSpec((1, model, 4 * width), lambda t: (t, 0, 0))
        out_shape = jax.ShapeDtypeStruct((quarter, model, 4 * width), F32)
    else:
        depth = model // 8 + extra.shape[1]
        out_spec = pl.BlockSpec(
            (1, 2, 1, 4, depth, model), lambda t: (t % 2, 0, t // 2, 0, 0, 0)
        )
        out_shape = jax.ShapeDtypeStruct((2, 2, 2, 4, depth, model), BF16)
    extras = [] if extra is None else [extra]
    return pl.pallas_call(
        attend_weights_kernel,
        grid=(quarter,),
        in_specs=[whole(n1.shape), whole(hb.shape)] + [heads] * 4 + [whole(e.shape) for e in extras],
        out_specs=out_spec,
        out_shape=out_shape,
        compiler_params=pltpu.CompilerParams(vmem_limit_bytes=56 * 2**20),
        cost_estimate=pl.CostEstimate(flops=0, bytes_accessed=0, transcendentals=0),
        name="attend_weights",
    )(n1, hb, dq, dk, dv, o, *extras)


def input_backward_kernel(
    h_grad_ref, tokens_ref, wq_ref, wk_ref, wv_ref, lines_ref, dq_ref, dk_ref, dv_ref,
    input_grad_ref, vec_ref,
):
    @pl.when(pl.program_id(0) == 0)
    def _():
        vec_ref[...] = jnp.zeros_like(vec_ref)

    rows = tokens_ref.shape[1]
    n1_grad = jnp.zeros((dq_ref.shape[2], tokens_ref.shape[2]), F32)
    for t in range(wq_ref.shape[0]):
        for grads, weights in ((dq_ref, wq_ref), (dk_ref, wk_ref), (dv_ref, wv_ref)):
            n1_grad += dot(grads[0, t], weights[t], 1, 1)
    n1_grad = n1_grad[:rows]
    _, unit_one, inverse_one = norm_forward(
        tokens_ref[0].astype(F32), lines_ref[0:1, :], lines_ref[1:2, :]
    )
    vec_ref[0:1, :] += jnp.sum(n1_grad * unit_one, 0, keepdims=True)
    vec_ref[1:2, :] += jnp.sum(n1_grad, 0, keepdims=True)
    input_grad_ref[0] = h_grad_ref[0] + norm_backward(
        n1_grad, unit_one, inverse_one, lines_ref[0:1, :]
    )


def input_backward(h_grad, tokens_in, wq, wk, wv, lines, dq, dk, dv):
    ins = (h_grad, tokens_in, wq, wk, wv, lines, dq, dk, dv)
    outs = [(h_grad.shape, F32), ((8, wq.shape[1]), F32)]
    return pl.pallas_call(
        input_backward_kernel,
        grid=(h_grad.shape[0],),
        in_specs=[whole(a.shape) if 2 <= i <= 5 else by_image(a.shape) for i, a in enumerate(ins)],
        out_specs=[by_image(outs[0][0]), whole(outs[1][0])],
        out_shape=[jax.ShapeDtypeStruct(s, d) for s, d in outs],
        compiler_params=pltpu.CompilerParams(vmem_limit_bytes=56 * 2**20),
        cost_estimate=pl.CostEstimate(flops=0, bytes_accessed=0, transcendentals=0),
        name="input_backward",
    )(*ins)


def pack_experts_kernel(up_ref, down_ref, *refs):
    up = up_ref[0].astype(BF16)
    down = down_ref[0].astype(BF16)
    start = 0
    for ref in refs:
        stop = start + ref.shape[3]
        ref[0, 0] = up[:, start:stop]
        ref[0, 1] = down[:, start:stop]
        start = stop


def pack_experts(up, down, sizes):
    experts, part, units = up.shape
    outs = [(experts, 2, part, size) for size in sizes]
    return pl.pallas_call(
        pack_experts_kernel,
        grid=(experts,),
        in_specs=[by_image(up.shape), by_image(down.shape)],
        out_specs=[by_image(s) for s in outs],
        out_shape=[jax.ShapeDtypeStruct(s, BF16) for s in outs],
        compiler_params=pltpu.CompilerParams(vmem_limit_bytes=32 * 2**20),
        cost_estimate=pl.CostEstimate(flops=0, bytes_accessed=8 * 10**6, transcendentals=0),
        name="pack_experts",
    )(up, down)


def to_column(line):
    return jnp.broadcast_to(line, (128, 256)).T[:, :1]


def to_line(column):
    return jnp.broadcast_to(column, (256, 128)).T[:1, :]


def expert_kernel(first, last, x_ref, g_ref, b_ref, shards_ref, *refs):
    if not first:
        (y_in, p_in), refs = refs[:2], refs[2:]
    (y_out, p_out, bias_ref), refs = refs[:3], refs[3:]
    acc_ref, w_ref, sem = refs[-3:]
    grads_ref = refs[0]
    step = pl.program_id(0)
    model = w_ref.shape[1]

    @pl.when(step == 0)
    def _():
        if len(shards_ref.shape) == 3:
            pltpu.make_async_copy(shards_ref, w_ref, sem).start()
        else:
            part, units = shards_ref.shape[3:]
            for z in range(4):
                for p in range(8):
                    row = (z * 2 + p // 4) * part
                    pltpu.make_async_copy(
                        shards_ref.at[z, p],
                        w_ref.at[:, pl.ds(row, part), pl.ds((p % 4) * units, units)],
                        sem,
                    ).start()
        acc_ref[...] = jnp.zeros_like(acc_ref)
        bias_ref[...] = jnp.zeros_like(bias_ref)
        pltpu.make_async_copy(w_ref, w_ref, sem).wait()

    sources, slots, _ = g_ref.shape
    x = x_ref[:, :slots].reshape(-1, model)
    g_raw = g_ref[...].reshape(-1, model)
    gates = []
    for k in range(sources):
        parts = x_ref[k, slots : slots + 16, :256].astype(F32)
        gates.append(to_column(parts[0:1] + parts[1:2])[:slots])
    gate = jnp.concatenate(gates, 0)
    g = (g_raw.astype(F32) * gate).astype(BF16)
    hidden = dot(x, w_ref[0]) + b_ref[...]
    cdf = 0.5 * (1.0 + lax.erf(hidden * (0.5 ** 0.5)))
    active = (hidden * cdf).astype(BF16)
    slope = cdf + hidden * (jnp.exp(-0.5 * hidden * hidden) * 0.3989422804014327)
    hidden_grad = (dot(g, w_ref[1]) * slope).astype(BF16)
    y = dot(active, w_ref[1], 1, 1)
    p = dot(hidden_grad, w_ref[0], 1, 1)
    if not first:
        y = y_in[...].reshape(-1, model) + y
        p = p_in[...].reshape(-1, model) + p
    if not last:
        y_out[...] = y.reshape(sources, slots, model)
        p_out[...] = p.reshape(sources, slots, model)
    else:
        y_out[...] = (y * gate).astype(BF16).reshape(sources, slots, model)
        p_out[:, :slots] = p.astype(BF16).reshape(sources, slots, model)
        gate_grad = jnp.sum(g_raw.astype(F32) * y, -1, keepdims=True)
        for k in range(sources):
            own = gate_grad[k * slots : (k + 1) * slots]
            line = to_line(jnp.concatenate([own, jnp.zeros((256 - slots, 1), F32)], 0))
            high = line.astype(BF16)
            low = (line - high.astype(F32)).astype(BF16)
            block = jnp.concatenate([high, low, jnp.zeros((14, 256), BF16)], 0)
            p_out[k, slots:] = jnp.concatenate([block, jnp.zeros((16, model - 256), BF16)], 1)
    bias_ref[...] += jnp.sum(hidden_grad.astype(F32), 0, keepdims=True)
    acc_ref[0] += dot(x, hidden_grad, 0, 0)
    acc_ref[1] += dot(g, active, 0, 0)

    @pl.when(step == pl.num_programs(0) - 1)
    def _():
        if len(shards_ref.shape) == 3:
            grads_ref[...] = acc_ref[...]
        else:
            part, units = shards_ref.shape[3:]
            for z in range(4):
                for q in range(8):
                    row = (z * 2 + q // 4) * part
                    columns = slice((q % 4) * units, (q % 4 + 1) * units)
                    grads_ref[z, q] = acc_ref[:, row : row + part, columns].astype(BF16)


def expert_chunk(x, g, b, sums, shards, last):
    experts, slots, model = g.shape
    units = b.shape[1]
    first = sums is None
    step = 2
    block = lambda rows: pl.BlockSpec((step, rows, model), lambda i: (i, 0, 0))
    full = whole
    ins = [x, g, b, shards] + ([] if first else list(sums))
    in_specs = [block(x.shape[1]), block(slots), full(b.shape)]
    in_specs.append(pl.BlockSpec(memory_space=pl.ANY))
    in_specs += [] if first else [block(slots)] * 2
    rows = (experts, slots, model)
    if last:
        outs = [(rows, BF16), (x.shape, BF16)]
    else:
        outs = [(rows, F32), (rows, F32)]
    out_specs = [block(s[1]) for s, _ in outs]
    outs.append((b.shape, F32))
    if len(shards.shape) == 3:
        outs.append(((2, model, units), F32))
    else:
        outs.append((shards.shape, BF16))
    out_specs += [full(s) for s, _ in outs[2:]]
    base = 4
    return pl.pallas_call(
        functools.partial(expert_kernel, first, last),
        grid=(experts // step,),
        in_specs=in_specs,
        out_specs=out_specs,
        scratch_shapes=[
            pltpu.VMEM((2, model, units), F32),
            pltpu.VMEM((2, model, units), BF16),
            pltpu.SemaphoreType.DMA(()),
        ],
        out_shape=[jax.ShapeDtypeStruct(s, d) for s, d in outs],
        input_output_aliases={} if first or last else {base: 0, base + 1: 1},
        compiler_params=pltpu.CompilerParams(vmem_limit_bytes=58 * 2**20),
        cost_estimate=pl.CostEstimate(
            flops=2 * experts * slots * model * units, bytes_accessed=4 * 10**6, transcendentals=0
        ),
        name="expert_chunk",
    )(*ins)


CAP = 128
GROUP_IMG = 2
CHUNK = 128
HIGHEST = lax.Precision.HIGHEST
TENSOR = ("y", "c")
PLANE = ("x", "y", "c")
EVERY = ("y", "c", "z", "x")


def tie(values, *events):
    events = [e for e in events if e is not None]
    if not events:
        return values
    return lax.optimization_barrier((values, *events))[0]


def gather_packs(pack):
    below = [pack] + [
        lax.ppermute(pack, "z", [(k, (k + far) % 4) for k in range(4)]) for far in (1, 2, 3)
    ]
    column = jnp.stack(below)
    swap = [(0, 1), (1, 0)]
    over_x = lax.ppermute(column, "x", swap)
    over_y = lax.ppermute(column, "y", swap)
    over_both = lax.ppermute(column, ("x", "y"), [(0, 3), (1, 2), (2, 1), (3, 0)])
    four = [column, over_x, over_y, over_both]
    return four + [lax.ppermute(each, "c", swap) for each in four], below[1:]


def shards(
    tokens_in,
    key_mask,
    expert_ids,
    expert_slots,
    norm1_gain,
    norm1_shift,
    qkv_weight,
    qv_bias,
    out_weight,
    out_bias,
    norm2_gain,
    norm2_shift,
    router_weight,
    up_weight,
    up_bias,
    down_weight,
    down_bias,
    out_grad,
):
    length = lax.axis_size("z")
    core = lax.axis_index("c")
    chip_y = lax.axis_index("y")
    quarter = lax.axis_size("y") * 2
    expert = (lax.axis_index("x") * lax.axis_size("y") + chip_y) * 2 + core
    piece, sequence, model = tokens_in.shape
    experts, part, units = up_weight.shape
    dp = model // part
    width = qkv_weight.shape[2]
    tokens = piece * sequence
    blocks = units // CHUNK
    spans = [(0, 4), (4, 6)] if blocks == 6 else [(0, blocks)]

    head = spans[0][1] * CHUNK
    sizes = [head, units - head] if units > head else [head]
    packed = pack_experts(up_weight, down_weight.transpose(0, 2, 1), sizes)
    qkv_weight, norm1_gain = tie((qkv_weight, norm1_gain), packed[0])

    smalls = jnp.concatenate(
        [
            norm1_gain[None],
            norm1_shift[None],
            qv_bias,
            out_bias[None],
            norm2_gain[None],
            norm2_shift[None],
            down_bias,
            router_weight.T,
            up_bias.reshape(experts * quarter, part),
        ],
        0,
    ).astype(BF16)
    small_rows = smalls.shape[0]
    pad = -(small_rows * part) % (16 * model)
    small_block = jnp.pad(smalls.reshape(-1), (0, pad)).reshape(-1, model)
    pack = jnp.concatenate(
        [
            jnp.concatenate(
                [qkv_weight[0], qkv_weight[1], qkv_weight[2], out_weight.T], 1
            ).astype(BF16),
            small_block,
        ],
        0,
    )
    place = [lax.axis_index(name) for name in ("z", "x", "y", "c")]
    if length == 4:
        packs, below = gather_packs(pack)
        by_x = jnp.stack([packs[0][:, part:], packs[1][:, part:]]).reshape(2, 4, -1)
        pick_x = (place[1] ^ jnp.arange(2))[:, None] == jnp.arange(2)
        pick_z = (place[0] - jnp.arange(4)[:, None]) % 4 == jnp.arange(4)
        pick = pick_z[:, None, None, :] & pick_x[None, :, :, None]
        vectors = dot(pick.reshape(8, 8).astype(BF16), by_x.reshape(8, -1)).astype(BF16)
    else:
        packs = lax.all_gather(pack, EVERY, axis=0, tiled=False)
        packs = packs.reshape(quarter, dp, pack.shape[0], model)
        vectors = packs[0, :, part:].reshape(dp, -1)
        packs = [packs[:, :, :part].reshape(quarter, model, model)]
    event = []
    parts = []
    for some in packed:
        some = lax.all_to_all(tie(some, *event), PLANE, 0, 0, tiled=True)
        event = [some, packs[len(packs) // 2]]
        starts = [CHUNK * f for f, _ in spans[1:]] if parts else [0]
        stops = [CHUNK * l for _, l in spans[1:]] if parts else [head]
        base = starts[0]
        parts += [some[..., f - base : l - base] for f, l in zip(starts, stops)]
    if length != 4:
        parts = [
            one.reshape(2, quarter, 2, part, -1).transpose(2, 0, 3, 1, 4).reshape(2, 2 * part, -1)
            for one in parts
        ]

    vectors = vectors[:, : small_rows * part].reshape(dp, small_rows, part).transpose(1, 0, 2)
    lines = vectors[: 7 + 2 * experts].reshape(-1, model).astype(F32)
    bias_pairs = lines[2:4].reshape(2, quarter, width).transpose(1, 0, 2)
    bias_down = lines[7 : 7 + experts]
    router = lines[7 + experts :].astype(BF16)
    bias_up = vectors[7 + 2 * experts :].reshape(experts, quarter, dp, part)
    bias_up = bias_up.transpose(0, 2, 1, 3).reshape(experts, quarter, units)
    bias_up = lax.dynamic_index_in_dim(bias_up, expert, 0, keepdims=False).astype(F32)

    first_group = chip_y * 3
    group_tokens = GROUP_IMG * sequence
    position = (expert_ids * CAP + expert_slots).reshape(-1, group_tokens, 2)
    position_full = lax.dynamic_index_in_dim(position, first_group + 2 * core, 0, keepdims=False)
    position_half = lax.dynamic_index_in_dim(position, first_group + 1, 0, keepdims=False)
    slots_full = jnp.arange(experts * CAP, dtype=jnp.int32)
    half = CAP // 2
    slots_half = (
        jnp.arange(experts, dtype=jnp.int32)[:, None] * CAP
        + core * half
        + jnp.arange(half, dtype=jnp.int32)
    ).reshape(-1)
    match_full = slots_full[:, None, None] == position_full.T[None]
    match_half = slots_half[:, None, None] == position_half.T[None]
    hot_full = (match_full[:, 0] | match_full[:, 1]).astype(BF16)
    hot_half = (match_half[:, 0] | match_half[:, 1]).astype(BF16)
    swap = [(0, 1), (1, 0)]

    def both_groups(values):
        lent = jnp.where(core == 0, values[2], values[0])
        other = lax.ppermute(lent, "c", swap)
        full = jnp.where(core == 0, values[:2], values[1:])
        shared = jnp.where(core == 0, jnp.stack([lent, other]), jnp.stack([other, lent]))
        return (
            full.reshape(group_tokens, -1),
            shared.reshape(group_tokens, -1),
        )

    def join_rows(full, shared):
        full = full.reshape((experts, CAP) + full.shape[1:])
        shared = shared.reshape((experts, half) + shared.shape[1:])
        return jnp.concatenate([full, shared], 1)

    def lines_of(values):
        high = values.astype(BF16)
        low = (values - high.astype(F32)).astype(BF16)
        both = jnp.stack([high, low], 1)
        return jnp.pad(both, ((0, 0), (0, 14), (0, model - both.shape[2])))

    def values_of(rows):
        both = rows[:, CAP + half : CAP + half + 2, : CAP + half].astype(F32)
        return both[:, 0] + both[:, 1]

    def swap_experts(rows, *events):
        return lax.all_to_all(tie(rows, *events), PLANE, 0, 0, tiled=True)

    def dispatch(full, shared):
        return join_rows(dot(hot_full, full).astype(BF16), dot(hot_half, shared).astype(BF16))

    def combine(back):
        full = dot(hot_full, back[:, :CAP].reshape(-1, model), 0, 0)
        shared = dot(hot_half, back[:, CAP : CAP + half].reshape(-1, model), 0, 0)
        full = full.reshape(GROUP_IMG, sequence, model)
        shared = shared.reshape(GROUP_IMG, sequence, model)
        mine = jnp.where(core == 0, shared[0], shared[1])
        theirs = jnp.where(core == 0, shared[1], shared[0])
        mine = mine + lax.ppermute(theirs, "c", swap)
        return jnp.where(
            core == 0,
            jnp.concatenate([full, mine[None]]),
            jnp.concatenate([mine[None], full]),
        )

    if length == 4:
        parts[0] = tie(parts[0], *below)
    full_parts = [
        lax.all_gather(one, "z", axis=0, tiled=False)
        if length == 4
        else lax.all_gather(one, "z", axis=1, tiled=True)
        for one in parts
    ]
    grad_full, grad_shared = both_groups(out_grad)
    incoming = swap_experts(dispatch(grad_full, grad_shared), packs[-1], parts[-1])

    local_start = (chip_y * 2 + core) * piece
    mask_here = lax.dynamic_slice_in_dim(key_mask, local_start, piece, 0)[:, None]
    n1, n2, residual, q, k, v, attended, lse, wq, wk, wv, wo = attend_forward(
        jnp.stack(place).astype(jnp.int32),
        tokens_in, mask_here, lines, bias_pairs,
        packs, width,
    )
    n2 = tie(n2, incoming)
    normed_two = n2.reshape(tokens, model)

    normed_full, normed_shared = both_groups(n2)

    def chances_of(rows):
        return jax.nn.softmax(dot(rows, router, 1, 1), -1)

    probabilities = chances_of(normed_two)
    hot_ids = expert_ids[..., None] == jnp.arange(experts, dtype=jnp.int32)
    hot_here = lax.dynamic_slice_in_dim(hot_ids, local_start, piece, 0).astype(F32)
    hot_here = jnp.sum(hot_here.reshape(tokens, 2, experts), 1)
    share_here = hot_here * probabilities

    def slot_gates(match, rows, position_here):
        chance = chances_of(rows)
        hot = (position_here // CAP)[..., None] == jnp.arange(experts, dtype=jnp.int32)
        gates = jnp.sum(hot.astype(F32) * chance[:, None], -1)
        return jnp.sum(jnp.where(match, gates.T[None], 0.0), (1, 2))

    gates_sent = join_rows(
        slot_gates(match_full, normed_full, position_full),
        slot_gates(match_half, normed_shared, position_half),
    )
    chosen = swap_experts(
        jnp.concatenate([dispatch(normed_full, normed_shared), lines_of(gates_sent)], 1),
        incoming,
    )

    sums = None
    bias_parts = []
    reduced = []
    count = len(spans)
    for index, (first, last) in enumerate(spans):
        bias_one = bias_up[:, first * CHUNK : last * CHUNK].reshape(1, -1)
        final = index == count - 1
        *sums, bias_part, grads = expert_chunk(
            chosen, incoming, bias_one, sums, full_parts[index], final
        )
        bias_parts.append(bias_part.reshape(quarter, -1))
        if length == 4:
            reduced.append(lax.psum_scatter(grads, "z", scatter_dimension=0, tiled=False))
        else:
            reduced.append(lax.psum_scatter(grads, "z", scatter_dimension=1, tiled=True))

    mixed, pulled = sums
    back = swap_experts(pulled)
    gate_back = values_of(back)
    norm_two_grad = combine(back)

    def send_back(some, *events):
        if not some:
            return None
        some = some[0].astype(BF16)
        if length != 4:
            some = some.reshape(2, 2, part, quarter, -1).transpose(1, 3, 0, 2, 4)
            some = some.reshape(experts, 2, part, -1)
        return swap_experts(some, *events)

    mixed = swap_experts(mixed, back)

    def slots_to_tokens(match, parts_here):
        parts_here = parts_here.reshape(experts, -1)
        match = (match[:, 0] | match[:, 1]).reshape(experts, -1, group_tokens)
        return jnp.sum(jnp.where(match, parts_here[..., None], 0.0), 1).T

    prob_full = slots_to_tokens(match_full, gate_back[:, :CAP])
    prob_shared = slots_to_tokens(match_half, gate_back[:, CAP:])
    prob_full = prob_full.reshape(GROUP_IMG, sequence, experts)
    prob_shared = prob_shared.reshape(GROUP_IMG, sequence, experts)
    mine = jnp.where(core == 0, prob_shared[0], prob_shared[1])
    theirs = jnp.where(core == 0, prob_shared[1], prob_shared[0])
    mine = mine + lax.ppermute(theirs, "c", swap)
    chance_grad = jnp.where(
        core == 0,
        jnp.concatenate([prob_full, mine[None]]),
        jnp.concatenate([mine[None], prob_full]),
    ).reshape(tokens, experts)
    grad_rows = out_grad.reshape(tokens, model)
    bias_dot = dot(grad_rows, bias_down.astype(BF16), 1, 1)
    chance_grad = chance_grad + hot_here * bias_dot
    logit_grad = probabilities * (
        chance_grad - jnp.sum(probabilities * chance_grad, -1, keepdims=True)
    )
    logit_grad = logit_grad.astype(BF16)
    router_grad = dot(logit_grad, normed_two, 0, 0)
    down_bias_grad = lax.dot_general(
        share_here, grad_rows.astype(F32), (((0,), (0,)), ((), ())), precision=HIGHEST
    )

    norm_two_grad = norm_two_grad + dot(logit_grad, router).reshape(norm_two_grad.shape)
    h_grad, hb, dq, dk, dv, line_sums, pair_sums = attend_backward(
        norm_two_grad, out_grad, residual, mask_here, wo, lines, q, k, v, lse
    )
    bias_rows = jnp.concatenate(bias_parts, 1).reshape(dp, quarter, part)
    bias_rows = jnp.where(
        jnp.arange(experts)[:, None, None, None] == expert, bias_rows[None], 0.0
    )
    bias_rows = bias_rows.transpose(0, 2, 1, 3).reshape(experts * quarter, dp, part)
    line_grads = jnp.concatenate(
        [
            jnp.zeros((2, model), F32),
            pair_sums[:, 0].reshape(1, model),
            pair_sums[:, 1].reshape(1, model),
            line_sums[:3],
            down_bias_grad,
            router_grad,
        ],
        0,
    ).reshape(-1, dp, part)
    sum_type = BF16 if length == 4 else F32
    vector_grads = jnp.concatenate([line_grads, bias_rows], 0).astype(sum_type)
    vector_grads = vector_grads.transpose(1, 0, 2).reshape(dp, small_rows * part)
    vector_grads = jnp.pad(vector_grads, ((0, 0), (0, pad))).reshape(dp, -1, model)

    hb = tie(hb, mixed)
    if length == 4:
        pack_grads = attend_weights(n1, hb, dq, dk, dv, attended, vector_grads)
    else:
        pack_grads = attend_weights(n1, hb, dq, dk, dv, attended, None)
        pack_grads = pack_grads.reshape(quarter, dp, part, model)
        vector_grads = jnp.broadcast_to(vector_grads[None], (quarter,) + vector_grads.shape)
        pack_grads = jnp.concatenate([pack_grads, vector_grads], 2)
        pack_grads = pack_grads.reshape(quarter // 2, 2, dp // 2, 2, -1, model)
        pack_grads = pack_grads.transpose(1, 3, 0, 2, 4, 5)
    h_grad = tie(h_grad, pack_grads)
    input_grad, line_ones = input_backward(h_grad, tokens_in, wq, wk, wv, lines, dq, dk, dv)
    mine = lax.dynamic_index_in_dim(pack_grads, core, 0, keepdims=False)
    theirs = lax.dynamic_index_in_dim(pack_grads, 1 - core, 0, keepdims=False)
    theirs = lax.ppermute(theirs, "c", swap)
    pack_grads = (mine.astype(F32) + theirs.astype(F32)).astype(sum_type)
    pack_grads = pack_grads.reshape((-1,) + pack_grads.shape[2:])
    pack_grads = lax.all_to_all(pack_grads, ("x", "y"), 0, 0, tiled=True)
    after_xy = pack_grads
    pack_grads = jnp.sum(pack_grads.astype(F32), 0)
    ones = line_ones[:2]
    for axis in ("c", "y", "x"):
        ones = ones + lax.ppermute(ones, axis, swap)
    ones = ones.reshape(2, dp // 2, 2, part)
    ones = lax.dynamic_index_in_dim(ones, place[1], 2, keepdims=False).transpose(1, 0, 2)
    ones = jnp.pad(
        ones.reshape(dp // 2, 1, 2 * part), ((0, 0), (0, 0), (0, model - 2 * part))
    )
    pack_grads = (
        pack_grads + jnp.pad(ones, ((0, 0), (part, pack_grads.shape[1] - part - 1), (0, 0)))
    ).astype(sum_type)
    if length == 4:
        pack_grad = lax.dynamic_index_in_dim(pack_grads, place[0], 0, keepdims=False).astype(F32)
        for far in (1, 2, 3):
            some = lax.dynamic_index_in_dim(pack_grads, (place[0] + far) % 4, 0, keepdims=False)
            some = lax.ppermute(some, "z", [(k, (k + far) % 4) for k in range(4)])
            pack_grad = pack_grad + some.astype(F32)
    else:
        pack_grad = lax.psum_scatter(pack_grads, "z", scatter_dimension=0, tiled=False)
    qkv_out = pack_grad[:part, : 3 * width].reshape(part, 3, width).transpose(1, 0, 2)
    out_weight_grad = pack_grad[:part, 3 * width :].T
    small_grads = pack_grad[part:].reshape(-1)[: small_rows * part].reshape(small_rows, part)

    mixture = combine(mixed)
    bias_term = jnp.dot(share_here, bias_down, precision=HIGHEST).reshape(residual.shape)
    output = (residual + mixture + bias_term).astype(BF16)

    sent = [send_back(reduced[:1], after_xy)]
    sent.append(send_back(reduced[1:2], *sent))
    sent.append(send_back(reduced[2:], *sent[1:]))
    sent = [one.astype(F32) for one in sent if one is not None]
    ups = [one[:, 0] for one in sent]
    downs = [one[:, 1] for one in sent]
    up_grad = jnp.concatenate(ups, -1)
    down_grad = jnp.concatenate(downs, -1).transpose(0, 2, 1)
    return (
        output,
        input_grad,
        small_grads[0],
        small_grads[1],
        qkv_out,
        small_grads[2:4],
        out_weight_grad,
        small_grads[4],
        small_grads[5],
        small_grads[6],
        small_grads[7 + experts : 7 + 2 * experts].T,
        up_grad,
        small_grads[7 + 2 * experts :].reshape(experts, -1),
        down_grad,
        small_grads[7 : 7 + experts],
    )


def solution(mesh):
    dp, tensor = mesh.devices.shape
    planes = jax.sharding.Mesh(
        mesh.devices.reshape(dp // 2, 2, tensor // 2, 2), ("z", "x", "y", "c")
    )
    rows = ("z", "x")
    images = P(("z", "x", "y", "c"), None, None)
    return jax.shard_map(
        shards,
        mesh=planes,
        in_specs=(
            images,
            P(rows, None),
            P(rows, None, None),
            P(rows, None, None),
            P(rows),
            P(rows),
            P(None, rows, TENSOR),
            P(None, rows),
            P(TENSOR, rows),
            P(rows),
            P(rows),
            P(rows),
            P(rows, None),
            P(None, rows, TENSOR),
            P(None, rows),
            P(None, TENSOR, rows),
            P(None, rows),
            images,
        ),
        out_specs=(
            images,
            images,
            P(rows),
            P(rows),
            P(None, rows, TENSOR),
            P(None, rows),
            P(TENSOR, rows),
            P(rows),
            P(rows),
            P(rows),
            P(rows, None),
            P(None, rows, TENSOR),
            P(None, rows),
            P(None, TENSOR, rows),
            P(None, rows),
        ),
        check_vma=False,
    )
```

```python
import functools
import jax
import jax.numpy as jnp
from jax import lax
from jax.experimental import pallas as pl
from jax.experimental.pallas import tpu as pltpu
from jax.sharding import PartitionSpec as P

HD = 64
CAP = 128
EPSILON = 1e-06
NEGATIVE = -1e30
F32 = jnp.float32
BF16 = jnp.bfloat16


def dot(left, right, left_dim=1, right_dim=0):
    return lax.dot_general(
        left, right, (((left_dim,), (right_dim,)), ((), ())), preferred_element_type=F32
    )


def norm_forward(values, gains, shifts):
    middle = jnp.mean(values, -1, keepdims=True)
    centred = values - middle
    inverse = lax.rsqrt(jnp.mean(centred * centred, -1, keepdims=True) + EPSILON)
    unit_rows = centred * inverse
    return (unit_rows * gains + shifts, unit_rows, inverse)


def norm_backward(grad_rows, unit_rows, inverse, gains):
    scaled = grad_rows * gains
    return inverse * (
        scaled
        - jnp.mean(scaled, -1, keepdims=True)
        - unit_rows * jnp.mean(scaled * unit_rows, -1, keepdims=True)
    )


def head_masks(width):
    lane = lax.broadcasted_iota(jnp.int32, (1, width), 1)
    return [(lane // HD == k) for k in range(width // HD)]


def arrange(w_ref, *parts):
    width = parts[0].shape[2]
    for t in range(w_ref.shape[0]):
        packed = w_ref[t]
        for k, ref in enumerate(parts):
            ref[t] = packed[:, k * width : (k + 1) * width]


def put_rows(ref, values):
    rows, columns = values.shape
    spare = jnp.zeros((ref.shape[0] - rows, columns), values.dtype)
    ref[...] = jnp.concatenate([values, spare], 0).astype(ref.dtype)


def attend_forward_kernel(
    place_ref, tokens_ref, mask_ref, lines_ref, bias_ref, *refs,
):
    (
        n1_ref, n2_ref, h_ref, q_ref, k_ref, v_ref, o_ref, lse_ref,
        wq_ref, wk_ref, wv_ref, wo_ref, all_ref, sem,
    ) = refs[-14:]
    packs = refs[:-14]

    @pl.when(pl.program_id(0) == 0)
    def _():
        if len(packs) == 1:
            pltpu.make_async_copy(packs[0], all_ref, sem).start()
        else:
            z, x, y, c = [place_ref[k] for k in range(4)]
            part = all_ref.shape[1] // 8
            for index, ref in enumerate(packs):
                dx, dy, dc = index & 1, (index >> 1) & 1, index >> 2
                t = (y ^ dy) * 2 + (c ^ dc)
                for back in range(4):
                    row = (((z - back) & 3) * 2 + (x ^ dx)) * part
                    pltpu.make_async_copy(
                        ref.at[back, pl.ds(0, part)],
                        all_ref.at[t, pl.ds(pl.multiple_of(row, 32), part)],
                        sem,
                    ).start()
        pltpu.make_async_copy(all_ref, all_ref, sem).wait()
        arrange(all_ref, wq_ref, wk_ref, wv_ref, wo_ref)

    x = tokens_ref[0].astype(F32)
    n1, _, _ = norm_forward(x, lines_ref[0:1, :], lines_ref[1:2, :])
    put_rows(n1_ref.at[0], n1)
    n1 = n1.astype(BF16)
    width = wq_ref.shape[2]
    masks = head_masks(width)
    keys = mask_ref[0] > 0
    total = x + lines_ref[4:5, :]
    for t in range(wq_ref.shape[0]):
        q = (dot(n1, wq_ref[t]) + bias_ref[t, 0:1, :]).astype(BF16)
        k = dot(n1, wk_ref[t]).astype(BF16)
        v = (dot(n1, wv_ref[t]) + bias_ref[t, 1:2, :]).astype(BF16)
        q_ref[0, t] = q
        k_ref[0, t] = k
        v_ref[0, t] = v
        scaled = q * jnp.asarray(HD ** (-0.5), BF16)
        o = jnp.zeros(q.shape, F32)
        for h, here in enumerate(masks):
            s = dot(jnp.where(here, scaled, jnp.zeros_like(scaled)), k, 1, 1)
            s = jnp.where(keys, s, NEGATIVE)
            largest = jnp.max(s, -1, keepdims=True)
            e = jnp.exp(s - largest)
            total_e = jnp.sum(e, -1, keepdims=True)
            p = (e / total_e).astype(BF16)
            o = jnp.where(here, dot(p, v), o)
            index = t * len(masks) + h
            lse_ref[0, :, index : index + 1] = largest + jnp.log(total_e)
        put_rows(o_ref.at[0, t], o)
        total = total + dot(o.astype(BF16), wo_ref[t], 1, 1)
    h_ref[0] = total
    n2, _, _ = norm_forward(total, lines_ref[5:6, :], lines_ref[6:7, :])
    n2_ref[0] = n2.astype(BF16)


def whole(shape):
    return pl.BlockSpec(shape, lambda b: (0,) * len(shape))


def by_image(shape):
    return pl.BlockSpec((1,) + shape[1:], lambda b: (b,) + (0,) * (len(shape) - 1))


def padded(rows):
    return -(-rows // 16) * 16


def attend_forward(place, tokens_in, mask, lines, bias_pairs, packs, width):
    images, sequence, model = tokens_in.shape
    quarter = model // width
    rows = (images, sequence, model)
    heads = (images, quarter, sequence, width)
    columns = (quarter, model, width)
    outs = [
        ((images, padded(sequence), model), BF16), (rows, BF16), (rows, F32), (heads, BF16), (heads, BF16),
        (heads, BF16), ((images, quarter, padded(sequence), width), BF16), ((images, sequence, 128), F32),
        (columns, BF16), (columns, BF16), (columns, BF16), (columns, BF16),
    ]
    place_spec = lambda spec: pl.BlockSpec(spec.block_shape, lambda b, p: spec.index_map(b))
    in_specs = [by_image(tokens_in.shape), by_image(mask.shape), whole(lines.shape), whole(bias_pairs.shape)]
    out_specs = [by_image(s) for s, _ in outs[:8]] + [whole(s) for s, _ in outs[8:]]
    return pl.pallas_call(
        attend_forward_kernel,
        grid_spec=pltpu.PrefetchScalarGridSpec(
            num_scalar_prefetch=1,
            grid=(images,),
            in_specs=[place_spec(s) for s in in_specs]
            + [pl.BlockSpec(memory_space=pl.ANY)] * len(packs),
            out_specs=[place_spec(s) for s in out_specs],
            scratch_shapes=[pltpu.VMEM((quarter, model, 4 * width), BF16), pltpu.SemaphoreType.DMA(())],
        ),
        out_shape=[jax.ShapeDtypeStruct(s, d) for s, d in outs],
        compiler_params=pltpu.CompilerParams(vmem_limit_bytes=56 * 2**20),
        cost_estimate=pl.CostEstimate(flops=2 * 10**9, bytes_accessed=4 * 10**6, transcendentals=0),
        name="attend_forward",
    )(place, tokens_in, mask, lines, bias_pairs, *packs)


def combine_kernel(core_ref, back_ref, full_at_ref, half_at_ref, full_ref, mine_ref, theirs_ref):
    experts, rows, model = back_ref.shape
    cap = full_ref.shape[2] - model
    half = cap // 2
    images, sequence, _ = full_ref.shape

    def gather(at_ref, first, size, slot):
        lanes = experts * size
        lane = lax.broadcasted_iota(jnp.int32, (1, lanes), 1)
        slots = lane // size * cap + slot + lane % size
        hot = (at_ref[:, 0:1] == slots) | (at_ref[:, 1:2] == slots)
        hot = jnp.where(hot, 1.0, 0.0).astype(BF16)
        taken = back_ref[:, first : first + size].reshape(lanes, model)
        sums = dot(hot, taken)
        owner = lax.broadcasted_iota(jnp.int32, (cap, lanes), 0) == lane // size
        scores = 0.0
        for k in range(2):
            line = jnp.concatenate(
                [
                    back_ref[e, cap + half :, first : first + size].astype(F32)[k : k + 1]
                    for e in range(experts)
                ],
                1,
            )
            scores += dot(hot, jnp.where(owner, line, 0.0).astype(BF16), 1, 1)
        joined = jnp.concatenate([sums, scores], 1)
        return [joined[k * sequence : (k + 1) * sequence] for k in range(images)]

    full = gather(full_at_ref, 0, cap, 0)
    shared = gather(half_at_ref, cap, half, core_ref[0] * half)
    for image in range(images):
        full_ref[image] = full[image]
        own = core_ref[0] == image

        def put(ref, image=image):
            ref[0] = shared[image]

        pl.when(own)(functools.partial(put, mine_ref))
        pl.when(jnp.logical_not(own))(functools.partial(put, theirs_ref))


def combine_rows(core, back, full_at, half_at, images):
    shape = (images, full_at.shape[0] // images, back.shape[2] + CAP)
    whole_at = lambda shape: pl.BlockSpec(shape, lambda i, c: (0,) * len(shape))
    return pl.pallas_call(
        combine_kernel,
        grid_spec=pltpu.PrefetchScalarGridSpec(
            num_scalar_prefetch=1,
            grid=(1,),
            in_specs=[whole_at(a.shape) for a in (back, full_at, half_at)],
            out_specs=[whole_at(shape)] + [whole_at((1,) + shape[1:])] * 2,
        ),
        out_shape=[
            jax.ShapeDtypeStruct(s, F32) for s in (shape, (1,) + shape[1:], (1,) + shape[1:])
        ],
        compiler_params=pltpu.CompilerParams(vmem_limit_bytes=56 * 2**20),
        cost_estimate=pl.CostEstimate(flops=0, bytes_accessed=0, transcendentals=0),
        name="combine_rows",
    )(core, back, full_at, half_at)


def attend_backward_kernel(
    core_ref, full_ref, mine_ref, theirs_ref, chance_ref, route_ref, router_ref,
    grad_ref, h_ref, mask_ref, wo_ref, lines_ref, q_ref, k_ref, v_ref, lse_ref,
    h_grad_ref, hb_ref, dq_ref, dk_ref, dv_ref, logit_ref, vec_ref, pair_ref,
):
    @pl.when(pl.program_id(0) == 0)
    def _():
        vec_ref[...] = jnp.zeros_like(vec_ref)
        pair_ref[...] = jnp.zeros_like(pair_ref)

    shared = pl.program_id(0) == 2 * (1 - core_ref[0])
    rows = jnp.where(shared, mine_ref[0] + theirs_ref[0], full_ref[0])
    model = wo_ref.shape[1]
    chances = chance_ref[0]
    chance_grad = rows[:, model:] + route_ref[0]
    logit_grad = chances * (
        chance_grad - jnp.sum(chances * chance_grad, -1, keepdims=True)
    )
    logit_grad = logit_grad.astype(BF16)
    logit_ref[0] = logit_grad
    n2_grad = rows[:, :model] + dot(logit_grad, router_ref[...])
    _, unit_two, inverse_two = norm_forward(h_ref[0], lines_ref[5:6, :], lines_ref[6:7, :])
    vec_ref[1:2, :] += jnp.sum(n2_grad * unit_two, 0, keepdims=True)
    vec_ref[2:3, :] += jnp.sum(n2_grad, 0, keepdims=True)
    h_grad = grad_ref[0].astype(F32) + norm_backward(
        n2_grad, unit_two, inverse_two, lines_ref[5:6, :]
    )
    vec_ref[0:1, :] += jnp.sum(h_grad, 0, keepdims=True)
    h_grad_ref[0] = h_grad
    put_rows(hb_ref.at[0], h_grad)
    hb = h_grad.astype(BF16)
    width = wo_ref.shape[2]
    masks = head_masks(width)
    keys = mask_ref[0] > 0
    scale = HD ** (-0.5)
    for t in range(wo_ref.shape[0]):
        do = dot(hb, wo_ref[t]).astype(BF16)
        q, k, v = q_ref[0, t], k_ref[0, t], v_ref[0, t]
        zero = jnp.zeros_like(q)
        scaled = q * jnp.asarray(scale, BF16)
        dq = jnp.zeros(q.shape, F32)
        dk = jnp.zeros(q.shape, F32)
        dv = jnp.zeros(q.shape, F32)
        for h, here in enumerate(masks):
            index = t * len(masks) + h
            s = dot(jnp.where(here, scaled, zero), k, 1, 1)
            s = jnp.where(keys, s, NEGATIVE)
            p = jnp.exp(s - lse_ref[0, :, index : index + 1])
            dp = dot(jnp.where(here, do, zero), v, 1, 1)
            ds = p * (dp - jnp.sum(p * dp, -1, keepdims=True))
            ds = ds.astype(BF16)
            dv = jnp.where(here, dot(p.astype(BF16), do, 0, 0), dv)
            dq = jnp.where(here, dot(ds, k), dq)
            dk = jnp.where(here, dot(ds, q, 0, 0), dk)
        dq = (dq * scale).astype(BF16).astype(F32)
        dv = dv.astype(BF16).astype(F32)
        pair_ref[t, 0:1, :] += jnp.sum(dq, 0, keepdims=True)
        pair_ref[t, 1:2, :] += jnp.sum(dv, 0, keepdims=True)
        put_rows(dq_ref.at[0, t], dq)
        put_rows(dk_ref.at[0, t], dk * scale)
        put_rows(dv_ref.at[0, t], dv)


def attend_backward(
    core, full, mine, theirs, chances, route, router, out_grad, h, mask, wo, lines, q, k, v, lse
):
    ins = (full, mine, theirs, chances, route, router, out_grad, h, mask, wo, lines, q, k, v, lse)
    images, sequence, model = h.shape
    quarter, _, width = wo.shape
    heads = ((images, quarter, padded(sequence), width), BF16)
    outs = [
        (h.shape, F32), ((images, padded(sequence), model), BF16), heads, heads, heads,
        (chances.shape, BF16), ((8, model), F32), ((quarter, 8, width), F32),
    ]

    def spec(index, shape):
        block = (1,) + shape[1:]
        rest = (0,) * (len(shape) - 1)
        if index == 0:
            return pl.BlockSpec(block, lambda b, c: (jnp.clip(b - c[0], 0, images - 2),) + rest)
        if index in (1, 2, 5, 9, 10):
            return pl.BlockSpec(shape, lambda b, c: (0,) * len(shape))
        return pl.BlockSpec(block, lambda b, c: (b,) + rest)

    return pl.pallas_call(
        attend_backward_kernel,
        grid_spec=pltpu.PrefetchScalarGridSpec(
            num_scalar_prefetch=1,
            grid=(images,),
            in_specs=[spec(i, a.shape) for i, a in enumerate(ins)],
            out_specs=[spec(3, s) for s, _ in outs[:6]] + [spec(2, s) for s, _ in outs[6:]],
        ),
        out_shape=[jax.ShapeDtypeStruct(s, d) for s, d in outs],
        compiler_params=pltpu.CompilerParams(vmem_limit_bytes=56 * 2**20),
        cost_estimate=pl.CostEstimate(flops=0, bytes_accessed=0, transcendentals=0),
        name="attend_backward",
    )(core, *ins)


def attend_weights_kernel(n1_ref, hb_ref, dq_ref, dk_ref, dv_ref, o_ref, *refs):
    width = dq_ref.shape[3]
    n1 = n1_ref[...].reshape(-1, n1_ref.shape[2])
    hb = hb_ref[...].reshape(-1, n1_ref.shape[2])
    pairs = ((n1, dq_ref), (n1, dk_ref), (n1, dv_ref), (hb, o_ref))
    t = pl.program_id(0)
    if len(refs) == 1:
        for k, (left, ref) in enumerate(pairs):
            sums = dot(left, ref[...].reshape(-1, width), 0, 0)
            refs[0][0, :, k * width : (k + 1) * width] = sums.astype(refs[0].dtype)
        return
    extra_ref, lines_ref, *weights, out_ref, gain_ref, shift_ref = refs
    part = n1.shape[1] // 8
    lanes = gain_ref.shape[1]

    @pl.when(t == 0)
    def _():
        gain_ref[...] = jnp.zeros_like(gain_ref)
        shift_ref[...] = jnp.zeros_like(shift_ref)

    for k, (left, ref) in enumerate(pairs):
        right = ref[...].reshape(-1, width)
        sums = dot(left, right, 0, 0)
        if k < 3:
            weight = weights[k][0].astype(F32)
            shift = weight * jnp.sum(right.astype(F32), 0, keepdims=True)
            gain = weight * sums
            for one, total_ref in ((gain, gain_ref), (shift, shift_ref)):
                total_ref[...] += one[:, :lanes]
                total_ref[:, : width - lanes] += one[:, lanes:]
        sums = sums.astype(BF16)
        for z in range(4):
            for x in range(2):
                start = (z * 2 + x) * part
                out_ref[t % 2, x, t // 2, z, :part, k * width : (k + 1) * width] = sums[
                    start : start + part
                ]

    @pl.when(t == pl.num_programs(0) - 1)
    def _():
        gain = jnp.sum(gain_ref[...].T, 0, keepdims=True)
        shift = jnp.sum(shift_ref[...].T, 0, keepdims=True)
        gain = (gain - lines_ref[1:2, :] * shift) / lines_ref[0:1, :]
        depth, model = extra_ref.shape[1:]
        row = lax.broadcasted_iota(jnp.int32, (depth, model), 0)
        for z in range(4):
            for x in range(2):
                here = slice((z * 2 + x) * part, (z * 2 + x + 1) * part)
                line = jnp.concatenate(
                    [gain[:, here], shift[:, here], jnp.zeros((1, model - 2 * part), F32)], 1
                )
                block = extra_ref[z * 2 + x].astype(F32) + jnp.where(row == 0, line, 0.0)
                block = block.astype(BF16)
                for y in range(2):
                    for c in range(2):
                        out_ref[c, x, y, z, part:, :] = block


def attend_weights(n1, hb, dq, dk, dv, o, extra, lines=None, weights=()):
    images, quarter, rows, width = dq.shape
    model = n1.shape[2]
    heads = pl.BlockSpec((images, 1, rows, width), lambda t: (0, t, 0, 0))
    in_specs = [whole(n1.shape), whole(hb.shape)] + [heads] * 4
    if extra is None:
        extras = []
        out_spec = pl.BlockSpec((1, model, 4 * width), lambda t: (t, 0, 0))
        out_shape = jax.ShapeDtypeStruct((quarter, model, 4 * width), F32)
        scratch = []
    else:
        extras = [extra, lines, *weights]
        in_specs += [whole(extra.shape), whole(lines.shape)]
        in_specs += [pl.BlockSpec((1, model, width), lambda t: (t, 0, 0))] * len(weights)
        shape = (2, 2, 2, 4, model // 8 + extra.shape[1], model)
        out_spec = whole(shape)
        out_shape = jax.ShapeDtypeStruct(shape, BF16)
        scratch = [pltpu.VMEM((model, 128), F32)] * 2
    return pl.pallas_call(
        attend_weights_kernel,
        grid=(quarter,),
        in_specs=in_specs,
        out_specs=out_spec,
        out_shape=out_shape,
        scratch_shapes=scratch,
        compiler_params=pltpu.CompilerParams(vmem_limit_bytes=56 * 2**20),
        cost_estimate=pl.CostEstimate(flops=0, bytes_accessed=0, transcendentals=0),
        name="attend_weights",
    )(n1, hb, dq, dk, dv, o, *extras)


def input_backward_kernel(
    h_grad_ref, tokens_ref, wq_ref, wk_ref, wv_ref, lines_ref, dq_ref, dk_ref, dv_ref,
    input_grad_ref, vec_ref,
):
    @pl.when(pl.program_id(0) == 0)
    def _():
        vec_ref[...] = jnp.zeros_like(vec_ref)

    rows = tokens_ref.shape[1]
    n1_grad = jnp.zeros((dq_ref.shape[2], tokens_ref.shape[2]), F32)
    for t in range(wq_ref.shape[0]):
        for grads, weights in ((dq_ref, wq_ref), (dk_ref, wk_ref), (dv_ref, wv_ref)):
            n1_grad += dot(grads[0, t], weights[t], 1, 1)
    n1_grad = n1_grad[:rows]
    _, unit_one, inverse_one = norm_forward(
        tokens_ref[0].astype(F32), lines_ref[0:1, :], lines_ref[1:2, :]
    )
    vec_ref[0:1, :] += jnp.sum(n1_grad * unit_one, 0, keepdims=True)
    vec_ref[1:2, :] += jnp.sum(n1_grad, 0, keepdims=True)
    input_grad_ref[0] = h_grad_ref[0] + norm_backward(
        n1_grad, unit_one, inverse_one, lines_ref[0:1, :]
    )


def input_backward(h_grad, tokens_in, wq, wk, wv, lines, dq, dk, dv):
    ins = (h_grad, tokens_in, wq, wk, wv, lines, dq, dk, dv)
    outs = [(h_grad.shape, F32), ((8, wq.shape[1]), F32)]
    return pl.pallas_call(
        input_backward_kernel,
        grid=(h_grad.shape[0],),
        in_specs=[whole(a.shape) if 2 <= i <= 5 else by_image(a.shape) for i, a in enumerate(ins)],
        out_specs=[by_image(outs[0][0]), whole(outs[1][0])],
        out_shape=[jax.ShapeDtypeStruct(s, d) for s, d in outs],
        compiler_params=pltpu.CompilerParams(vmem_limit_bytes=56 * 2**20),
        cost_estimate=pl.CostEstimate(flops=0, bytes_accessed=0, transcendentals=0),
        name="input_backward",
    )(*ins)


def pack_experts_kernel(up_ref, down_ref, *refs):
    up = up_ref[0].astype(BF16)
    down = down_ref[0].astype(BF16)
    start = 0
    for ref in refs:
        stop = start + ref.shape[3]
        ref[0, 0] = up[:, start:stop]
        ref[0, 1] = down[:, start:stop]
        start = stop


def pack_experts(up, down, sizes):
    experts, part, units = up.shape
    outs = [(experts, 2, part, size) for size in sizes]
    return pl.pallas_call(
        pack_experts_kernel,
        grid=(experts,),
        in_specs=[by_image(up.shape), by_image(down.shape)],
        out_specs=[by_image(s) for s in outs],
        out_shape=[jax.ShapeDtypeStruct(s, BF16) for s in outs],
        compiler_params=pltpu.CompilerParams(vmem_limit_bytes=56 * 2**20),
        cost_estimate=pl.CostEstimate(flops=0, bytes_accessed=8 * 10**6, transcendentals=0),
        name="pack_experts",
    )(up, down)


def to_column(line):
    return jnp.broadcast_to(line, (128, 256)).T[:, :1]


def to_line(column):
    return jnp.broadcast_to(column, (256, 128)).T[:1, :]


def expert_kernel(first, last, x_ref, g_ref, b_ref, shards_ref, *refs):
    if not first:
        (y_in, p_in), refs = refs[:2], refs[2:]
    (y_out, p_out, bias_ref), refs = refs[:3], refs[3:]
    acc_ref, w_ref, sem = refs[-3:]
    grads_ref = refs[0]
    step = pl.program_id(0)
    model = w_ref.shape[1]

    @pl.when(step == 0)
    def _():
        if len(shards_ref.shape) == 3:
            pltpu.make_async_copy(shards_ref, w_ref, sem).start()
        else:
            part, units = shards_ref.shape[3:]
            for z in range(4):
                for p in range(8):
                    row = (z * 2 + p // 4) * part
                    pltpu.make_async_copy(
                        shards_ref.at[z, p],
                        w_ref.at[:, pl.ds(row, part), pl.ds((p % 4) * units, units)],
                        sem,
                    ).start()
        acc_ref[...] = jnp.zeros_like(acc_ref)
        bias_ref[...] = jnp.zeros_like(bias_ref)
        pltpu.make_async_copy(w_ref, w_ref, sem).wait()

    sources, slots, _ = g_ref.shape
    x = x_ref[:, :slots].reshape(-1, model)
    g_raw = g_ref[...].reshape(-1, model)
    gates = []
    for k in range(sources):
        parts = x_ref[k, slots : slots + 16, :256].astype(F32)
        gates.append(to_column(parts[0:1] + parts[1:2])[:slots])
    gate = jnp.concatenate(gates, 0)
    g = (g_raw.astype(F32) * gate).astype(BF16)
    hidden = dot(x, w_ref[0]) + b_ref[...]
    cdf = 0.5 * (1.0 + lax.erf(hidden * (0.5 ** 0.5)))
    active = (hidden * cdf).astype(BF16)
    slope = cdf + hidden * (jnp.exp(-0.5 * hidden * hidden) * 0.3989422804014327)
    hidden_grad = (dot(g, w_ref[1]) * slope).astype(BF16)
    y = dot(active, w_ref[1], 1, 1)
    p = dot(hidden_grad, w_ref[0], 1, 1)
    if not first:
        y = y_in[...].reshape(-1, model) + y
        p = p_in[...].reshape(-1, model) + p
    if not last:
        y_out[...] = y.reshape(sources, slots, model)
        p_out[...] = p.reshape(sources, slots, model)
    else:
        y_out[...] = (y * gate).astype(BF16).reshape(sources, slots, model)
        p_out[:, :slots] = p.astype(BF16).reshape(sources, slots, model)
        gate_grad = jnp.sum(g_raw.astype(F32) * y, -1, keepdims=True)
        for k in range(sources):
            own = gate_grad[k * slots : (k + 1) * slots]
            line = to_line(jnp.concatenate([own, jnp.zeros((256 - slots, 1), F32)], 0))
            high = line.astype(BF16)
            low = (line - high.astype(F32)).astype(BF16)
            block = jnp.concatenate([high, low, jnp.zeros((14, 256), BF16)], 0)
            p_out[k, slots:] = jnp.concatenate([block, jnp.zeros((16, model - 256), BF16)], 1)
    bias_ref[...] += jnp.sum(hidden_grad.astype(F32), 0, keepdims=True)
    acc_ref[0] += dot(x, hidden_grad, 0, 0)
    acc_ref[1] += dot(g, active, 0, 0)

    @pl.when(step == pl.num_programs(0) - 1)
    def _():
        if len(shards_ref.shape) == 3:
            grads_ref[...] = acc_ref[...]
        else:
            part, units = shards_ref.shape[3:]
            for z in range(4):
                for q in range(8):
                    row = (z * 2 + q // 4) * part
                    columns = slice((q % 4) * units, (q % 4 + 1) * units)
                    grads_ref[z, q] = acc_ref[:, row : row + part, columns].astype(BF16)


def expert_chunk(x, g, b, sums, shards, last):
    experts, slots, model = g.shape
    units = b.shape[1]
    first = sums is None
    step = 2
    block = lambda rows: pl.BlockSpec((step, rows, model), lambda i: (i, 0, 0))
    full = whole
    ins = [x, g, b, shards] + ([] if first else list(sums))
    in_specs = [block(x.shape[1]), block(slots), full(b.shape)]
    in_specs.append(pl.BlockSpec(memory_space=pl.ANY))
    in_specs += [] if first else [block(slots)] * 2
    rows = (experts, slots, model)
    if last:
        outs = [(rows, BF16), (x.shape, BF16)]
    else:
        outs = [(rows, F32), (rows, F32)]
    out_specs = [block(s[1]) for s, _ in outs]
    outs.append((b.shape, F32))
    if len(shards.shape) == 3:
        outs.append(((2, model, units), F32))
    else:
        outs.append((shards.shape, BF16))
    out_specs += [full(s) for s, _ in outs[2:]]
    base = 4
    return pl.pallas_call(
        functools.partial(expert_kernel, first, last),
        grid=(experts // step,),
        in_specs=in_specs,
        out_specs=out_specs,
        scratch_shapes=[
            pltpu.VMEM((2, model, units), F32),
            pltpu.VMEM((2, model, units), BF16),
            pltpu.SemaphoreType.DMA(()),
        ],
        out_shape=[jax.ShapeDtypeStruct(s, d) for s, d in outs],
        input_output_aliases={} if first or last else {base: 0, base + 1: 1},
        compiler_params=pltpu.CompilerParams(vmem_limit_bytes=58 * 2**20),
        cost_estimate=pl.CostEstimate(
            flops=2 * experts * slots * model * units, bytes_accessed=4 * 10**6, transcendentals=0
        ),
        name="expert_chunk",
    )(*ins)


GROUP_IMG = 2
CHUNK = 128
HIGHEST = lax.Precision.HIGHEST
TENSOR = ("y", "c")
PLANE = ("x", "y", "c")
EVERY = ("y", "c", "z", "x")


def tie(values, *events):
    events = [e for e in events if e is not None]
    if not events:
        return values
    return lax.optimization_barrier((values, *events))[0]


def gather_packs(pack):
    below = [pack] + [
        lax.ppermute(pack, "z", [(k, (k + far) % 4) for k in range(4)]) for far in (1, 2, 3)
    ]
    column = jnp.stack(below)
    swap = [(0, 1), (1, 0)]
    over_x = lax.ppermute(column, "x", swap)
    over_y = lax.ppermute(column, "y", swap)
    over_both = lax.ppermute(column, ("x", "y"), [(0, 3), (1, 2), (2, 1), (3, 0)])
    four = [column, over_x, over_y, over_both]
    return four + [lax.ppermute(each, "c", swap) for each in four], below[1:]


def shards(
    tokens_in,
    key_mask,
    expert_ids,
    expert_slots,
    norm1_gain,
    norm1_shift,
    qkv_weight,
    qv_bias,
    out_weight,
    out_bias,
    norm2_gain,
    norm2_shift,
    router_weight,
    up_weight,
    up_bias,
    down_weight,
    down_bias,
    out_grad,
):
    length = lax.axis_size("z")
    core = lax.axis_index("c")
    chip_y = lax.axis_index("y")
    quarter = lax.axis_size("y") * 2
    expert = (lax.axis_index("x") * lax.axis_size("y") + chip_y) * 2 + core
    piece, sequence, model = tokens_in.shape
    experts, part, units = up_weight.shape
    dp = model // part
    width = qkv_weight.shape[2]
    tokens = piece * sequence
    blocks = units // CHUNK
    spans = [(0, 4), (4, 6)] if blocks == 6 else [(0, blocks)]

    head = spans[0][1] * CHUNK
    sizes = [head, units - head] if units > head else [head]
    packed = pack_experts(up_weight, down_weight.transpose(0, 2, 1), sizes)
    qkv_weight, norm1_gain = tie((qkv_weight, norm1_gain), packed[0])

    smalls = jnp.concatenate(
        [
            norm1_gain[None],
            norm1_shift[None],
            qv_bias,
            out_bias[None],
            norm2_gain[None],
            norm2_shift[None],
            down_bias,
            router_weight.T,
            up_bias.reshape(experts * quarter, part),
        ],
        0,
    ).astype(BF16)
    small_rows = smalls.shape[0]
    pad = -(small_rows * part) % (16 * model)
    small_block = jnp.pad(smalls.reshape(-1), (0, pad)).reshape(-1, model)
    pack = jnp.concatenate(
        [
            jnp.concatenate(
                [qkv_weight[0], qkv_weight[1], qkv_weight[2], out_weight.T], 1
            ).astype(BF16),
            small_block,
        ],
        0,
    )
    place = [lax.axis_index(name) for name in ("z", "x", "y", "c")]
    if length == 4:
        packs, below = gather_packs(pack)
        by_x = jnp.stack([packs[0][:, part:], packs[1][:, part:]]).reshape(2, 4, -1)
        pick_x = (place[1] ^ jnp.arange(2))[:, None] == jnp.arange(2)
        pick_z = (place[0] - jnp.arange(4)[:, None]) % 4 == jnp.arange(4)
        pick = pick_z[:, None, None, :] & pick_x[None, :, :, None]
        vectors = dot(pick.reshape(8, 8).astype(BF16), by_x.reshape(8, -1)).astype(BF16)
    else:
        packs = lax.all_gather(pack, EVERY, axis=0, tiled=False)
        packs = packs.reshape(quarter, dp, pack.shape[0], model)
        vectors = packs[0, :, part:].reshape(dp, -1)
        packs = [packs[:, :, :part].reshape(quarter, model, model)]
    event = []
    parts = []
    for some in packed:
        some = lax.all_to_all(tie(some, *event), PLANE, 0, 0, tiled=True)
        event = [some, *packs[3:4]]
        starts = [CHUNK * f for f, _ in spans[1:]] if parts else [0]
        stops = [CHUNK * l for _, l in spans[1:]] if parts else [head]
        base = starts[0]
        parts += [some[..., f - base : l - base] for f, l in zip(starts, stops)]
    if length != 4:
        parts = [
            one.reshape(2, quarter, 2, part, -1).transpose(2, 0, 3, 1, 4).reshape(2, 2 * part, -1)
            for one in parts
        ]

    vectors = vectors[:, : small_rows * part].reshape(dp, small_rows, part).transpose(1, 0, 2)
    lines = vectors[: 7 + 2 * experts].reshape(-1, model).astype(F32)
    bias_pairs = lines[2:4].reshape(2, quarter, width).transpose(1, 0, 2)
    bias_down = lines[7 : 7 + experts]
    router = lines[7 + experts :].astype(BF16)
    bias_up = vectors[7 + 2 * experts :].reshape(experts, quarter, dp, part)
    bias_up = bias_up.transpose(0, 2, 1, 3).reshape(experts, quarter, units)
    bias_up = lax.dynamic_index_in_dim(bias_up, expert, 0, keepdims=False).astype(F32)

    first_group = chip_y * 3
    group_tokens = GROUP_IMG * sequence
    position = (expert_ids * CAP + expert_slots).reshape(-1, group_tokens, 2)
    position_full = lax.dynamic_index_in_dim(position, first_group + 2 * core, 0, keepdims=False)
    position_half = lax.dynamic_index_in_dim(position, first_group + 1, 0, keepdims=False)
    slots_full = jnp.arange(experts * CAP, dtype=jnp.int32)
    half = CAP // 2
    slots_half = (
        jnp.arange(experts, dtype=jnp.int32)[:, None] * CAP
        + core * half
        + jnp.arange(half, dtype=jnp.int32)
    ).reshape(-1)
    match_full = slots_full[:, None, None] == position_full.T[None]
    match_half = slots_half[:, None, None] == position_half.T[None]
    hot_full = (match_full[:, 0] | match_full[:, 1]).astype(BF16)
    hot_half = (match_half[:, 0] | match_half[:, 1]).astype(BF16)
    swap = [(0, 1), (1, 0)]

    def both_groups(values):
        lent = jnp.where(core == 0, values[2], values[0])
        other = lax.ppermute(lent, "c", swap)
        full = jnp.where(core == 0, values[:2], values[1:])
        shared = jnp.where(core == 0, jnp.stack([lent, other]), jnp.stack([other, lent]))
        return (
            full.reshape(group_tokens, -1),
            shared.reshape(group_tokens, -1),
        )

    def join_rows(full, shared):
        full = full.reshape((experts, CAP) + full.shape[1:])
        shared = shared.reshape((experts, half) + shared.shape[1:])
        return jnp.concatenate([full, shared], 1)

    def lines_of(values):
        high = values.astype(BF16)
        low = (values - high.astype(F32)).astype(BF16)
        both = jnp.stack([high, low], 1)
        return jnp.pad(both, ((0, 0), (0, 14), (0, model - both.shape[2])))

    def values_of(rows):
        both = rows[:, CAP + half : CAP + half + 2, : CAP + half].astype(F32)
        return both[:, 0] + both[:, 1]

    def swap_experts(rows, *events):
        return lax.all_to_all(tie(rows, *events), PLANE, 0, 0, tiled=True)

    def dispatch(full, shared):
        return join_rows(dot(hot_full, full).astype(BF16), dot(hot_half, shared).astype(BF16))

    def combine(back):
        full = dot(hot_full, back[:, :CAP].reshape(-1, model), 0, 0)
        shared = dot(hot_half, back[:, CAP : CAP + half].reshape(-1, model), 0, 0)
        full = full.reshape(GROUP_IMG, sequence, model)
        shared = shared.reshape(GROUP_IMG, sequence, model)
        mine = jnp.where(core == 0, shared[0], shared[1])
        theirs = jnp.where(core == 0, shared[1], shared[0])
        mine = mine + lax.ppermute(theirs, "c", swap)
        return jnp.where(
            core == 0,
            jnp.concatenate([full, mine[None]]),
            jnp.concatenate([mine[None], full]),
        )

    if length == 4:
        parts[0] = tie(parts[0], *below)
    full_parts = [
        lax.all_gather(one, "z", axis=0, tiled=False)
        if length == 4
        else lax.all_gather(one, "z", axis=1, tiled=True)
        for one in parts
    ]
    grad_full, grad_shared = both_groups(out_grad)
    incoming = swap_experts(dispatch(grad_full, grad_shared), *packs[1:4], parts[-1])

    local_start = (chip_y * 2 + core) * piece
    mask_here = lax.dynamic_slice_in_dim(key_mask, local_start, piece, 0)[:, None]
    n1, n2, residual, q, k, v, attended, lse, wq, wk, wv, wo = attend_forward(
        jnp.stack(place).astype(jnp.int32),
        tokens_in, mask_here, lines, bias_pairs,
        packs, width,
    )
    n2 = tie(n2, incoming)
    normed_two = n2.reshape(tokens, model)

    normed_full, normed_shared = both_groups(n2)

    def chances_of(rows):
        return jax.nn.softmax(dot(rows, router, 1, 1), -1)

    probabilities = chances_of(normed_two)
    hot_ids = expert_ids[..., None] == jnp.arange(experts, dtype=jnp.int32)
    hot_here = lax.dynamic_slice_in_dim(hot_ids, local_start, piece, 0).astype(F32)
    hot_here = jnp.sum(hot_here.reshape(tokens, 2, experts), 1)
    share_here = hot_here * probabilities

    def slot_gates(match, rows, position_here):
        chance = chances_of(rows)
        hot = (position_here // CAP)[..., None] == jnp.arange(experts, dtype=jnp.int32)
        gates = jnp.sum(hot.astype(F32) * chance[:, None], -1)
        return jnp.sum(jnp.where(match, gates.T[None], 0.0), (1, 2))

    gates_sent = join_rows(
        slot_gates(match_full, normed_full, position_full),
        slot_gates(match_half, normed_shared, position_half),
    )
    chosen = swap_experts(
        jnp.concatenate([dispatch(normed_full, normed_shared), lines_of(gates_sent)], 1),
        incoming,
    )

    grad_rows = out_grad.reshape(tokens, model)
    bias_dot = dot(grad_rows, bias_down.astype(BF16), 1, 1)

    def lanes(values):
        values = jnp.pad(values, ((0, 0), (0, CAP - experts)))
        return values.reshape(piece, sequence, CAP)

    down_bias_grad = lax.dot_general(
        share_here, grad_rows.astype(F32), (((0,), (0,)), ((), ())), precision=HIGHEST
    )

    routes = (
        lanes(probabilities), lanes(hot_here * bias_dot), jnp.pad(router, ((0, CAP - experts), (0, 0)))
    )

    sums = None
    bias_parts = []
    reduced = []
    count = len(spans)
    for index, (first, last) in enumerate(spans):
        bias_one = bias_up[:, first * CHUNK : last * CHUNK].reshape(1, -1)
        final = index == count - 1
        if final:
            bias_one = tie(bias_one, *routes, down_bias_grad)
        *sums, bias_part, grads = expert_chunk(
            chosen, incoming, bias_one, sums, full_parts[index], final
        )
        bias_parts.append(bias_part.reshape(quarter, -1))
        if length == 4:
            reduced.append(lax.psum_scatter(grads, "z", scatter_dimension=0, tiled=False))
        else:
            reduced.append(lax.psum_scatter(grads, "z", scatter_dimension=1, tiled=True))

    mixed, pulled = sums
    back = swap_experts(pulled)
    core_line = jnp.reshape(core, (1,)).astype(jnp.int32)
    full_rows, mine_rows, theirs = combine_rows(
        core_line, back, position_full, position_half, GROUP_IMG
    )
    theirs = lax.ppermute(theirs, "c", swap)

    def send_back(some, *events):
        if not some:
            return None
        some = some[0].astype(BF16)
        if length != 4:
            some = some.reshape(2, 2, part, quarter, -1).transpose(1, 3, 0, 2, 4)
            some = some.reshape(experts, 2, part, -1)
        return swap_experts(some, *events)

    mixed = swap_experts(mixed, back)

    h_grad, hb, dq, dk, dv, logit_grad, line_sums, pair_sums = attend_backward(
        core_line, full_rows, mine_rows, theirs, *routes, out_grad, residual, mask_here, wo, lines, q, k, v, lse,
    )
    router_grad = dot(logit_grad.reshape(tokens, CAP), normed_two, 0, 0)[:experts]
    if length != 4:
        input_grad, line_ones = input_backward(h_grad, tokens_in, wq, wk, wv, lines, dq, dk, dv)

    bias_rows = jnp.concatenate(bias_parts, 1).reshape(dp, quarter, part)
    bias_rows = jnp.where(
        jnp.arange(experts)[:, None, None, None] == expert, bias_rows[None], 0.0
    )
    bias_rows = bias_rows.transpose(0, 2, 1, 3).reshape(experts * quarter, dp, part)
    line_grads = jnp.concatenate(
        [
            jnp.zeros((2, model), F32) if length == 4 else line_ones[:2],
            pair_sums[:, 0].reshape(1, model),
            pair_sums[:, 1].reshape(1, model),
            line_sums[:3],
            down_bias_grad,
            router_grad,
        ],
        0,
    ).reshape(-1, dp, part)
    sum_type = BF16 if length == 4 else F32
    vector_grads = jnp.concatenate([line_grads, bias_rows], 0).astype(sum_type)
    vector_grads = vector_grads.transpose(1, 0, 2).reshape(dp, small_rows * part)
    vector_grads = jnp.pad(vector_grads, ((0, 0), (0, pad))).reshape(dp, -1, model)

    hb = tie(hb, mixed)
    if length == 4:
        pack_grads = attend_weights(
            n1, hb, dq, dk, dv, attended, vector_grads, lines, (wq, wk, wv)
        )
    else:
        pack_grads = attend_weights(n1, hb, dq, dk, dv, attended, None)
        pack_grads = pack_grads.reshape(quarter, dp, part, model)
        vector_grads = jnp.broadcast_to(vector_grads[None], (quarter,) + vector_grads.shape)
        pack_grads = jnp.concatenate([pack_grads, vector_grads], 2)
        pack_grads = pack_grads.reshape(quarter // 2, 2, dp // 2, 2, -1, model)
        pack_grads = pack_grads.transpose(1, 3, 0, 2, 4, 5)
    weights_done = pack_grads
    mine = lax.dynamic_index_in_dim(pack_grads, core, 0, keepdims=False)
    theirs = lax.dynamic_index_in_dim(pack_grads, 1 - core, 0, keepdims=False)
    theirs = lax.ppermute(theirs, "c", swap)
    pack_grads = (mine.astype(F32) + theirs.astype(F32)).astype(sum_type)
    pack_grads = pack_grads.reshape((-1,) + pack_grads.shape[2:])
    if length == 4:
        h_grad = tie(h_grad, pack_grads)
        input_grad, _ = input_backward(h_grad, tokens_in, wq, wk, wv, lines, dq, dk, dv)
    sent = [send_back(reduced[:1], weights_done)]
    pack_grads = tie(pack_grads, *sent)
    pack_grads = lax.all_to_all(pack_grads, ("x", "y"), 0, 0, tiled=True)
    after_xy = pack_grads
    mixture = combine(mixed)
    bias_term = jnp.dot(share_here, bias_down, precision=HIGHEST).reshape(residual.shape)
    output = (residual + mixture + bias_term).astype(BF16)

    sent = [one.astype(F32) for one in sent if one is not None]
    ups = [one[:, 0] for one in sent]
    downs = [one[:, 1] for one in sent]
    pack_grads = tie(pack_grads, input_grad, output, *ups, *downs)
    pack_grads = jnp.sum(pack_grads.astype(F32), 0)
    pack_grads = pack_grads.astype(sum_type)
    if length == 4:
        pack_grad = lax.dynamic_index_in_dim(pack_grads, place[0], 0, keepdims=False).astype(F32)
        for far in (1, 2, 3):
            some = lax.dynamic_index_in_dim(pack_grads, (place[0] + far) % 4, 0, keepdims=False)
            some = lax.ppermute(some, "z", [(k, (k + far) % 4) for k in range(4)])
            pack_grad = pack_grad + some.astype(F32)
    else:
        pack_grad = lax.psum_scatter(pack_grads, "z", scatter_dimension=0, tiled=False)
    qkv_out = pack_grad[:part, : 3 * width].reshape(part, 3, width).transpose(1, 0, 2)
    out_weight_grad = pack_grad[:part, 3 * width :].T
    small_grads = pack_grad[part:].reshape(-1)[: small_rows * part].reshape(small_rows, part)

    some = send_back(reduced[1:], pack_grads)
    if some is not None:
        ups.append(some.astype(F32)[:, 0])
        downs.append(some.astype(F32)[:, 1])
    up_grad = jnp.concatenate(ups, -1)
    down_grad = jnp.concatenate(downs, -1).transpose(0, 2, 1)
    return (
        output,
        input_grad,
        small_grads[0],
        small_grads[1],
        qkv_out,
        small_grads[2:4],
        out_weight_grad,
        small_grads[4],
        small_grads[5],
        small_grads[6],
        small_grads[7 + experts : 7 + 2 * experts].T,
        up_grad,
        small_grads[7 + 2 * experts :].reshape(experts, -1),
        down_grad,
        small_grads[7 : 7 + experts],
    )


def solution(mesh):
    dp, tensor = mesh.devices.shape
    planes = jax.sharding.Mesh(
        mesh.devices.reshape(dp // 2, 2, tensor // 2, 2), ("z", "x", "y", "c")
    )
    rows = ("z", "x")
    images = P(("z", "x", "y", "c"), None, None)
    return jax.shard_map(
        shards,
        mesh=planes,
        in_specs=(
            images,
            P(rows, None),
            P(rows, None, None),
            P(rows, None, None),
            P(rows),
            P(rows),
            P(None, rows, TENSOR),
            P(None, rows),
            P(TENSOR, rows),
            P(rows),
            P(rows),
            P(rows),
            P(rows, None),
            P(None, rows, TENSOR),
            P(None, rows),
            P(None, TENSOR, rows),
            P(None, rows),
            images,
        ),
        out_specs=(
            images,
            images,
            P(rows),
            P(rows),
            P(None, rows, TENSOR),
            P(None, rows),
            P(TENSOR, rows),
            P(rows),
            P(rows),
            P(rows),
            P(rows, None),
            P(None, rows, TENSOR),
            P(None, rows),
            P(None, TENSOR, rows),
            P(None, rows),
        ),
        check_vma=False,
    )
```

```python
import functools
import jax
import jax.numpy as jnp
from jax import lax
from jax.experimental import pallas as pl
from jax.experimental.pallas import tpu as pltpu
from jax.sharding import PartitionSpec as P

HD = 64
CAP = 128
EPSILON = 1e-06
NEGATIVE = -1e30
F32 = jnp.float32
BF16 = jnp.bfloat16


def dot(left, right, left_dim=1, right_dim=0):
    return lax.dot_general(
        left, right, (((left_dim,), (right_dim,)), ((), ())), preferred_element_type=F32
    )


def norm_forward(values, gains, shifts):
    middle = jnp.mean(values, -1, keepdims=True)
    centred = values - middle
    inverse = lax.rsqrt(jnp.mean(centred * centred, -1, keepdims=True) + EPSILON)
    unit_rows = centred * inverse
    return (unit_rows * gains + shifts, unit_rows, inverse)


def norm_backward(grad_rows, unit_rows, inverse, gains):
    scaled = grad_rows * gains
    return inverse * (
        scaled
        - jnp.mean(scaled, -1, keepdims=True)
        - unit_rows * jnp.mean(scaled * unit_rows, -1, keepdims=True)
    )


def head_masks(width):
    lane = lax.broadcasted_iota(jnp.int32, (1, width), 1)
    return [(lane // HD == k) for k in range(width // HD)]


def arrange(w_ref, *parts):
    width = parts[0].shape[2]
    for t in range(w_ref.shape[0]):
        packed = w_ref[t]
        for k, ref in enumerate(parts):
            ref[t] = packed[:, k * width : (k + 1) * width]


def put_rows(ref, values):
    rows, columns = values.shape
    spare = jnp.zeros((ref.shape[0] - rows, columns), values.dtype)
    ref[...] = jnp.concatenate([values, spare], 0).astype(ref.dtype)


def attend_forward_kernel(
    place_ref, tokens_ref, mask_ref, lines_ref, bias_ref, *refs,
):
    (
        n1_ref, n2_ref, h_ref, q_ref, k_ref, v_ref, o_ref, lse_ref,
        wq_ref, wk_ref, wv_ref, wo_ref, all_ref, sem,
    ) = refs[-14:]
    packs = refs[:-14]

    @pl.when(pl.program_id(0) == 0)
    def _():
        if len(packs) == 1:
            pltpu.make_async_copy(packs[0], all_ref, sem).start()
        else:
            z, x, y, c = [place_ref[k] for k in range(4)]
            part = all_ref.shape[1] // 8
            for index, ref in enumerate(packs):
                dx, dy, dc = index & 1, (index >> 1) & 1, index >> 2
                t = (y ^ dy) * 2 + (c ^ dc)
                for back in range(4):
                    row = (((z - back) & 3) * 2 + (x ^ dx)) * part
                    pltpu.make_async_copy(
                        ref.at[back, pl.ds(0, part)],
                        all_ref.at[t, pl.ds(pl.multiple_of(row, 32), part)],
                        sem,
                    ).start()
        pltpu.make_async_copy(all_ref, all_ref, sem).wait()
        arrange(all_ref, wq_ref, wk_ref, wv_ref, wo_ref)

    x = tokens_ref[0].astype(F32)
    n1, _, _ = norm_forward(x, lines_ref[0:1, :], lines_ref[1:2, :])
    put_rows(n1_ref.at[0], n1)
    n1 = n1.astype(BF16)
    width = wq_ref.shape[2]
    masks = head_masks(width)
    keys = mask_ref[0] > 0
    total = x + lines_ref[4:5, :]
    for t in range(wq_ref.shape[0]):
        q = (dot(n1, wq_ref[t]) + bias_ref[t, 0:1, :]).astype(BF16)
        k = dot(n1, wk_ref[t]).astype(BF16)
        v = (dot(n1, wv_ref[t]) + bias_ref[t, 1:2, :]).astype(BF16)
        q_ref[0, t] = q
        k_ref[0, t] = k
        v_ref[0, t] = v
        scaled = q * jnp.asarray(HD ** (-0.5), BF16)
        o = jnp.zeros(q.shape, F32)
        for h, here in enumerate(masks):
            s = dot(jnp.where(here, scaled, jnp.zeros_like(scaled)), k, 1, 1)
            s = jnp.where(keys, s, NEGATIVE)
            largest = jnp.max(s, -1, keepdims=True)
            e = jnp.exp(s - largest)
            total_e = jnp.sum(e, -1, keepdims=True)
            p = (e / total_e).astype(BF16)
            o = jnp.where(here, dot(p, v), o)
            index = t * len(masks) + h
            lse_ref[0, :, index : index + 1] = largest + jnp.log(total_e)
        put_rows(o_ref.at[0, t], o)
        total = total + dot(o.astype(BF16), wo_ref[t], 1, 1)
    h_ref[0] = total
    n2, _, _ = norm_forward(total, lines_ref[5:6, :], lines_ref[6:7, :])
    n2_ref[0] = n2.astype(BF16)


def whole(shape):
    return pl.BlockSpec(shape, lambda b: (0,) * len(shape))


def by_image(shape):
    return pl.BlockSpec((1,) + shape[1:], lambda b: (b,) + (0,) * (len(shape) - 1))


def padded(rows):
    return -(-rows // 16) * 16


def attend_forward(place, tokens_in, mask, lines, bias_pairs, packs, width):
    images, sequence, model = tokens_in.shape
    quarter = model // width
    rows = (images, sequence, model)
    heads = (images, quarter, sequence, width)
    columns = (quarter, model, width)
    outs = [
        ((images, padded(sequence), model), BF16), (rows, BF16), (rows, F32), (heads, BF16), (heads, BF16),
        (heads, BF16), ((images, quarter, padded(sequence), width), BF16), ((images, sequence, 128), F32),
        (columns, BF16), (columns, BF16), (columns, BF16), (columns, BF16),
    ]
    place_spec = lambda spec: pl.BlockSpec(spec.block_shape, lambda b, p: spec.index_map(b))
    in_specs = [by_image(tokens_in.shape), by_image(mask.shape), whole(lines.shape), whole(bias_pairs.shape)]
    out_specs = [by_image(s) for s, _ in outs[:8]] + [whole(s) for s, _ in outs[8:]]
    return pl.pallas_call(
        attend_forward_kernel,
        grid_spec=pltpu.PrefetchScalarGridSpec(
            num_scalar_prefetch=1,
            grid=(images,),
            in_specs=[place_spec(s) for s in in_specs]
            + [pl.BlockSpec(memory_space=pl.ANY)] * len(packs),
            out_specs=[place_spec(s) for s in out_specs],
            scratch_shapes=[pltpu.VMEM((quarter, model, 4 * width), BF16), pltpu.SemaphoreType.DMA(())],
        ),
        out_shape=[jax.ShapeDtypeStruct(s, d) for s, d in outs],
        compiler_params=pltpu.CompilerParams(vmem_limit_bytes=56 * 2**20),
        cost_estimate=pl.CostEstimate(flops=2 * 10**9, bytes_accessed=4 * 10**6, transcendentals=0),
        name="attend_forward",
    )(place, tokens_in, mask, lines, bias_pairs, *packs)


def combine_kernel(core_ref, back_ref, full_at_ref, half_at_ref, full_ref, mine_ref, theirs_ref):
    experts, rows, model = back_ref.shape
    cap = full_ref.shape[2] - model
    half = cap // 2
    images, sequence, _ = full_ref.shape

    def gather(at_ref, first, size, slot):
        lanes = experts * size
        lane = lax.broadcasted_iota(jnp.int32, (1, lanes), 1)
        slots = lane // size * cap + slot + lane % size
        hot = (at_ref[:, 0:1] == slots) | (at_ref[:, 1:2] == slots)
        hot = jnp.where(hot, 1.0, 0.0).astype(BF16)
        taken = back_ref[:, first : first + size].reshape(lanes, model)
        sums = dot(hot, taken)
        owner = lax.broadcasted_iota(jnp.int32, (cap, lanes), 0) == lane // size
        scores = 0.0
        for k in range(2):
            line = jnp.concatenate(
                [
                    back_ref[e, cap + half :, first : first + size].astype(F32)[k : k + 1]
                    for e in range(experts)
                ],
                1,
            )
            scores += dot(hot, jnp.where(owner, line, 0.0).astype(BF16), 1, 1)
        joined = jnp.concatenate([sums, scores], 1)
        return [joined[k * sequence : (k + 1) * sequence] for k in range(images)]

    full = gather(full_at_ref, 0, cap, 0)
    shared = gather(half_at_ref, cap, half, core_ref[0] * half)
    for image in range(images):
        full_ref[image] = full[image]
        own = core_ref[0] == image

        def put(ref, image=image):
            ref[0] = shared[image]

        pl.when(own)(functools.partial(put, mine_ref))
        pl.when(jnp.logical_not(own))(functools.partial(put, theirs_ref))


def combine_rows(core, back, full_at, half_at, images):
    shape = (images, full_at.shape[0] // images, back.shape[2] + CAP)
    whole_at = lambda shape: pl.BlockSpec(shape, lambda i, c: (0,) * len(shape))
    return pl.pallas_call(
        combine_kernel,
        grid_spec=pltpu.PrefetchScalarGridSpec(
            num_scalar_prefetch=1,
            grid=(1,),
            in_specs=[whole_at(a.shape) for a in (back, full_at, half_at)],
            out_specs=[whole_at(shape)] + [whole_at((1,) + shape[1:])] * 2,
        ),
        out_shape=[
            jax.ShapeDtypeStruct(s, F32) for s in (shape, (1,) + shape[1:], (1,) + shape[1:])
        ],
        compiler_params=pltpu.CompilerParams(vmem_limit_bytes=56 * 2**20),
        cost_estimate=pl.CostEstimate(flops=0, bytes_accessed=0, transcendentals=0),
        name="combine_rows",
    )(core, back, full_at, half_at)


def attend_backward_kernel(
    core_ref, full_ref, mine_ref, theirs_ref, chance_ref, route_ref, router_ref,
    grad_ref, h_ref, mask_ref, wo_ref, lines_ref, q_ref, k_ref, v_ref, lse_ref,
    h_grad_ref, hb_ref, dq_ref, dk_ref, dv_ref, logit_ref, vec_ref, pair_ref,
):
    @pl.when(pl.program_id(0) == 0)
    def _():
        vec_ref[...] = jnp.zeros_like(vec_ref)
        pair_ref[...] = jnp.zeros_like(pair_ref)

    shared = pl.program_id(0) == 2 * (1 - core_ref[0])
    rows = jnp.where(shared, mine_ref[0] + theirs_ref[0], full_ref[0])
    model = wo_ref.shape[1]
    chances = chance_ref[0]
    chance_grad = rows[:, model:] + route_ref[0]
    logit_grad = chances * (
        chance_grad - jnp.sum(chances * chance_grad, -1, keepdims=True)
    )
    logit_grad = logit_grad.astype(BF16)
    logit_ref[0] = logit_grad
    n2_grad = rows[:, :model] + dot(logit_grad, router_ref[...])
    _, unit_two, inverse_two = norm_forward(h_ref[0], lines_ref[5:6, :], lines_ref[6:7, :])
    vec_ref[1:2, :] += jnp.sum(n2_grad * unit_two, 0, keepdims=True)
    vec_ref[2:3, :] += jnp.sum(n2_grad, 0, keepdims=True)
    h_grad = grad_ref[0].astype(F32) + norm_backward(
        n2_grad, unit_two, inverse_two, lines_ref[5:6, :]
    )
    vec_ref[0:1, :] += jnp.sum(h_grad, 0, keepdims=True)
    h_grad_ref[0] = h_grad
    put_rows(hb_ref.at[0], h_grad)
    hb = h_grad.astype(BF16)
    width = wo_ref.shape[2]
    masks = head_masks(width)
    keys = mask_ref[0] > 0
    scale = HD ** (-0.5)
    for t in range(wo_ref.shape[0]):
        do = dot(hb, wo_ref[t]).astype(BF16)
        q, k, v = q_ref[0, t], k_ref[0, t], v_ref[0, t]
        zero = jnp.zeros_like(q)
        scaled = q * jnp.asarray(scale, BF16)
        dq = jnp.zeros(q.shape, F32)
        dk = jnp.zeros(q.shape, F32)
        dv = jnp.zeros(q.shape, F32)
        for h, here in enumerate(masks):
            index = t * len(masks) + h
            s = dot(jnp.where(here, scaled, zero), k, 1, 1)
            s = jnp.where(keys, s, NEGATIVE)
            p = jnp.exp(s - lse_ref[0, :, index : index + 1])
            dp = dot(jnp.where(here, do, zero), v, 1, 1)
            ds = p * (dp - jnp.sum(p * dp, -1, keepdims=True))
            ds = ds.astype(BF16)
            dv = jnp.where(here, dot(p.astype(BF16), do, 0, 0), dv)
            dq = jnp.where(here, dot(ds, k), dq)
            dk = jnp.where(here, dot(ds, q, 0, 0), dk)
        dq = (dq * scale).astype(BF16).astype(F32)
        dv = dv.astype(BF16).astype(F32)
        pair_ref[t, 0:1, :] += jnp.sum(dq, 0, keepdims=True)
        pair_ref[t, 1:2, :] += jnp.sum(dv, 0, keepdims=True)
        put_rows(dq_ref.at[0, t], dq)
        put_rows(dk_ref.at[0, t], dk * scale)
        put_rows(dv_ref.at[0, t], dv)


def attend_backward(
    core, full, mine, theirs, chances, route, router, out_grad, h, mask, wo, lines, q, k, v, lse
):
    ins = (full, mine, theirs, chances, route, router, out_grad, h, mask, wo, lines, q, k, v, lse)
    images, sequence, model = h.shape
    quarter, _, width = wo.shape
    heads = ((images, quarter, padded(sequence), width), BF16)
    outs = [
        (h.shape, F32), ((images, padded(sequence), model), BF16), heads, heads, heads,
        (chances.shape, BF16), ((8, model), F32), ((quarter, 8, width), F32),
    ]

    def spec(index, shape):
        block = (1,) + shape[1:]
        rest = (0,) * (len(shape) - 1)
        if index == 0:
            return pl.BlockSpec(block, lambda b, c: (jnp.clip(b - c[0], 0, images - 2),) + rest)
        if index in (1, 2, 5, 9, 10):
            return pl.BlockSpec(shape, lambda b, c: (0,) * len(shape))
        return pl.BlockSpec(block, lambda b, c: (b,) + rest)

    return pl.pallas_call(
        attend_backward_kernel,
        grid_spec=pltpu.PrefetchScalarGridSpec(
            num_scalar_prefetch=1,
            grid=(images,),
            in_specs=[spec(i, a.shape) for i, a in enumerate(ins)],
            out_specs=[spec(3, s) for s, _ in outs[:6]] + [spec(2, s) for s, _ in outs[6:]],
        ),
        out_shape=[jax.ShapeDtypeStruct(s, d) for s, d in outs],
        compiler_params=pltpu.CompilerParams(vmem_limit_bytes=56 * 2**20),
        cost_estimate=pl.CostEstimate(flops=0, bytes_accessed=0, transcendentals=0),
        name="attend_backward",
    )(core, *ins)


def attend_weights_kernel(n1_ref, hb_ref, dq_ref, dk_ref, dv_ref, o_ref, *refs):
    width = dq_ref.shape[3]
    n1 = n1_ref[...].reshape(-1, n1_ref.shape[2])
    hb = hb_ref[...].reshape(-1, n1_ref.shape[2])
    pairs = ((n1, dq_ref), (n1, dk_ref), (n1, dv_ref), (hb, o_ref))
    t = pl.program_id(0)
    if len(refs) == 1:
        for k, (left, ref) in enumerate(pairs):
            sums = dot(left, ref[...].reshape(-1, width), 0, 0)
            refs[0][0, :, k * width : (k + 1) * width] = sums.astype(refs[0].dtype)
        return
    extra_ref, lines_ref, *weights, out_ref, gain_ref, shift_ref = refs
    part = n1.shape[1] // 8
    lanes = gain_ref.shape[1]

    @pl.when(t == 0)
    def _():
        gain_ref[...] = jnp.zeros_like(gain_ref)
        shift_ref[...] = jnp.zeros_like(shift_ref)

    for k, (left, ref) in enumerate(pairs):
        right = ref[...].reshape(-1, width)
        sums = dot(left, right, 0, 0)
        if k < 3:
            weight = weights[k][0].astype(F32)
            shift = weight * jnp.sum(right.astype(F32), 0, keepdims=True)
            gain = weight * sums
            for one, total_ref in ((gain, gain_ref), (shift, shift_ref)):
                total_ref[...] += one[:, :lanes]
                total_ref[:, : width - lanes] += one[:, lanes:]
        sums = sums.astype(BF16)
        for z in range(4):
            for x in range(2):
                start = (z * 2 + x) * part
                out_ref[t % 2, x, t // 2, z, :part, k * width : (k + 1) * width] = sums[
                    start : start + part
                ]

    @pl.when(t == pl.num_programs(0) - 1)
    def _():
        gain = jnp.sum(gain_ref[...].T, 0, keepdims=True)
        shift = jnp.sum(shift_ref[...].T, 0, keepdims=True)
        gain = (gain - lines_ref[1:2, :] * shift) / lines_ref[0:1, :]
        depth, model = extra_ref.shape[1:]
        row = lax.broadcasted_iota(jnp.int32, (depth, model), 0)
        for z in range(4):
            for x in range(2):
                here = slice((z * 2 + x) * part, (z * 2 + x + 1) * part)
                line = jnp.concatenate(
                    [gain[:, here], shift[:, here], jnp.zeros((1, model - 2 * part), F32)], 1
                )
                block = extra_ref[z * 2 + x].astype(F32) + jnp.where(row == 0, line, 0.0)
                block = block.astype(BF16)
                for y in range(2):
                    for c in range(2):
                        out_ref[c, x, y, z, part:, :] = block


def attend_weights(n1, hb, dq, dk, dv, o, extra, lines=None, weights=()):
    images, quarter, rows, width = dq.shape
    model = n1.shape[2]
    heads = pl.BlockSpec((images, 1, rows, width), lambda t: (0, t, 0, 0))
    in_specs = [whole(n1.shape), whole(hb.shape)] + [heads] * 4
    if extra is None:
        extras = []
        out_spec = pl.BlockSpec((1, model, 4 * width), lambda t: (t, 0, 0))
        out_shape = jax.ShapeDtypeStruct((quarter, model, 4 * width), F32)
        scratch = []
    else:
        extras = [extra, lines, *weights]
        in_specs += [whole(extra.shape), whole(lines.shape)]
        in_specs += [pl.BlockSpec((1, model, width), lambda t: (t, 0, 0))] * len(weights)
        shape = (2, 2, 2, 4, model // 8 + extra.shape[1], model)
        out_spec = whole(shape)
        out_shape = jax.ShapeDtypeStruct(shape, BF16)
        scratch = [pltpu.VMEM((model, 128), F32)] * 2
    return pl.pallas_call(
        attend_weights_kernel,
        grid=(quarter,),
        in_specs=in_specs,
        out_specs=out_spec,
        out_shape=out_shape,
        scratch_shapes=scratch,
        compiler_params=pltpu.CompilerParams(vmem_limit_bytes=56 * 2**20),
        cost_estimate=pl.CostEstimate(flops=0, bytes_accessed=0, transcendentals=0),
        name="attend_weights",
    )(n1, hb, dq, dk, dv, o, *extras)


def input_backward_kernel(
    h_grad_ref, tokens_ref, wq_ref, wk_ref, wv_ref, lines_ref, dq_ref, dk_ref, dv_ref,
    input_grad_ref, vec_ref,
):
    @pl.when(pl.program_id(0) == 0)
    def _():
        vec_ref[...] = jnp.zeros_like(vec_ref)

    rows = tokens_ref.shape[1]
    n1_grad = jnp.zeros((dq_ref.shape[2], tokens_ref.shape[2]), F32)
    for t in range(wq_ref.shape[0]):
        for grads, weights in ((dq_ref, wq_ref), (dk_ref, wk_ref), (dv_ref, wv_ref)):
            n1_grad += dot(grads[0, t], weights[t], 1, 1)
    n1_grad = n1_grad[:rows]
    _, unit_one, inverse_one = norm_forward(
        tokens_ref[0].astype(F32), lines_ref[0:1, :], lines_ref[1:2, :]
    )
    vec_ref[0:1, :] += jnp.sum(n1_grad * unit_one, 0, keepdims=True)
    vec_ref[1:2, :] += jnp.sum(n1_grad, 0, keepdims=True)
    input_grad_ref[0] = h_grad_ref[0] + norm_backward(
        n1_grad, unit_one, inverse_one, lines_ref[0:1, :]
    )


def input_backward(h_grad, tokens_in, wq, wk, wv, lines, dq, dk, dv):
    ins = (h_grad, tokens_in, wq, wk, wv, lines, dq, dk, dv)
    outs = [(h_grad.shape, F32), ((8, wq.shape[1]), F32)]
    return pl.pallas_call(
        input_backward_kernel,
        grid=(h_grad.shape[0],),
        in_specs=[whole(a.shape) if 2 <= i <= 5 else by_image(a.shape) for i, a in enumerate(ins)],
        out_specs=[by_image(outs[0][0]), whole(outs[1][0])],
        out_shape=[jax.ShapeDtypeStruct(s, d) for s, d in outs],
        compiler_params=pltpu.CompilerParams(vmem_limit_bytes=56 * 2**20),
        cost_estimate=pl.CostEstimate(flops=0, bytes_accessed=0, transcendentals=0),
        name="input_backward",
    )(*ins)


def pack_experts_kernel(up_ref, down_ref, *refs):
    up = up_ref[...].astype(BF16)
    down = down_ref[...].astype(BF16)
    start = 0
    for ref in refs:
        stop = start + ref.shape[3]
        ref[:, 0] = up[:, :, start:stop]
        ref[:, 1] = down[:, :, start:stop]
        start = stop


def pack_experts(up, down, sizes):
    experts, part, units = up.shape
    step = 4
    block = lambda shape: pl.BlockSpec((step,) + shape[1:], lambda i: (i,) + (0,) * (len(shape) - 1))
    outs = [(experts, 2, part, size) for size in sizes]
    return pl.pallas_call(
        pack_experts_kernel,
        grid=(experts // step,),
        in_specs=[block(up.shape), block(down.shape)],
        out_specs=[block(s) for s in outs],
        out_shape=[jax.ShapeDtypeStruct(s, BF16) for s in outs],
        compiler_params=pltpu.CompilerParams(vmem_limit_bytes=56 * 2**20),
        cost_estimate=pl.CostEstimate(flops=0, bytes_accessed=8 * 10**6, transcendentals=0),
        name="pack_experts",
    )(up, down)


def to_column(line):
    return jnp.broadcast_to(line, (128, 256)).T[:, :1]


def to_line(column):
    return jnp.broadcast_to(column, (256, 128)).T[:1, :]


def expert_kernel(first, last, x_ref, g_ref, b_ref, shards_ref, *refs):
    if not first:
        (y_in, p_in), refs = refs[:2], refs[2:]
    (y_out, p_out, bias_ref), refs = refs[:3], refs[3:]
    acc_ref, w_ref, sem = refs[-3:]
    grads_ref = refs[0]
    step = pl.program_id(0)
    model = w_ref.shape[1]

    @pl.when(step == 0)
    def _():
        if len(shards_ref.shape) == 3:
            pltpu.make_async_copy(shards_ref, w_ref, sem).start()
        else:
            part, units = shards_ref.shape[3:]
            for z in range(4):
                for p in range(8):
                    row = (z * 2 + p // 4) * part
                    pltpu.make_async_copy(
                        shards_ref.at[z, p],
                        w_ref.at[:, pl.ds(row, part), pl.ds((p % 4) * units, units)],
                        sem,
                    ).start()
        acc_ref[...] = jnp.zeros_like(acc_ref)
        bias_ref[...] = jnp.zeros_like(bias_ref)
        pltpu.make_async_copy(w_ref, w_ref, sem).wait()

    sources, slots, _ = g_ref.shape
    x = x_ref[:, :slots].reshape(-1, model)
    g_raw = g_ref[...].reshape(-1, model)
    gates = []
    for k in range(sources):
        parts = x_ref[k, slots : slots + 16, :256].astype(F32)
        gates.append(to_column(parts[0:1] + parts[1:2])[:slots])
    gate = jnp.concatenate(gates, 0)
    g = (g_raw.astype(F32) * gate).astype(BF16)
    hidden = dot(x, w_ref[0]) + b_ref[...]
    cdf = 0.5 * (1.0 + lax.erf(hidden * (0.5 ** 0.5)))
    active = (hidden * cdf).astype(BF16)
    slope = cdf + hidden * (jnp.exp(-0.5 * hidden * hidden) * 0.3989422804014327)
    hidden_grad = (dot(g, w_ref[1]) * slope).astype(BF16)
    y = dot(active, w_ref[1], 1, 1)
    p = dot(hidden_grad, w_ref[0], 1, 1)
    if not first:
        y = y_in[...].reshape(-1, model) + y
        p = p_in[...].reshape(-1, model) + p
    if not last:
        y_out[...] = y.reshape(sources, slots, model)
        p_out[...] = p.reshape(sources, slots, model)
    else:
        y_out[...] = (y * gate).astype(BF16).reshape(sources, slots, model)
        p_out[:, :slots] = p.astype(BF16).reshape(sources, slots, model)
        gate_grad = jnp.sum(g_raw.astype(F32) * y, -1, keepdims=True)
        for k in range(sources):
            own = gate_grad[k * slots : (k + 1) * slots]
            line = to_line(jnp.concatenate([own, jnp.zeros((256 - slots, 1), F32)], 0))
            high = line.astype(BF16)
            low = (line - high.astype(F32)).astype(BF16)
            block = jnp.concatenate([high, low, jnp.zeros((14, 256), BF16)], 0)
            p_out[k, slots:] = jnp.concatenate([block, jnp.zeros((16, model - 256), BF16)], 1)
    bias_ref[...] += jnp.sum(hidden_grad.astype(F32), 0, keepdims=True)
    acc_ref[0] += dot(x, hidden_grad, 0, 0)
    acc_ref[1] += dot(g, active, 0, 0)

    @pl.when(step == pl.num_programs(0) - 1)
    def _():
        if len(shards_ref.shape) == 3:
            grads_ref[...] = acc_ref[...]
        else:
            part, units = shards_ref.shape[3:]
            for z in range(4):
                for q in range(8):
                    row = (z * 2 + q // 4) * part
                    columns = slice((q % 4) * units, (q % 4 + 1) * units)
                    grads_ref[z, q] = acc_ref[:, row : row + part, columns].astype(BF16)


def expert_chunk(x, g, b, sums, shards, last):
    experts, slots, model = g.shape
    units = b.shape[1]
    first = sums is None
    step = 2
    block = lambda rows: pl.BlockSpec((step, rows, model), lambda i: (i, 0, 0))
    full = whole
    ins = [x, g, b, shards] + ([] if first else list(sums))
    in_specs = [block(x.shape[1]), block(slots), full(b.shape)]
    in_specs.append(pl.BlockSpec(memory_space=pl.ANY))
    in_specs += [] if first else [block(slots)] * 2
    rows = (experts, slots, model)
    if last:
        outs = [(rows, BF16), (x.shape, BF16)]
    else:
        outs = [(rows, F32), (rows, F32)]
    out_specs = [block(s[1]) for s, _ in outs]
    outs.append((b.shape, F32))
    if len(shards.shape) == 3:
        outs.append(((2, model, units), F32))
    else:
        outs.append((shards.shape, BF16))
    out_specs += [full(s) for s, _ in outs[2:]]
    base = 4
    return pl.pallas_call(
        functools.partial(expert_kernel, first, last),
        grid=(experts // step,),
        in_specs=in_specs,
        out_specs=out_specs,
        scratch_shapes=[
            pltpu.VMEM((2, model, units), F32),
            pltpu.VMEM((2, model, units), BF16),
            pltpu.SemaphoreType.DMA(()),
        ],
        out_shape=[jax.ShapeDtypeStruct(s, d) for s, d in outs],
        input_output_aliases={} if first or last else {base: 0, base + 1: 1},
        compiler_params=pltpu.CompilerParams(vmem_limit_bytes=58 * 2**20),
        cost_estimate=pl.CostEstimate(
            flops=2 * experts * slots * model * units, bytes_accessed=4 * 10**6, transcendentals=0
        ),
        name="expert_chunk",
    )(*ins)


GROUP_IMG = 2
CHUNK = 128
HIGHEST = lax.Precision.HIGHEST
TENSOR = ("y", "c")
PLANE = ("x", "y", "c")
EVERY = ("y", "c", "z", "x")


def tie(values, *events):
    events = [e for e in events if e is not None]
    if not events:
        return values
    return lax.optimization_barrier((values, *events))[0]


def gather_packs(pack):
    below = [pack] + [
        lax.ppermute(pack, "z", [(k, (k + far) % 4) for k in range(4)]) for far in (1, 2, 3)
    ]
    column = jnp.stack(below)
    swap = [(0, 1), (1, 0)]
    over_x = lax.ppermute(column, "x", swap)
    over_y = lax.ppermute(column, "y", swap)
    over_both = lax.ppermute(column, ("x", "y"), [(0, 3), (1, 2), (2, 1), (3, 0)])
    four = [column, over_x, over_y, over_both]
    return four + [lax.ppermute(each, "c", swap) for each in four], below[1:]


def shards(
    tokens_in,
    key_mask,
    expert_ids,
    expert_slots,
    norm1_gain,
    norm1_shift,
    qkv_weight,
    qv_bias,
    out_weight,
    out_bias,
    norm2_gain,
    norm2_shift,
    router_weight,
    up_weight,
    up_bias,
    down_weight,
    down_bias,
    out_grad,
):
    length = lax.axis_size("z")
    core = lax.axis_index("c")
    chip_y = lax.axis_index("y")
    quarter = lax.axis_size("y") * 2
    expert = (lax.axis_index("x") * lax.axis_size("y") + chip_y) * 2 + core
    piece, sequence, model = tokens_in.shape
    experts, part, units = up_weight.shape
    dp = model // part
    width = qkv_weight.shape[2]
    tokens = piece * sequence
    blocks = units // CHUNK
    spans = [(0, 4), (4, 6)] if blocks == 6 else [(0, blocks)]

    head = spans[0][1] * CHUNK
    sizes = [head, units - head] if units > head else [head]
    packed = pack_experts(up_weight, down_weight.transpose(0, 2, 1), sizes)
    qkv_weight, norm1_gain = tie((qkv_weight, norm1_gain), packed[0])

    smalls = jnp.concatenate(
        [
            norm1_gain[None],
            norm1_shift[None],
            qv_bias,
            out_bias[None],
            norm2_gain[None],
            norm2_shift[None],
            down_bias,
            router_weight.T,
            up_bias.reshape(experts * quarter, part),
        ],
        0,
    ).astype(BF16)
    small_rows = smalls.shape[0]
    pad = -(small_rows * part) % (16 * model)
    small_block = jnp.pad(smalls.reshape(-1), (0, pad)).reshape(-1, model)
    pack = jnp.concatenate(
        [
            jnp.concatenate(
                [qkv_weight[0], qkv_weight[1], qkv_weight[2], out_weight.T], 1
            ).astype(BF16),
            small_block,
        ],
        0,
    )
    place = [lax.axis_index(name) for name in ("z", "x", "y", "c")]
    if length == 4:
        packs, below = gather_packs(pack)
        by_x = jnp.stack([packs[0][:, part:], packs[1][:, part:]]).reshape(2, 4, -1)
        pick_x = (place[1] ^ jnp.arange(2))[:, None] == jnp.arange(2)
        pick_z = (place[0] - jnp.arange(4)[:, None]) % 4 == jnp.arange(4)
        pick = pick_z[:, None, None, :] & pick_x[None, :, :, None]
        vectors = dot(pick.reshape(8, 8).astype(BF16), by_x.reshape(8, -1)).astype(BF16)
    else:
        packs = lax.all_gather(pack, EVERY, axis=0, tiled=False)
        packs = packs.reshape(quarter, dp, pack.shape[0], model)
        vectors = packs[0, :, part:].reshape(dp, -1)
        packs = [packs[:, :, :part].reshape(quarter, model, model)]
    event = []
    parts = []
    for some in packed:
        some = lax.all_to_all(tie(some, *event), PLANE, 0, 0, tiled=True)
        event = [some, *packs[3:4]]
        starts = [CHUNK * f for f, _ in spans[1:]] if parts else [0]
        stops = [CHUNK * l for _, l in spans[1:]] if parts else [head]
        base = starts[0]
        parts += [some[..., f - base : l - base] for f, l in zip(starts, stops)]
    if length != 4:
        parts = [
            one.reshape(2, quarter, 2, part, -1).transpose(2, 0, 3, 1, 4).reshape(2, 2 * part, -1)
            for one in parts
        ]

    vectors = vectors[:, : small_rows * part].reshape(dp, small_rows, part).transpose(1, 0, 2)
    lines = vectors[: 7 + 2 * experts].reshape(-1, model).astype(F32)
    bias_pairs = lines[2:4].reshape(2, quarter, width).transpose(1, 0, 2)
    bias_down = lines[7 : 7 + experts]
    router = lines[7 + experts :].astype(BF16)
    bias_up = vectors[7 + 2 * experts :].reshape(experts, quarter, dp, part)
    bias_up = bias_up.transpose(0, 2, 1, 3).reshape(experts, quarter, units)
    bias_up = lax.dynamic_index_in_dim(bias_up, expert, 0, keepdims=False).astype(F32)

    first_group = chip_y * 3
    group_tokens = GROUP_IMG * sequence
    position = (expert_ids * CAP + expert_slots).reshape(-1, group_tokens, 2)
    position_full = lax.dynamic_index_in_dim(position, first_group + 2 * core, 0, keepdims=False)
    position_half = lax.dynamic_index_in_dim(position, first_group + 1, 0, keepdims=False)
    slots_full = jnp.arange(experts * CAP, dtype=jnp.int32)
    half = CAP // 2
    slots_half = (
        jnp.arange(experts, dtype=jnp.int32)[:, None] * CAP
        + core * half
        + jnp.arange(half, dtype=jnp.int32)
    ).reshape(-1)
    match_full = slots_full[:, None, None] == position_full.T[None]
    match_half = slots_half[:, None, None] == position_half.T[None]
    hot_full = (match_full[:, 0] | match_full[:, 1]).astype(BF16)
    hot_half = (match_half[:, 0] | match_half[:, 1]).astype(BF16)
    swap = [(0, 1), (1, 0)]

    def both_groups(values):
        lent = jnp.where(core == 0, values[2], values[0])
        other = lax.ppermute(lent, "c", swap)
        full = jnp.where(core == 0, values[:2], values[1:])
        shared = jnp.where(core == 0, jnp.stack([lent, other]), jnp.stack([other, lent]))
        return (
            full.reshape(group_tokens, -1),
            shared.reshape(group_tokens, -1),
        )

    def join_rows(full, shared):
        full = full.reshape((experts, CAP) + full.shape[1:])
        shared = shared.reshape((experts, half) + shared.shape[1:])
        return jnp.concatenate([full, shared], 1)

    def lines_of(values):
        high = values.astype(BF16)
        low = (values - high.astype(F32)).astype(BF16)
        both = jnp.stack([high, low], 1)
        return jnp.pad(both, ((0, 0), (0, 14), (0, model - both.shape[2])))

    def values_of(rows):
        both = rows[:, CAP + half : CAP + half + 2, : CAP + half].astype(F32)
        return both[:, 0] + both[:, 1]

    def swap_experts(rows, *events):
        return lax.all_to_all(tie(rows, *events), PLANE, 0, 0, tiled=True)

    def dispatch(full, shared):
        return join_rows(dot(hot_full, full).astype(BF16), dot(hot_half, shared).astype(BF16))

    def combine(back):
        full = dot(hot_full, back[:, :CAP].reshape(-1, model), 0, 0)
        shared = dot(hot_half, back[:, CAP : CAP + half].reshape(-1, model), 0, 0)
        full = full.reshape(GROUP_IMG, sequence, model)
        shared = shared.reshape(GROUP_IMG, sequence, model)
        mine = jnp.where(core == 0, shared[0], shared[1])
        theirs = jnp.where(core == 0, shared[1], shared[0])
        mine = mine + lax.ppermute(theirs, "c", swap)
        return jnp.where(
            core == 0,
            jnp.concatenate([full, mine[None]]),
            jnp.concatenate([mine[None], full]),
        )

    if length == 4:
        parts[0] = tie(parts[0], *below)
    full_parts = [
        lax.all_gather(one, "z", axis=0, tiled=False)
        if length == 4
        else lax.all_gather(one, "z", axis=1, tiled=True)
        for one in parts
    ]
    grad_full, grad_shared = both_groups(out_grad)
    incoming = swap_experts(dispatch(grad_full, grad_shared), *packs[1:4], parts[-1])

    local_start = (chip_y * 2 + core) * piece
    mask_here = lax.dynamic_slice_in_dim(key_mask, local_start, piece, 0)[:, None]
    n1, n2, residual, q, k, v, attended, lse, wq, wk, wv, wo = attend_forward(
        jnp.stack(place).astype(jnp.int32),
        tokens_in, mask_here, lines, bias_pairs,
        packs, width,
    )
    n2 = tie(n2, incoming)
    normed_two = n2.reshape(tokens, model)

    normed_full, normed_shared = both_groups(n2)

    def chances_of(rows):
        return jax.nn.softmax(dot(rows, router, 1, 1), -1)

    probabilities = chances_of(normed_two)
    hot_ids = expert_ids[..., None] == jnp.arange(experts, dtype=jnp.int32)
    hot_here = lax.dynamic_slice_in_dim(hot_ids, local_start, piece, 0).astype(F32)
    hot_here = jnp.sum(hot_here.reshape(tokens, 2, experts), 1)
    share_here = hot_here * probabilities

    def slot_gates(match, rows, position_here):
        chance = chances_of(rows)
        hot = (position_here // CAP)[..., None] == jnp.arange(experts, dtype=jnp.int32)
        gates = jnp.sum(hot.astype(F32) * chance[:, None], -1)
        return jnp.sum(jnp.where(match, gates.T[None], 0.0), (1, 2))

    gates_sent = join_rows(
        slot_gates(match_full, normed_full, position_full),
        slot_gates(match_half, normed_shared, position_half),
    )
    chosen = swap_experts(
        jnp.concatenate([dispatch(normed_full, normed_shared), lines_of(gates_sent)], 1),
        incoming,
    )

    grad_rows = out_grad.reshape(tokens, model)
    bias_dot = dot(grad_rows, bias_down.astype(BF16), 1, 1)

    def lanes(values):
        values = jnp.pad(values, ((0, 0), (0, CAP - experts)))
        return values.reshape(piece, sequence, CAP)

    down_bias_grad = lax.dot_general(
        share_here, grad_rows.astype(F32), (((0,), (0,)), ((), ())), precision=HIGHEST
    )

    routes = (
        lanes(probabilities), lanes(hot_here * bias_dot), jnp.pad(router, ((0, CAP - experts), (0, 0)))
    )

    sums = None
    bias_parts = []
    reduced = []
    count = len(spans)
    for index, (first, last) in enumerate(spans):
        bias_one = bias_up[:, first * CHUNK : last * CHUNK].reshape(1, -1)
        final = index == count - 1
        if final:
            bias_one = tie(bias_one, *routes, down_bias_grad)
        *sums, bias_part, grads = expert_chunk(
            chosen, incoming, bias_one, sums, full_parts[index], final
        )
        bias_parts.append(bias_part.reshape(quarter, -1))
        if length == 4:
            reduced.append(lax.psum_scatter(grads, "z", scatter_dimension=0, tiled=False))
        else:
            reduced.append(lax.psum_scatter(grads, "z", scatter_dimension=1, tiled=True))

    mixed, pulled = sums
    back = swap_experts(pulled)
    core_line = jnp.reshape(core, (1,)).astype(jnp.int32)
    full_rows, mine_rows, theirs = combine_rows(
        core_line, back, position_full, position_half, GROUP_IMG
    )
    theirs = lax.ppermute(theirs, "c", swap)

    def send_back(some, *events):
        if not some:
            return None
        some = some[0].astype(BF16)
        if length != 4:
            some = some.reshape(2, 2, part, quarter, -1).transpose(1, 3, 0, 2, 4)
            some = some.reshape(experts, 2, part, -1)
        return swap_experts(some, *events)

    mixed = swap_experts(mixed, back)

    h_grad, hb, dq, dk, dv, logit_grad, line_sums, pair_sums = attend_backward(
        core_line, full_rows, mine_rows, theirs, *routes, out_grad, residual, mask_here, wo, lines, q, k, v, lse,
    )
    router_grad = dot(logit_grad.reshape(tokens, CAP), normed_two, 0, 0)[:experts]
    if length != 4:
        input_grad, line_ones = input_backward(h_grad, tokens_in, wq, wk, wv, lines, dq, dk, dv)

    bias_rows = jnp.concatenate(bias_parts, 1).reshape(dp, quarter, part)
    bias_rows = jnp.where(
        jnp.arange(experts)[:, None, None, None] == expert, bias_rows[None], 0.0
    )
    bias_rows = bias_rows.transpose(0, 2, 1, 3).reshape(experts * quarter, dp, part)
    line_grads = jnp.concatenate(
        [
            jnp.zeros((2, model), F32) if length == 4 else line_ones[:2],
            pair_sums[:, 0].reshape(1, model),
            pair_sums[:, 1].reshape(1, model),
            line_sums[:3],
            down_bias_grad,
            router_grad,
        ],
        0,
    ).reshape(-1, dp, part)
    sum_type = BF16 if length == 4 else F32
    vector_grads = jnp.concatenate([line_grads, bias_rows], 0).astype(sum_type)
    vector_grads = vector_grads.transpose(1, 0, 2).reshape(dp, small_rows * part)
    vector_grads = jnp.pad(vector_grads, ((0, 0), (0, pad))).reshape(dp, -1, model)

    hb = tie(hb, mixed)
    if length == 4:
        pack_grads = attend_weights(
            n1, hb, dq, dk, dv, attended, vector_grads, lines, (wq, wk, wv)
        )
    else:
        pack_grads = attend_weights(n1, hb, dq, dk, dv, attended, None)
        pack_grads = pack_grads.reshape(quarter, dp, part, model)
        vector_grads = jnp.broadcast_to(vector_grads[None], (quarter,) + vector_grads.shape)
        pack_grads = jnp.concatenate([pack_grads, vector_grads], 2)
        pack_grads = pack_grads.reshape(quarter // 2, 2, dp // 2, 2, -1, model)
        pack_grads = pack_grads.transpose(1, 3, 0, 2, 4, 5)
    weights_done = pack_grads
    mine = lax.dynamic_index_in_dim(pack_grads, core, 0, keepdims=False)
    theirs = lax.dynamic_index_in_dim(pack_grads, 1 - core, 0, keepdims=False)
    theirs = lax.ppermute(theirs, "c", swap)
    pack_grads = (mine.astype(F32) + theirs.astype(F32)).astype(sum_type)
    pack_grads = pack_grads.reshape((-1,) + pack_grads.shape[2:])
    if length == 4:
        h_grad = tie(h_grad, pack_grads)
        input_grad, _ = input_backward(h_grad, tokens_in, wq, wk, wv, lines, dq, dk, dv)
    sent = [send_back(reduced[:1], weights_done)]
    pack_grads = tie(pack_grads, *sent)
    pack_grads = lax.all_to_all(pack_grads, ("x", "y"), 0, 0, tiled=True)
    after_xy = pack_grads
    mixture = combine(mixed)
    bias_term = jnp.dot(share_here, bias_down, precision=HIGHEST).reshape(residual.shape)
    output = (residual + mixture + bias_term).astype(BF16)

    sent = [one.astype(F32) for one in sent if one is not None]
    ups = [one[:, 0] for one in sent]
    downs = [one[:, 1] for one in sent]
    pack_grads = tie(pack_grads, input_grad, output, *ups, *downs)
    pack_grads = jnp.sum(pack_grads.astype(F32), 0)
    pack_grads = pack_grads.astype(sum_type)
    if length == 4:
        pack_grad = lax.dynamic_index_in_dim(pack_grads, place[0], 0, keepdims=False).astype(F32)
        for far in (1, 2, 3):
            some = lax.dynamic_index_in_dim(pack_grads, (place[0] + far) % 4, 0, keepdims=False)
            some = lax.ppermute(some, "z", [(k, (k + far) % 4) for k in range(4)])
            pack_grad = pack_grad + some.astype(F32)
    else:
        pack_grad = lax.psum_scatter(pack_grads, "z", scatter_dimension=0, tiled=False)
    qkv_out = pack_grad[:part, : 3 * width].reshape(part, 3, width).transpose(1, 0, 2)
    out_weight_grad = pack_grad[:part, 3 * width :].T
    small_grads = pack_grad[part:].reshape(-1)[: small_rows * part].reshape(small_rows, part)

    some = send_back(reduced[1:], pack_grads)
    if some is not None:
        ups.append(some.astype(F32)[:, 0])
        downs.append(some.astype(F32)[:, 1])
    up_grad = jnp.concatenate(ups, -1)
    down_grad = jnp.concatenate(downs, -1).transpose(0, 2, 1)
    return (
        output,
        input_grad,
        small_grads[0],
        small_grads[1],
        qkv_out,
        small_grads[2:4],
        out_weight_grad,
        small_grads[4],
        small_grads[5],
        small_grads[6],
        small_grads[7 + experts : 7 + 2 * experts].T,
        up_grad,
        small_grads[7 + 2 * experts :].reshape(experts, -1),
        down_grad,
        small_grads[7 : 7 + experts],
    )


def solution(mesh):
    dp, tensor = mesh.devices.shape
    planes = jax.sharding.Mesh(
        mesh.devices.reshape(dp // 2, 2, tensor // 2, 2), ("z", "x", "y", "c")
    )
    rows = ("z", "x")
    images = P(("z", "x", "y", "c"), None, None)
    return jax.shard_map(
        shards,
        mesh=planes,
        in_specs=(
            images,
            P(rows, None),
            P(rows, None, None),
            P(rows, None, None),
            P(rows),
            P(rows),
            P(None, rows, TENSOR),
            P(None, rows),
            P(TENSOR, rows),
            P(rows),
            P(rows),
            P(rows),
            P(rows, None),
            P(None, rows, TENSOR),
            P(None, rows),
            P(None, TENSOR, rows),
            P(None, rows),
            images,
        ),
        out_specs=(
            images,
            images,
            P(rows),
            P(rows),
            P(None, rows, TENSOR),
            P(None, rows),
            P(TENSOR, rows),
            P(rows),
            P(rows),
            P(rows),
            P(rows, None),
            P(None, rows, TENSOR),
            P(None, rows),
            P(None, TENSOR, rows),
            P(None, rows),
        ),
        check_vma=False,
    )
```

```python
import functools
import jax
import jax.numpy as jnp
from jax import lax
from jax.experimental import pallas as pl
from jax.experimental.pallas import tpu as pltpu
from jax.sharding import PartitionSpec as P

HD = 64
CAP = 128
EPSILON = 1e-06
NEGATIVE = -1e30
F32 = jnp.float32
BF16 = jnp.bfloat16


def dot(left, right, left_dim=1, right_dim=0):
    return lax.dot_general(
        left, right, (((left_dim,), (right_dim,)), ((), ())), preferred_element_type=F32
    )


def norm_forward(values, gains, shifts):
    middle = jnp.mean(values, -1, keepdims=True)
    centred = values - middle
    inverse = lax.rsqrt(jnp.mean(centred * centred, -1, keepdims=True) + EPSILON)
    unit_rows = centred * inverse
    return (unit_rows * gains + shifts, unit_rows, inverse)


def norm_backward(grad_rows, unit_rows, inverse, gains):
    scaled = grad_rows * gains
    return inverse * (
        scaled
        - jnp.mean(scaled, -1, keepdims=True)
        - unit_rows * jnp.mean(scaled * unit_rows, -1, keepdims=True)
    )


def head_masks(width):
    lane = lax.broadcasted_iota(jnp.int32, (1, width), 1)
    return [(lane // HD == k) for k in range(width // HD)]


def arrange(w_ref, *parts):
    width = parts[0].shape[2]
    for t in range(w_ref.shape[0]):
        packed = w_ref[t]
        for k, ref in enumerate(parts):
            ref[t] = packed[:, k * width : (k + 1) * width]


def put_rows(ref, values):
    rows, columns = values.shape
    spare = jnp.zeros((ref.shape[0] - rows, columns), values.dtype)
    ref[...] = jnp.concatenate([values, spare], 0).astype(ref.dtype)


def attend_forward_kernel(
    place_ref, tokens_ref, mask_ref, lines_ref, bias_ref, *refs,
):
    (
        n1_ref, n2_ref, h_ref, q_ref, k_ref, v_ref, o_ref, lse_ref,
        wq_ref, wk_ref, wv_ref, wo_ref, all_ref, sem,
    ) = refs[-14:]
    packs = refs[:-14]

    @pl.when(pl.program_id(0) == 0)
    def _():
        if len(packs) == 1:
            pltpu.make_async_copy(packs[0], all_ref, sem).start()
        else:
            z, x, y, c = [place_ref[k] for k in range(4)]
            part = all_ref.shape[1] // 8
            for index, ref in enumerate(packs):
                dx, dy, dc = index & 1, (index >> 1) & 1, index >> 2
                t = (y ^ dy) * 2 + (c ^ dc)
                for back in range(4):
                    row = (((z - back) & 3) * 2 + (x ^ dx)) * part
                    pltpu.make_async_copy(
                        ref.at[back, pl.ds(0, part)],
                        all_ref.at[t, pl.ds(pl.multiple_of(row, 32), part)],
                        sem,
                    ).start()
        pltpu.make_async_copy(all_ref, all_ref, sem).wait()
        arrange(all_ref, wq_ref, wk_ref, wv_ref, wo_ref)

    x = tokens_ref[0].astype(F32)
    n1, _, _ = norm_forward(x, lines_ref[0:1, :], lines_ref[1:2, :])
    put_rows(n1_ref.at[0], n1)
    n1 = n1.astype(BF16)
    width = wq_ref.shape[2]
    masks = head_masks(width)
    keys = mask_ref[0] > 0
    total = x + lines_ref[4:5, :]
    for t in range(wq_ref.shape[0]):
        q = (dot(n1, wq_ref[t]) + bias_ref[t, 0:1, :]).astype(BF16)
        k = dot(n1, wk_ref[t]).astype(BF16)
        v = (dot(n1, wv_ref[t]) + bias_ref[t, 1:2, :]).astype(BF16)
        q_ref[0, t] = q
        k_ref[0, t] = k
        v_ref[0, t] = v
        scaled = q * jnp.asarray(HD ** (-0.5), BF16)
        o = jnp.zeros(q.shape, F32)
        for h, here in enumerate(masks):
            s = dot(jnp.where(here, scaled, jnp.zeros_like(scaled)), k, 1, 1)
            s = jnp.where(keys, s, NEGATIVE)
            largest = jnp.max(s, -1, keepdims=True)
            e = jnp.exp(s - largest)
            total_e = jnp.sum(e, -1, keepdims=True)
            p = (e / total_e).astype(BF16)
            o = jnp.where(here, dot(p, v), o)
            index = t * len(masks) + h
            lse_ref[0, :, index : index + 1] = largest + jnp.log(total_e)
        put_rows(o_ref.at[0, t], o)
        total = total + dot(o.astype(BF16), wo_ref[t], 1, 1)
    h_ref[0] = total
    n2, _, _ = norm_forward(total, lines_ref[5:6, :], lines_ref[6:7, :])
    n2_ref[0] = n2.astype(BF16)


def whole(shape):
    return pl.BlockSpec(shape, lambda b: (0,) * len(shape))


def by_image(shape):
    return pl.BlockSpec((1,) + shape[1:], lambda b: (b,) + (0,) * (len(shape) - 1))


def padded(rows):
    return -(-rows // 16) * 16


def attend_forward(place, tokens_in, mask, lines, bias_pairs, packs, width):
    images, sequence, model = tokens_in.shape
    quarter = model // width
    rows = (images, sequence, model)
    heads = (images, quarter, sequence, width)
    columns = (quarter, model, width)
    outs = [
        ((images, padded(sequence), model), BF16), (rows, BF16), (rows, F32), (heads, BF16), (heads, BF16),
        (heads, BF16), ((images, quarter, padded(sequence), width), BF16), ((images, sequence, 128), F32),
        (columns, BF16), (columns, BF16), (columns, BF16), (columns, BF16),
    ]
    place_spec = lambda spec: pl.BlockSpec(spec.block_shape, lambda b, p: spec.index_map(b))
    in_specs = [by_image(tokens_in.shape), by_image(mask.shape), whole(lines.shape), whole(bias_pairs.shape)]
    out_specs = [by_image(s) for s, _ in outs[:8]] + [whole(s) for s, _ in outs[8:]]
    return pl.pallas_call(
        attend_forward_kernel,
        grid_spec=pltpu.PrefetchScalarGridSpec(
            num_scalar_prefetch=1,
            grid=(images,),
            in_specs=[place_spec(s) for s in in_specs]
            + [pl.BlockSpec(memory_space=pl.ANY)] * len(packs),
            out_specs=[place_spec(s) for s in out_specs],
            scratch_shapes=[pltpu.VMEM((quarter, model, 4 * width), BF16), pltpu.SemaphoreType.DMA(())],
        ),
        out_shape=[jax.ShapeDtypeStruct(s, d) for s, d in outs],
        compiler_params=pltpu.CompilerParams(vmem_limit_bytes=56 * 2**20),
        cost_estimate=pl.CostEstimate(flops=2 * 10**9, bytes_accessed=4 * 10**6, transcendentals=0),
        name="attend_forward",
    )(place, tokens_in, mask, lines, bias_pairs, *packs)


def combine_kernel(core_ref, back_ref, full_at_ref, half_at_ref, full_ref, mine_ref, theirs_ref):
    experts, rows, model = back_ref.shape
    cap = full_ref.shape[2] - model
    half = cap // 2
    images, sequence, _ = full_ref.shape

    def gather(at_ref, first, size, slot):
        lanes = experts * size
        lane = lax.broadcasted_iota(jnp.int32, (1, lanes), 1)
        slots = lane // size * cap + slot + lane % size
        hot = (at_ref[:, 0:1] == slots) | (at_ref[:, 1:2] == slots)
        hot = jnp.where(hot, 1.0, 0.0).astype(BF16)
        taken = back_ref[:, first : first + size].reshape(lanes, model)
        sums = dot(hot, taken)
        owner = lax.broadcasted_iota(jnp.int32, (cap, lanes), 0) == lane // size
        scores = 0.0
        for k in range(2):
            line = jnp.concatenate(
                [
                    back_ref[e, cap + half :, first : first + size].astype(F32)[k : k + 1]
                    for e in range(experts)
                ],
                1,
            )
            scores += dot(hot, jnp.where(owner, line, 0.0).astype(BF16), 1, 1)
        joined = jnp.concatenate([sums, scores], 1)
        return [joined[k * sequence : (k + 1) * sequence] for k in range(images)]

    full = gather(full_at_ref, 0, cap, 0)
    shared = gather(half_at_ref, cap, half, core_ref[0] * half)
    for image in range(images):
        full_ref[image] = full[image]
        own = core_ref[0] == image

        def put(ref, image=image):
            ref[0] = shared[image]

        pl.when(own)(functools.partial(put, mine_ref))
        pl.when(jnp.logical_not(own))(functools.partial(put, theirs_ref))


def combine_rows(core, back, full_at, half_at, images):
    shape = (images, full_at.shape[0] // images, back.shape[2] + CAP)
    whole_at = lambda shape: pl.BlockSpec(shape, lambda i, c: (0,) * len(shape))
    return pl.pallas_call(
        combine_kernel,
        grid_spec=pltpu.PrefetchScalarGridSpec(
            num_scalar_prefetch=1,
            grid=(1,),
            in_specs=[whole_at(a.shape) for a in (back, full_at, half_at)],
            out_specs=[whole_at(shape)] + [whole_at((1,) + shape[1:])] * 2,
        ),
        out_shape=[
            jax.ShapeDtypeStruct(s, F32) for s in (shape, (1,) + shape[1:], (1,) + shape[1:])
        ],
        compiler_params=pltpu.CompilerParams(vmem_limit_bytes=56 * 2**20),
        cost_estimate=pl.CostEstimate(flops=0, bytes_accessed=0, transcendentals=0),
        name="combine_rows",
    )(core, back, full_at, half_at)


def attend_backward_kernel(
    core_ref, full_ref, mine_ref, theirs_ref, chance_ref, route_ref, router_ref,
    grad_ref, h_ref, mask_ref, wo_ref, lines_ref, q_ref, k_ref, v_ref, lse_ref,
    h_grad_ref, hb_ref, dq_ref, dk_ref, dv_ref, logit_ref, vec_ref, pair_ref,
):
    @pl.when(pl.program_id(0) == 0)
    def _():
        vec_ref[...] = jnp.zeros_like(vec_ref)
        pair_ref[...] = jnp.zeros_like(pair_ref)

    shared = pl.program_id(0) == 2 * (1 - core_ref[0])
    rows = jnp.where(shared, mine_ref[0] + theirs_ref[0], full_ref[0])
    model = wo_ref.shape[1]
    chances = chance_ref[0]
    chance_grad = rows[:, model:] + route_ref[0]
    logit_grad = chances * (
        chance_grad - jnp.sum(chances * chance_grad, -1, keepdims=True)
    )
    logit_grad = logit_grad.astype(BF16)
    logit_ref[0] = logit_grad
    n2_grad = rows[:, :model] + dot(logit_grad, router_ref[...])
    _, unit_two, inverse_two = norm_forward(h_ref[0], lines_ref[5:6, :], lines_ref[6:7, :])
    vec_ref[1:2, :] += jnp.sum(n2_grad * unit_two, 0, keepdims=True)
    vec_ref[2:3, :] += jnp.sum(n2_grad, 0, keepdims=True)
    h_grad = grad_ref[0].astype(F32) + norm_backward(
        n2_grad, unit_two, inverse_two, lines_ref[5:6, :]
    )
    vec_ref[0:1, :] += jnp.sum(h_grad, 0, keepdims=True)
    h_grad_ref[0] = h_grad
    put_rows(hb_ref.at[0], h_grad)
    hb = h_grad.astype(BF16)
    width = wo_ref.shape[2]
    masks = head_masks(width)
    keys = mask_ref[0] > 0
    scale = HD ** (-0.5)
    for t in range(wo_ref.shape[0]):
        do = dot(hb, wo_ref[t]).astype(BF16)
        q, k, v = q_ref[0, t], k_ref[0, t], v_ref[0, t]
        zero = jnp.zeros_like(q)
        scaled = q * jnp.asarray(scale, BF16)
        dq = jnp.zeros(q.shape, F32)
        dk = jnp.zeros(q.shape, F32)
        dv = jnp.zeros(q.shape, F32)
        for h, here in enumerate(masks):
            index = t * len(masks) + h
            s = dot(jnp.where(here, scaled, zero), k, 1, 1)
            s = jnp.where(keys, s, NEGATIVE)
            p = jnp.exp(s - lse_ref[0, :, index : index + 1])
            dp = dot(jnp.where(here, do, zero), v, 1, 1)
            ds = p * (dp - jnp.sum(p * dp, -1, keepdims=True))
            ds = ds.astype(BF16)
            dv = jnp.where(here, dot(p.astype(BF16), do, 0, 0), dv)
            dq = jnp.where(here, dot(ds, k), dq)
            dk = jnp.where(here, dot(ds, q, 0, 0), dk)
        dq = (dq * scale).astype(BF16).astype(F32)
        dv = dv.astype(BF16).astype(F32)
        pair_ref[t, 0:1, :] += jnp.sum(dq, 0, keepdims=True)
        pair_ref[t, 1:2, :] += jnp.sum(dv, 0, keepdims=True)
        put_rows(dq_ref.at[0, t], dq)
        put_rows(dk_ref.at[0, t], dk * scale)
        put_rows(dv_ref.at[0, t], dv)


def attend_backward(
    core, full, mine, theirs, chances, route, router, out_grad, h, mask, wo, lines, q, k, v, lse
):
    ins = (full, mine, theirs, chances, route, router, out_grad, h, mask, wo, lines, q, k, v, lse)
    images, sequence, model = h.shape
    quarter, _, width = wo.shape
    heads = ((images, quarter, padded(sequence), width), BF16)
    outs = [
        (h.shape, F32), ((images, padded(sequence), model), BF16), heads, heads, heads,
        (chances.shape, BF16), ((8, model), F32), ((quarter, 8, width), F32),
    ]

    def spec(index, shape):
        block = (1,) + shape[1:]
        rest = (0,) * (len(shape) - 1)
        if index == 0:
            return pl.BlockSpec(block, lambda b, c: (jnp.clip(b - c[0], 0, images - 2),) + rest)
        if index in (1, 2, 5, 9, 10):
            return pl.BlockSpec(shape, lambda b, c: (0,) * len(shape))
        return pl.BlockSpec(block, lambda b, c: (b,) + rest)

    return pl.pallas_call(
        attend_backward_kernel,
        grid_spec=pltpu.PrefetchScalarGridSpec(
            num_scalar_prefetch=1,
            grid=(images,),
            in_specs=[spec(i, a.shape) for i, a in enumerate(ins)],
            out_specs=[spec(3, s) for s, _ in outs[:6]] + [spec(2, s) for s, _ in outs[6:]],
        ),
        out_shape=[jax.ShapeDtypeStruct(s, d) for s, d in outs],
        compiler_params=pltpu.CompilerParams(vmem_limit_bytes=56 * 2**20),
        cost_estimate=pl.CostEstimate(flops=0, bytes_accessed=0, transcendentals=0),
        name="attend_backward",
    )(core, *ins)


def attend_weights_kernel(n1_ref, hb_ref, dq_ref, dk_ref, dv_ref, o_ref, *refs):
    width = dq_ref.shape[3]
    n1 = n1_ref[...].reshape(-1, n1_ref.shape[2])
    hb = hb_ref[...].reshape(-1, n1_ref.shape[2])
    pairs = ((n1, dq_ref), (n1, dk_ref), (n1, dv_ref), (hb, o_ref))
    t = pl.program_id(0)
    if len(refs) == 1:
        for k, (left, ref) in enumerate(pairs):
            sums = dot(left, ref[...].reshape(-1, width), 0, 0)
            refs[0][0, :, k * width : (k + 1) * width] = sums.astype(refs[0].dtype)
        return
    extra_ref, lines_ref, *weights, out_ref, gain_ref, shift_ref = refs
    part = n1.shape[1] // 8
    lanes = gain_ref.shape[1]

    @pl.when(t == 0)
    def _():
        gain_ref[...] = jnp.zeros_like(gain_ref)
        shift_ref[...] = jnp.zeros_like(shift_ref)

    for k, (left, ref) in enumerate(pairs):
        right = ref[...].reshape(-1, width)
        sums = dot(left, right, 0, 0)
        if k < 3:
            weight = weights[k][0].astype(F32)
            shift = weight * jnp.sum(right.astype(F32), 0, keepdims=True)
            gain = weight * sums
            for one, total_ref in ((gain, gain_ref), (shift, shift_ref)):
                total_ref[...] += one[:, :lanes]
                total_ref[:, : width - lanes] += one[:, lanes:]
        sums = sums.astype(BF16)
        for z in range(4):
            for x in range(2):
                start = (z * 2 + x) * part
                out_ref[t % 2, x, t // 2, z, :part, k * width : (k + 1) * width] = sums[
                    start : start + part
                ]

    @pl.when(t == pl.num_programs(0) - 1)
    def _():
        gain = jnp.sum(gain_ref[...].T, 0, keepdims=True)
        shift = jnp.sum(shift_ref[...].T, 0, keepdims=True)
        gain = (gain - lines_ref[1:2, :] * shift) / lines_ref[0:1, :]
        depth, model = extra_ref.shape[1:]
        row = lax.broadcasted_iota(jnp.int32, (depth, model), 0)
        for z in range(4):
            for x in range(2):
                here = slice((z * 2 + x) * part, (z * 2 + x + 1) * part)
                line = jnp.concatenate(
                    [gain[:, here], shift[:, here], jnp.zeros((1, model - 2 * part), F32)], 1
                )
                block = extra_ref[z * 2 + x].astype(F32) + jnp.where(row == 0, line, 0.0)
                block = block.astype(BF16)
                for y in range(2):
                    for c in range(2):
                        out_ref[c, x, y, z, part:, :] = block


def attend_weights(n1, hb, dq, dk, dv, o, extra, lines=None, weights=()):
    images, quarter, rows, width = dq.shape
    model = n1.shape[2]
    heads = pl.BlockSpec((images, 1, rows, width), lambda t: (0, t, 0, 0))
    in_specs = [whole(n1.shape), whole(hb.shape)] + [heads] * 4
    if extra is None:
        extras = []
        out_spec = pl.BlockSpec((1, model, 4 * width), lambda t: (t, 0, 0))
        out_shape = jax.ShapeDtypeStruct((quarter, model, 4 * width), F32)
        scratch = []
    else:
        extras = [extra, lines, *weights]
        in_specs += [whole(extra.shape), whole(lines.shape)]
        in_specs += [pl.BlockSpec((1, model, width), lambda t: (t, 0, 0))] * len(weights)
        shape = (2, 2, 2, 4, model // 8 + extra.shape[1], model)
        out_spec = whole(shape)
        out_shape = jax.ShapeDtypeStruct(shape, BF16)
        scratch = [pltpu.VMEM((model, 128), F32)] * 2
    return pl.pallas_call(
        attend_weights_kernel,
        grid=(quarter,),
        in_specs=in_specs,
        out_specs=out_spec,
        out_shape=out_shape,
        scratch_shapes=scratch,
        compiler_params=pltpu.CompilerParams(vmem_limit_bytes=56 * 2**20),
        cost_estimate=pl.CostEstimate(flops=0, bytes_accessed=0, transcendentals=0),
        name="attend_weights",
    )(n1, hb, dq, dk, dv, o, *extras)


def input_backward_kernel(
    h_grad_ref, tokens_ref, wq_ref, wk_ref, wv_ref, lines_ref, dq_ref, dk_ref, dv_ref,
    input_grad_ref, vec_ref,
):
    @pl.when(pl.program_id(0) == 0)
    def _():
        vec_ref[...] = jnp.zeros_like(vec_ref)

    rows = tokens_ref.shape[1]
    n1_grad = jnp.zeros((dq_ref.shape[2], tokens_ref.shape[2]), F32)
    for t in range(wq_ref.shape[0]):
        for grads, weights in ((dq_ref, wq_ref), (dk_ref, wk_ref), (dv_ref, wv_ref)):
            n1_grad += dot(grads[0, t], weights[t], 1, 1)
    n1_grad = n1_grad[:rows]
    _, unit_one, inverse_one = norm_forward(
        tokens_ref[0].astype(F32), lines_ref[0:1, :], lines_ref[1:2, :]
    )
    vec_ref[0:1, :] += jnp.sum(n1_grad * unit_one, 0, keepdims=True)
    vec_ref[1:2, :] += jnp.sum(n1_grad, 0, keepdims=True)
    input_grad_ref[0] = h_grad_ref[0] + norm_backward(
        n1_grad, unit_one, inverse_one, lines_ref[0:1, :]
    )


def input_backward(h_grad, tokens_in, wq, wk, wv, lines, dq, dk, dv):
    ins = (h_grad, tokens_in, wq, wk, wv, lines, dq, dk, dv)
    outs = [(h_grad.shape, F32), ((8, wq.shape[1]), F32)]
    return pl.pallas_call(
        input_backward_kernel,
        grid=(h_grad.shape[0],),
        in_specs=[whole(a.shape) if 2 <= i <= 5 else by_image(a.shape) for i, a in enumerate(ins)],
        out_specs=[by_image(outs[0][0]), whole(outs[1][0])],
        out_shape=[jax.ShapeDtypeStruct(s, d) for s, d in outs],
        compiler_params=pltpu.CompilerParams(vmem_limit_bytes=56 * 2**20),
        cost_estimate=pl.CostEstimate(flops=0, bytes_accessed=0, transcendentals=0),
        name="input_backward",
    )(*ins)


def pack_experts_kernel(up_ref, down_ref, *refs):
    up = up_ref[...].astype(BF16)
    down = down_ref[...].astype(BF16)
    start = 0
    for ref in refs:
        stop = start + ref.shape[3]
        ref[:, 0] = up[:, :, start:stop]
        ref[:, 1] = down[:, :, start:stop]
        start = stop


def pack_experts(up, down, sizes):
    experts, part, units = up.shape
    step = 4
    block = lambda shape: pl.BlockSpec((step,) + shape[1:], lambda i: (i,) + (0,) * (len(shape) - 1))
    outs = [(experts, 2, part, size) for size in sizes]
    return pl.pallas_call(
        pack_experts_kernel,
        grid=(experts // step,),
        in_specs=[block(up.shape), block(down.shape)],
        out_specs=[block(s) for s in outs],
        out_shape=[jax.ShapeDtypeStruct(s, BF16) for s in outs],
        compiler_params=pltpu.CompilerParams(vmem_limit_bytes=56 * 2**20),
        cost_estimate=pl.CostEstimate(flops=0, bytes_accessed=8 * 10**6, transcendentals=0),
        name="pack_experts",
    )(up, down)


def unpack_experts_kernel(*refs):
    up_ref, down_ref = refs[-2:]
    start = 0
    for ref in refs[:-2]:
        stop = start + ref.shape[3]
        up_ref[:, :, start:stop] = ref[:, 0].astype(F32)
        down_ref[:, :, start:stop] = ref[:, 1].astype(F32)
        start = stop


def unpack_experts(pieces):
    experts, _, part, _ = pieces[0].shape
    step = 4
    block = lambda shape: pl.BlockSpec((step,) + shape[1:], lambda i: (i,) + (0,) * (len(shape) - 1))
    shape = (experts, part, sum(one.shape[3] for one in pieces))
    return pl.pallas_call(
        unpack_experts_kernel,
        grid=(experts // step,),
        in_specs=[block(one.shape) for one in pieces],
        out_specs=[block(shape)] * 2,
        out_shape=[jax.ShapeDtypeStruct(shape, F32)] * 2,
        compiler_params=pltpu.CompilerParams(vmem_limit_bytes=56 * 2**20),
        cost_estimate=pl.CostEstimate(flops=0, bytes_accessed=8 * 10**6, transcendentals=0),
        name="unpack_experts",
    )(*pieces)


def to_column(line):
    return jnp.broadcast_to(line, (128, 256)).T[:, :1]


def to_line(column):
    return jnp.broadcast_to(column, (256, 128)).T[:1, :]


def expert_kernel(first, last, x_ref, g_ref, b_ref, shards_ref, *refs):
    if not first:
        (y_in, p_in), refs = refs[:2], refs[2:]
    (y_out, p_out, bias_ref), refs = refs[:3], refs[3:]
    acc_ref, w_ref, sem = refs[-3:]
    grads_ref = refs[0]
    step = pl.program_id(0)
    model = w_ref.shape[1]

    @pl.when(step == 0)
    def _():
        if len(shards_ref.shape) == 3:
            pltpu.make_async_copy(shards_ref, w_ref, sem).start()
        else:
            part, units = shards_ref.shape[3:]
            for z in range(4):
                for p in range(8):
                    row = (z * 2 + p // 4) * part
                    pltpu.make_async_copy(
                        shards_ref.at[z, p],
                        w_ref.at[:, pl.ds(row, part), pl.ds((p % 4) * units, units)],
                        sem,
                    ).start()
        acc_ref[...] = jnp.zeros_like(acc_ref)
        bias_ref[...] = jnp.zeros_like(bias_ref)
        pltpu.make_async_copy(w_ref, w_ref, sem).wait()

    sources, slots, _ = g_ref.shape
    x = x_ref[:, :slots].reshape(-1, model)
    g_raw = g_ref[...].reshape(-1, model)
    gates = []
    for k in range(sources):
        parts = x_ref[k, slots : slots + 16, :256].astype(F32)
        gates.append(to_column(parts[0:1] + parts[1:2])[:slots])
    gate = jnp.concatenate(gates, 0)
    g = (g_raw.astype(F32) * gate).astype(BF16)
    hidden = dot(x, w_ref[0]) + b_ref[...]
    cdf = 0.5 * (1.0 + lax.erf(hidden * (0.5 ** 0.5)))
    active = (hidden * cdf).astype(BF16)
    slope = cdf + hidden * (jnp.exp(-0.5 * hidden * hidden) * 0.3989422804014327)
    hidden_grad = (dot(g, w_ref[1]) * slope).astype(BF16)
    y = dot(active, w_ref[1], 1, 1)
    p = dot(hidden_grad, w_ref[0], 1, 1)
    if not first:
        y = y_in[...].reshape(-1, model) + y
        p = p_in[...].reshape(-1, model) + p
    if not last:
        y_out[...] = y.reshape(sources, slots, model)
        p_out[...] = p.reshape(sources, slots, model)
    else:
        y_out[...] = (y * gate).astype(BF16).reshape(sources, slots, model)
        p_out[:, :slots] = p.astype(BF16).reshape(sources, slots, model)
        gate_grad = jnp.sum(g_raw.astype(F32) * y, -1, keepdims=True)
        for k in range(sources):
            own = gate_grad[k * slots : (k + 1) * slots]
            line = to_line(jnp.concatenate([own, jnp.zeros((256 - slots, 1), F32)], 0))
            high = line.astype(BF16)
            low = (line - high.astype(F32)).astype(BF16)
            block = jnp.concatenate([high, low, jnp.zeros((14, 256), BF16)], 0)
            p_out[k, slots:] = jnp.concatenate([block, jnp.zeros((16, model - 256), BF16)], 1)
    bias_ref[...] += jnp.sum(hidden_grad.astype(F32), 0, keepdims=True)
    acc_ref[0] += dot(x, hidden_grad, 0, 0)
    acc_ref[1] += dot(g, active, 0, 0)

    @pl.when(step == pl.num_programs(0) - 1)
    def _():
        if len(shards_ref.shape) == 3:
            grads_ref[...] = acc_ref[...]
        else:
            part, units = shards_ref.shape[3:]
            for z in range(4):
                for q in range(8):
                    row = (z * 2 + q // 4) * part
                    columns = slice((q % 4) * units, (q % 4 + 1) * units)
                    grads_ref[z, q] = acc_ref[:, row : row + part, columns].astype(BF16)


def expert_chunk(x, g, b, sums, shards, last):
    experts, slots, model = g.shape
    units = b.shape[1]
    first = sums is None
    step = 2
    block = lambda rows: pl.BlockSpec((step, rows, model), lambda i: (i, 0, 0))
    full = whole
    ins = [x, g, b, shards] + ([] if first else list(sums))
    in_specs = [block(x.shape[1]), block(slots), full(b.shape)]
    in_specs.append(pl.BlockSpec(memory_space=pl.ANY))
    in_specs += [] if first else [block(slots)] * 2
    rows = (experts, slots, model)
    if last:
        outs = [(rows, BF16), (x.shape, BF16)]
    else:
        outs = [(rows, F32), (rows, F32)]
    out_specs = [block(s[1]) for s, _ in outs]
    outs.append((b.shape, F32))
    if len(shards.shape) == 3:
        outs.append(((2, model, units), F32))
    else:
        outs.append((shards.shape, BF16))
    out_specs += [full(s) for s, _ in outs[2:]]
    base = 4
    return pl.pallas_call(
        functools.partial(expert_kernel, first, last),
        grid=(experts // step,),
        in_specs=in_specs,
        out_specs=out_specs,
        scratch_shapes=[
            pltpu.VMEM((2, model, units), F32),
            pltpu.VMEM((2, model, units), BF16),
            pltpu.SemaphoreType.DMA(()),
        ],
        out_shape=[jax.ShapeDtypeStruct(s, d) for s, d in outs],
        input_output_aliases={} if first or last else {base: 0, base + 1: 1},
        compiler_params=pltpu.CompilerParams(vmem_limit_bytes=58 * 2**20),
        cost_estimate=pl.CostEstimate(
            flops=2 * experts * slots * model * units, bytes_accessed=4 * 10**6, transcendentals=0
        ),
        name="expert_chunk",
    )(*ins)


GROUP_IMG = 2
CHUNK = 128
HIGHEST = lax.Precision.HIGHEST
TENSOR = ("y", "c")
PLANE = ("x", "y", "c")
EVERY = ("y", "c", "z", "x")


def tie(values, *events):
    events = [e for e in events if e is not None]
    if not events:
        return values
    return lax.optimization_barrier((values, *events))[0]


def gather_packs(pack):
    below = [pack] + [
        lax.ppermute(pack, "z", [(k, (k + far) % 4) for k in range(4)]) for far in (1, 2, 3)
    ]
    column = jnp.stack(below)
    swap = [(0, 1), (1, 0)]
    over_x = lax.ppermute(column, "x", swap)
    over_y = lax.ppermute(column, "y", swap)
    over_both = lax.ppermute(column, ("x", "y"), [(0, 3), (1, 2), (2, 1), (3, 0)])
    four = [column, over_x, over_y, over_both]
    return four + [lax.ppermute(each, "c", swap) for each in four], below[1:]


def shards(
    tokens_in,
    key_mask,
    expert_ids,
    expert_slots,
    norm1_gain,
    norm1_shift,
    qkv_weight,
    qv_bias,
    out_weight,
    out_bias,
    norm2_gain,
    norm2_shift,
    router_weight,
    up_weight,
    up_bias,
    down_weight,
    down_bias,
    out_grad,
):
    length = lax.axis_size("z")
    core = lax.axis_index("c")
    chip_y = lax.axis_index("y")
    quarter = lax.axis_size("y") * 2
    expert = (lax.axis_index("x") * lax.axis_size("y") + chip_y) * 2 + core
    piece, sequence, model = tokens_in.shape
    experts, part, units = up_weight.shape
    dp = model // part
    width = qkv_weight.shape[2]
    tokens = piece * sequence
    blocks = units // CHUNK
    spans = [(0, 4), (4, 6)] if blocks == 6 else [(0, blocks)]

    head = spans[0][1] * CHUNK
    sizes = [head, units - head] if units > head else [head]
    packed = pack_experts(up_weight, down_weight.transpose(0, 2, 1), sizes)
    qkv_weight, norm1_gain = tie((qkv_weight, norm1_gain), packed[0])

    smalls = jnp.concatenate(
        [
            norm1_gain[None],
            norm1_shift[None],
            qv_bias,
            out_bias[None],
            norm2_gain[None],
            norm2_shift[None],
            down_bias,
            router_weight.T,
            up_bias.reshape(experts * quarter, part),
        ],
        0,
    ).astype(BF16)
    small_rows = smalls.shape[0]
    pad = -(small_rows * part) % (16 * model)
    small_block = jnp.pad(smalls.reshape(-1), (0, pad)).reshape(-1, model)
    pack = jnp.concatenate(
        [
            jnp.concatenate(
                [qkv_weight[0], qkv_weight[1], qkv_weight[2], out_weight.T], 1
            ).astype(BF16),
            small_block,
        ],
        0,
    )
    place = [lax.axis_index(name) for name in ("z", "x", "y", "c")]
    if length == 4:
        packs, below = gather_packs(pack)
        by_x = jnp.stack([packs[0][:, part:], packs[1][:, part:]]).reshape(2, 4, -1)
        pick_x = (place[1] ^ jnp.arange(2))[:, None] == jnp.arange(2)
        pick_z = (place[0] - jnp.arange(4)[:, None]) % 4 == jnp.arange(4)
        pick = pick_z[:, None, None, :] & pick_x[None, :, :, None]
        vectors = dot(pick.reshape(8, 8).astype(BF16), by_x.reshape(8, -1)).astype(BF16)
    else:
        packs = lax.all_gather(pack, EVERY, axis=0, tiled=False)
        packs = packs.reshape(quarter, dp, pack.shape[0], model)
        vectors = packs[0, :, part:].reshape(dp, -1)
        packs = [packs[:, :, :part].reshape(quarter, model, model)]
    event = []
    parts = []
    for some in packed:
        some = lax.all_to_all(tie(some, *event), PLANE, 0, 0, tiled=True)
        event = [some, *packs[3:4]]
        starts = [CHUNK * f for f, _ in spans[1:]] if parts else [0]
        stops = [CHUNK * l for _, l in spans[1:]] if parts else [head]
        base = starts[0]
        parts += [some[..., f - base : l - base] for f, l in zip(starts, stops)]
    if length != 4:
        parts = [
            one.reshape(2, quarter, 2, part, -1).transpose(2, 0, 3, 1, 4).reshape(2, 2 * part, -1)
            for one in parts
        ]

    vectors = vectors[:, : small_rows * part].reshape(dp, small_rows, part).transpose(1, 0, 2)
    lines = vectors[: 7 + 2 * experts].reshape(-1, model).astype(F32)
    bias_pairs = lines[2:4].reshape(2, quarter, width).transpose(1, 0, 2)
    bias_down = lines[7 : 7 + experts]
    router = lines[7 + experts :].astype(BF16)
    bias_up = vectors[7 + 2 * experts :].reshape(experts, quarter, dp, part)
    bias_up = bias_up.transpose(0, 2, 1, 3).reshape(experts, quarter, units)
    bias_up = lax.dynamic_index_in_dim(bias_up, expert, 0, keepdims=False).astype(F32)

    first_group = chip_y * 3
    group_tokens = GROUP_IMG * sequence
    position = (expert_ids * CAP + expert_slots).reshape(-1, group_tokens, 2)
    position_full = lax.dynamic_index_in_dim(position, first_group + 2 * core, 0, keepdims=False)
    position_half = lax.dynamic_index_in_dim(position, first_group + 1, 0, keepdims=False)
    slots_full = jnp.arange(experts * CAP, dtype=jnp.int32)
    half = CAP // 2
    slots_half = (
        jnp.arange(experts, dtype=jnp.int32)[:, None] * CAP
        + core * half
        + jnp.arange(half, dtype=jnp.int32)
    ).reshape(-1)
    match_full = slots_full[:, None, None] == position_full.T[None]
    match_half = slots_half[:, None, None] == position_half.T[None]
    hot_full = (match_full[:, 0] | match_full[:, 1]).astype(BF16)
    hot_half = (match_half[:, 0] | match_half[:, 1]).astype(BF16)
    swap = [(0, 1), (1, 0)]

    def both_groups(values):
        lent = jnp.where(core == 0, values[2], values[0])
        other = lax.ppermute(lent, "c", swap)
        full = jnp.where(core == 0, values[:2], values[1:])
        shared = jnp.where(core == 0, jnp.stack([lent, other]), jnp.stack([other, lent]))
        return (
            full.reshape(group_tokens, -1),
            shared.reshape(group_tokens, -1),
        )

    def join_rows(full, shared):
        full = full.reshape((experts, CAP) + full.shape[1:])
        shared = shared.reshape((experts, half) + shared.shape[1:])
        return jnp.concatenate([full, shared], 1)

    def lines_of(values):
        high = values.astype(BF16)
        low = (values - high.astype(F32)).astype(BF16)
        both = jnp.stack([high, low], 1)
        return jnp.pad(both, ((0, 0), (0, 14), (0, model - both.shape[2])))

    def values_of(rows):
        both = rows[:, CAP + half : CAP + half + 2, : CAP + half].astype(F32)
        return both[:, 0] + both[:, 1]

    def swap_experts(rows, *events):
        return lax.all_to_all(tie(rows, *events), PLANE, 0, 0, tiled=True)

    def dispatch(full, shared):
        return join_rows(dot(hot_full, full).astype(BF16), dot(hot_half, shared).astype(BF16))

    def combine(back):
        full = dot(hot_full, back[:, :CAP].reshape(-1, model), 0, 0)
        shared = dot(hot_half, back[:, CAP : CAP + half].reshape(-1, model), 0, 0)
        full = full.reshape(GROUP_IMG, sequence, model)
        shared = shared.reshape(GROUP_IMG, sequence, model)
        mine = jnp.where(core == 0, shared[0], shared[1])
        theirs = jnp.where(core == 0, shared[1], shared[0])
        mine = mine + lax.ppermute(theirs, "c", swap)
        return jnp.where(
            core == 0,
            jnp.concatenate([full, mine[None]]),
            jnp.concatenate([mine[None], full]),
        )

    if length == 4:
        parts[0] = tie(parts[0], *below)
    full_parts = [
        lax.all_gather(one, "z", axis=0, tiled=False)
        if length == 4
        else lax.all_gather(one, "z", axis=1, tiled=True)
        for one in parts
    ]
    grad_full, grad_shared = both_groups(out_grad)
    incoming = swap_experts(dispatch(grad_full, grad_shared), *packs[1:4], parts[-1])

    local_start = (chip_y * 2 + core) * piece
    mask_here = lax.dynamic_slice_in_dim(key_mask, local_start, piece, 0)[:, None]
    n1, n2, residual, q, k, v, attended, lse, wq, wk, wv, wo = attend_forward(
        jnp.stack(place).astype(jnp.int32),
        tokens_in, mask_here, lines, bias_pairs,
        packs, width,
    )
    n2 = tie(n2, incoming)
    normed_two = n2.reshape(tokens, model)

    normed_full, normed_shared = both_groups(n2)

    def chances_of(rows):
        return jax.nn.softmax(dot(rows, router, 1, 1), -1)

    probabilities = chances_of(normed_two)
    hot_ids = expert_ids[..., None] == jnp.arange(experts, dtype=jnp.int32)
    hot_here = lax.dynamic_slice_in_dim(hot_ids, local_start, piece, 0).astype(F32)
    hot_here = jnp.sum(hot_here.reshape(tokens, 2, experts), 1)
    share_here = hot_here * probabilities

    def slot_gates(match, rows, position_here):
        chance = chances_of(rows)
        hot = (position_here // CAP)[..., None] == jnp.arange(experts, dtype=jnp.int32)
        gates = jnp.sum(hot.astype(F32) * chance[:, None], -1)
        return jnp.sum(jnp.where(match, gates.T[None], 0.0), (1, 2))

    gates_sent = join_rows(
        slot_gates(match_full, normed_full, position_full),
        slot_gates(match_half, normed_shared, position_half),
    )
    chosen = swap_experts(
        jnp.concatenate([dispatch(normed_full, normed_shared), lines_of(gates_sent)], 1),
        incoming,
    )

    grad_rows = out_grad.reshape(tokens, model)
    bias_dot = dot(grad_rows, bias_down.astype(BF16), 1, 1)

    def lanes(values):
        values = jnp.pad(values, ((0, 0), (0, CAP - experts)))
        return values.reshape(piece, sequence, CAP)

    down_bias_grad = lax.dot_general(
        share_here, grad_rows.astype(F32), (((0,), (0,)), ((), ())), precision=HIGHEST
    )

    routes = (
        lanes(probabilities), lanes(hot_here * bias_dot), jnp.pad(router, ((0, CAP - experts), (0, 0)))
    )

    sums = None
    bias_parts = []
    reduced = []
    count = len(spans)
    for index, (first, last) in enumerate(spans):
        bias_one = bias_up[:, first * CHUNK : last * CHUNK].reshape(1, -1)
        final = index == count - 1
        if final:
            bias_one = tie(bias_one, *routes, down_bias_grad)
        *sums, bias_part, grads = expert_chunk(
            chosen, incoming, bias_one, sums, full_parts[index], final
        )
        bias_parts.append(bias_part.reshape(quarter, -1))
        if length == 4:
            reduced.append(lax.psum_scatter(grads, "z", scatter_dimension=0, tiled=False))
        else:
            reduced.append(lax.psum_scatter(grads, "z", scatter_dimension=1, tiled=True))

    mixed, pulled = sums
    back = swap_experts(pulled)
    core_line = jnp.reshape(core, (1,)).astype(jnp.int32)
    full_rows, mine_rows, theirs = combine_rows(
        core_line, back, position_full, position_half, GROUP_IMG
    )
    theirs = lax.ppermute(theirs, "c", swap)

    def send_back(some, *events):
        if not some:
            return None
        some = some[0].astype(BF16)
        if length != 4:
            some = some.reshape(2, 2, part, quarter, -1).transpose(1, 3, 0, 2, 4)
            some = some.reshape(experts, 2, part, -1)
        return swap_experts(some, *events)

    mixed = swap_experts(mixed, back)

    h_grad, hb, dq, dk, dv, logit_grad, line_sums, pair_sums = attend_backward(
        core_line, full_rows, mine_rows, theirs, *routes, out_grad, residual, mask_here, wo, lines, q, k, v, lse,
    )
    router_grad = dot(logit_grad.reshape(tokens, CAP), normed_two, 0, 0)[:experts]
    if length != 4:
        input_grad, line_ones = input_backward(h_grad, tokens_in, wq, wk, wv, lines, dq, dk, dv)

    bias_rows = jnp.concatenate(bias_parts, 1).reshape(dp, quarter, part)
    bias_rows = jnp.where(
        jnp.arange(experts)[:, None, None, None] == expert, bias_rows[None], 0.0
    )
    bias_rows = bias_rows.transpose(0, 2, 1, 3).reshape(experts * quarter, dp, part)
    line_grads = jnp.concatenate(
        [
            jnp.zeros((2, model), F32) if length == 4 else line_ones[:2],
            pair_sums[:, 0].reshape(1, model),
            pair_sums[:, 1].reshape(1, model),
            line_sums[:3],
            down_bias_grad,
            router_grad,
        ],
        0,
    ).reshape(-1, dp, part)
    sum_type = BF16 if length == 4 else F32
    vector_grads = jnp.concatenate([line_grads, bias_rows], 0).astype(sum_type)
    vector_grads = vector_grads.transpose(1, 0, 2).reshape(dp, small_rows * part)
    vector_grads = jnp.pad(vector_grads, ((0, 0), (0, pad))).reshape(dp, -1, model)

    hb = tie(hb, mixed)
    if length == 4:
        pack_grads = attend_weights(
            n1, hb, dq, dk, dv, attended, vector_grads, lines, (wq, wk, wv)
        )
    else:
        pack_grads = attend_weights(n1, hb, dq, dk, dv, attended, None)
        pack_grads = pack_grads.reshape(quarter, dp, part, model)
        vector_grads = jnp.broadcast_to(vector_grads[None], (quarter,) + vector_grads.shape)
        pack_grads = jnp.concatenate([pack_grads, vector_grads], 2)
        pack_grads = pack_grads.reshape(quarter // 2, 2, dp // 2, 2, -1, model)
        pack_grads = pack_grads.transpose(1, 3, 0, 2, 4, 5)
    weights_done = pack_grads
    mine = lax.dynamic_index_in_dim(pack_grads, core, 0, keepdims=False)
    theirs = lax.dynamic_index_in_dim(pack_grads, 1 - core, 0, keepdims=False)
    theirs = lax.ppermute(theirs, "c", swap)
    pack_grads = (mine.astype(F32) + theirs.astype(F32)).astype(sum_type)
    pack_grads = pack_grads.reshape((-1,) + pack_grads.shape[2:])
    if length == 4:
        h_grad = tie(h_grad, pack_grads)
        input_grad, _ = input_backward(h_grad, tokens_in, wq, wk, wv, lines, dq, dk, dv)
    sent = [send_back(reduced[:1], weights_done)]
    pack_grads = tie(pack_grads, *sent)
    pack_grads = lax.all_to_all(pack_grads, ("x", "y"), 0, 0, tiled=True)
    after_xy = pack_grads
    mixture = combine(mixed)
    bias_term = jnp.dot(share_here, bias_down, precision=HIGHEST).reshape(residual.shape)
    output = (residual + mixture + bias_term).astype(BF16)

    pack_grads = tie(pack_grads, input_grad, output)
    pack_grads = jnp.sum(pack_grads.astype(F32), 0)
    pack_grads = pack_grads.astype(sum_type)
    if length == 4:
        pack_grad = lax.dynamic_index_in_dim(pack_grads, place[0], 0, keepdims=False).astype(F32)
        for far in (1, 2, 3):
            some = lax.dynamic_index_in_dim(pack_grads, (place[0] + far) % 4, 0, keepdims=False)
            some = lax.ppermute(some, "z", [(k, (k + far) % 4) for k in range(4)])
            pack_grad = pack_grad + some.astype(F32)
    else:
        pack_grad = lax.psum_scatter(pack_grads, "z", scatter_dimension=0, tiled=False)
    qkv_out = pack_grad[:part, : 3 * width].reshape(part, 3, width).transpose(1, 0, 2)
    out_weight_grad = pack_grad[:part, 3 * width :].T
    small_grads = pack_grad[part:].reshape(-1)[: small_rows * part].reshape(small_rows, part)

    some = send_back(reduced[1:], pack_grads)
    up_grad, down_grad = unpack_experts([one for one in (*sent, some) if one is not None])
    down_grad = down_grad.transpose(0, 2, 1)
    return (
        output,
        input_grad,
        small_grads[0],
        small_grads[1],
        qkv_out,
        small_grads[2:4],
        out_weight_grad,
        small_grads[4],
        small_grads[5],
        small_grads[6],
        small_grads[7 + experts : 7 + 2 * experts].T,
        up_grad,
        small_grads[7 + 2 * experts :].reshape(experts, -1),
        down_grad,
        small_grads[7 : 7 + experts],
    )


def solution(mesh):
    dp, tensor = mesh.devices.shape
    planes = jax.sharding.Mesh(
        mesh.devices.reshape(dp // 2, 2, tensor // 2, 2), ("z", "x", "y", "c")
    )
    rows = ("z", "x")
    images = P(("z", "x", "y", "c"), None, None)
    return jax.shard_map(
        shards,
        mesh=planes,
        in_specs=(
            images,
            P(rows, None),
            P(rows, None, None),
            P(rows, None, None),
            P(rows),
            P(rows),
            P(None, rows, TENSOR),
            P(None, rows),
            P(TENSOR, rows),
            P(rows),
            P(rows),
            P(rows),
            P(rows, None),
            P(None, rows, TENSOR),
            P(None, rows),
            P(None, TENSOR, rows),
            P(None, rows),
            images,
        ),
        out_specs=(
            images,
            images,
            P(rows),
            P(rows),
            P(None, rows, TENSOR),
            P(None, rows),
            P(TENSOR, rows),
            P(rows),
            P(rows),
            P(rows),
            P(rows, None),
            P(None, rows, TENSOR),
            P(None, rows),
            P(None, TENSOR, rows),
            P(None, rows),
        ),
        check_vma=False,
    )
```
